32 devices in a mesh: dp: 8 (over z, y), tensor: 4 (over x, core).
Axes of the slice: x: 2, y: 2, z: 4, core: 2. Of those that a mesh axis runs over, the one named last changes fastest.
Arguments:
- hidden_in: bfloat16 [8192, 1024], P(('dp', 'tensor')), may hold values from -11 to 11
- out_grad: bfloat16 [8192, 1024], P(('dp', 'tensor')), may hold values from -6 to 6
- prefix_len: int32 [8], P('dp'), may hold values from 102 to 512
- qkv_weight: bfloat16 [1024, 3072], P(None, 'tensor'), may hold values from -1 to 1
- qv_bias: float32 [16, 2, 64], P('tensor'), may hold values from -1.8 to 1.8
- dense_weight: bfloat16 [1024, 1024], P('tensor'), may hold values from -0.5 to 0.5
- dense_bias: float32 [1024], replicated, may hold values from -1.8 to 1.8
- norm1_gain: float32 [1024], replicated, may hold values from 0.25 to 1.75
- norm1_shift: float32 [1024], replicated, may hold values from -1.8 to 1.8
- norm2_gain: float32 [1024], replicated, may hold values from 0.25 to 1.75
- norm2_shift: float32 [1024], replicated, may hold values from -1.8 to 1.8
- fc1_weight: bfloat16 [1024, 4096], P(None, 'tensor'), may hold values from -1 to 1
- fc1_bias: float32 [4096], P('tensor'), may hold values from -1.8 to 1.8
- fc2_weight: bfloat16 [4096, 1024], P('tensor'), may hold values from -0.1875 to 0.1875
- fc2_bias: float32 [1024], replicated, may hold values from -1.8 to 1.8
Outputs:
- hidden_out: bfloat16 [8192, 1024], P(('dp', 'tensor'))
- hidden_grad: bfloat16 [8192, 1024], P(('dp', 'tensor'))
- qkv_weight_grad: float32 [1024, 3072], P(None, 'tensor')
- qv_bias_grad: float32 [16, 2, 64], P('tensor')
- dense_weight_grad: float32 [1024, 1024], P('tensor')
- dense_bias_grad: float32 [1024], replicated
- norm1_gain_grad: float32 [1024], replicated
- norm1_shift_grad: float32 [1024], replicated
- norm2_gain_grad: float32 [1024], replicated
- norm2_shift_grad: float32 [1024], replicated
- fc1_weight_grad: float32 [1024, 4096], P(None, 'tensor')
- fc1_bias_grad: float32 [4096], P('tensor')
- fc2_weight_grad: float32 [4096, 1024], P('tensor')
- fc2_bias_grad: float32 [1024], replicated
- sublayer_rms: float32 [4], replicated
The draws below stay inside these ranges and needn't reach their ends.
All inputs are finite; a program needn't handle non-finite values.
Results may differ from the reference program's by a relative error of at most 0.015.
Values may be sent and summed in bfloat16 or wider, within the bound.
No kernel may reach another device: no remote copies, remote signals or barrier semaphores. Data moves between devices by JAX's collectives and lax.ppermute only.
A program may use at most 128 MiB of HBM per device.

```python
import math
import jax
import jax.numpy as jnp
from jax import lax

D = 1024
HEADS = 16
FF = 4096
HD = 64
SEQ = 1024
SEQS = 8
TOKENS = 8192


def draw_hidden_in(key, part):
    key = jax.random.fold_in(key, 11)
    position = jnp.arange(TOKENS, dtype=jnp.float32) / max(TOKENS - 1, 1)
    entries = jnp.clip(jax.random.normal(key, (TOKENS, D), jnp.float32), -6.0, 6.0)
    row_scale = 0.6 * 3.0 ** position
    return (entries * row_scale[:, None]).astype(jnp.bfloat16)


def draw_qkv_weight(key, part):
    key = jax.random.fold_in(key, 23)
    main_key, column_key = jax.random.split(key)
    entries = jnp.clip(jax.random.normal(main_key, (D, 3 * D), jnp.float32), -6.0, 6.0)
    columns = 0.3 * jnp.clip(jax.random.normal(column_key, (3 * D,), jnp.float32), -4.0, 4.0)
    return ((entries + columns[None, :]) * D ** (-0.5)).astype(jnp.bfloat16)


def draw_fc1_weight(key, part):
    key = jax.random.fold_in(key, 37)
    main_key, column_key = jax.random.split(key)
    entries = jnp.clip(jax.random.normal(main_key, (D, FF), jnp.float32), -6.0, 6.0)
    columns = 0.3 * jnp.clip(jax.random.normal(column_key, (FF,), jnp.float32), -4.0, 4.0)
    return ((entries + columns[None, :]) * D ** (-0.5)).astype(jnp.bfloat16)


def set_ends(array, stream_key, low, top_value):
    extent = array.shape
    place = [jax.random.randint(jax.random.fold_in(stream_key, axis), (), 0, extent[axis]) for axis in range(len(extent))]
    array = array.at[tuple(place)].set(low)
    longest = extent.index(max(extent))
    place[longest] = (place[longest] + 1) % extent[longest]
    return array.at[tuple(place)].set(top_value)


def steps_of(rng, shape, pieces, least, high):
    def one(axis_at, shards_of):
        draws = jax.random.uniform(jax.random.fold_in(jax.random.fold_in(rng, 6), axis_at), (shards_of,), jnp.float32, least / len(pieces), high / len(pieces))
        return jnp.repeat(jnp.exp(draws), shape[axis_at] // shards_of).reshape((-1,) + (1,) * (len(shape) - axis_at - 1))

    factor_of = one(*pieces[0])
    for cut in pieces[1:]:
        factor_of = factor_of * one(*cut)
    return factor_of


def normal_values(rng, shape, width, most, cuts=(), held_as=jnp.bfloat16):
    values = jax.random.normal(rng, shape, jnp.float32) * width
    if len(cuts) > 0:
        values = steps_of(rng, shape, cuts, -0.22, 0.18) * values
    return jnp.clip(values, min=-most, max=most).astype(held_as)


def setup_inputs(seed: int = 0) -> dict:
    key_of = jax.random.split(jax.random.key(seed), 16)
    return {
        "hidden_in": draw_hidden_in(jax.random.fold_in(key_of[15], 71), 0),
        "out_grad": normal_values(key_of[1], (TOKENS, D), 1.0, 6.0, ((0, 32),)),
        "prefix_len": set_ends(jax.random.randint(key_of[2], (SEQS,), SEQ // 10, SEQ // 2 + 1), jax.random.fold_in(key_of[2], 1), SEQ // 10, (SEQ // 2 + 1) - 1).astype(jnp.int32),
        "qkv_weight": draw_qkv_weight(jax.random.fold_in(key_of[15], 71), 0),
        "qv_bias": normal_values(key_of[4], (HEADS, 2, HD), 0.3, 1.8, ((0, 4),), jnp.float32),
        "dense_weight": normal_values(key_of[5], (D, D), (D // 8) ** -0.5, 0.5, ((0, 4),)),
        "dense_bias": normal_values(key_of[6], (D,), 0.3, 1.8, (), jnp.float32),
        "norm1_gain": jnp.clip(1.0 + 0.15 * jax.random.normal(key_of[7], (D,), jnp.float32), 0.25, 1.75),
        "norm1_shift": normal_values(key_of[8], (D,), 0.3, 1.8, (), jnp.float32),
        "norm2_gain": jnp.clip(1.0 + 0.15 * jax.random.normal(key_of[9], (D,), jnp.float32), 0.25, 1.75),
        "norm2_shift": normal_values(key_of[10], (D,), 0.3, 1.8, (), jnp.float32),
        "fc1_weight": draw_fc1_weight(jax.random.fold_in(key_of[15], 71), 0),
        "fc1_bias": normal_values(key_of[12], (FF,), 0.3, 1.8, ((0, 4),), jnp.float32),
        "fc2_weight": normal_values(key_of[13], (FF, D), (FF // 4) ** -0.5, 0.1875, ((0, 4),)),
        "fc2_bias": normal_values(key_of[14], (D,), 0.3, 1.8, (), jnp.float32),
    }


@jax.custom_vjp
def low(v):
    return lax.optimization_barrier(v.astype(jnp.bfloat16)).astype(jnp.float32)

@jax.custom_vjp
def low_back(v):
    return v

def low_keep(v):
    return (low(v), None)

def low_pass(kept, grad):
    return (grad,)

def back_keep(v):
    return (v, None)

def back_low(kept, grad):
    return (low(grad),)
low.defvjp(low_keep, low_pass)
low_back.defvjp(back_keep, back_low)
epsilon = 1e-05
highest = lax.Precision.HIGHEST

def layer_norm(values, gain, shift):
    center = lax.optimization_barrier(jnp.mean(values, axis=-1, keepdims=True))
    deviation = values - center
    variance = lax.optimization_barrier(jnp.mean(deviation * deviation, axis=-1, keepdims=True))
    return deviation * lax.rsqrt(variance + epsilon) * gain + shift

def attend(joined, prefix):
    queries = joined[:, :, 0, :]
    key_rows = joined[:, :, 1, :]
    value_rows = joined[:, :, 2, :]
    places = jnp.arange(SEQ, dtype=jnp.int32)
    row_pos = places[:, None]
    col_pos = places[None, :]
    allowed = (col_pos <= row_pos) | (col_pos < prefix) & (row_pos < prefix)
    distance = jnp.abs(row_pos - col_pos).astype(jnp.float32)
    slopes = 2.0 ** (-8.0 * (jnp.arange(HEADS, dtype=jnp.float32) + 1.0) / HEADS)
    scores = jnp.einsum('qhc,khc->hqk', queries, key_rows, precision=highest) * HD ** (-0.5)
    scores = scores - slopes[:, None, None] * distance[None, :, :]
    scores = low_back(jnp.where(allowed[None, :, :], scores, -1e+30))
    highest_score = lax.optimization_barrier(jnp.max(scores, axis=-1, keepdims=True))
    powered = jnp.exp(scores - highest_score)
    probs = powered / lax.optimization_barrier(jnp.sum(powered, axis=-1, keepdims=True))
    return jnp.einsum('hqk,khc->qhc', low(probs), value_rows, precision=highest)

def attend_item(item):
    return attend(item[0], item[1])

def forward(residual, qkv_weight, qv_bias, dense_weight, dense_bias, norm1_gain, norm1_shift, norm2_gain, norm2_shift, fc1_weight, fc1_bias, fc2_weight, fc2_bias, prefixes):
    normed1 = low(layer_norm(residual, norm1_gain, norm1_shift))
    bias_full = jnp.stack([qv_bias[:, 0], jnp.zeros_like(qv_bias[:, 0]), qv_bias[:, 1]], axis=1).reshape(-1)
    joined = low(low_back(jnp.dot(normed1, qkv_weight, precision=highest, preferred_element_type=jnp.float32) + bias_full))
    joined = joined.reshape(-1, SEQ, HEADS, 3, HD)
    context = lax.map(jax.checkpoint(attend_item), (joined, prefixes))
    context = low(low_back(context.reshape(-1, D)))
    attn_out = low_back(jnp.dot(context, dense_weight, precision=highest, preferred_element_type=jnp.float32)) + dense_bias
    middle = residual + attn_out
    normed2 = low(layer_norm(middle, norm2_gain, norm2_shift))
    hidden_pre = low_back(jnp.dot(normed2, fc1_weight, precision=highest, preferred_element_type=jnp.float32) + fc1_bias)
    activated = low(jax.nn.gelu(hidden_pre, approximate=True))
    mlp_out = low_back(jnp.dot(activated, fc2_weight, precision=highest, preferred_element_type=jnp.float32)) + fc2_bias
    return (middle + mlp_out, (attn_out, mlp_out))

def reference(hidden_in, out_grad, prefix_len, qkv_weight, qv_bias, dense_weight, dense_bias, norm1_gain, norm1_shift, norm2_gain, norm2_shift, fc1_weight, fc1_bias, fc2_weight, fc2_bias):
    params = tuple((value.astype(jnp.float32) for value in (qkv_weight, qv_bias, dense_weight, dense_bias, norm1_gain, norm1_shift, norm2_gain, norm2_shift, fc1_weight, fc1_bias, fc2_weight, fc2_bias)))
    group = math.gcd(SEQS, max(1, 4096 // SEQ))
    rounds = SEQS // group
    inputs = hidden_in.reshape(rounds, group * SEQ, D)
    cotangents = out_grad.reshape(rounds, group * SEQ, D)
    prefixes = prefix_len.reshape(rounds, group)

    def one_round(carry, item):
        gradients, squares = carry
        rows_in, rows_grad, prefix_part = item
        residual = rows_in.astype(jnp.float32)

        def run(values, *weights):
            return forward(values, *weights, prefix_part)
        result, pullback, branches = jax.vjp(run, residual, *params, has_aux=True)
        pulled = pullback(rows_grad.astype(jnp.float32))
        gradients = tuple((total + fresh for total, fresh in zip(gradients, pulled[1:])))
        attn_out, mlp_out = branches
        squares = squares + jnp.stack([jnp.sum(residual * residual), jnp.sum(attn_out * attn_out), jnp.sum(mlp_out * mlp_out), jnp.sum(result * result)])
        return ((gradients, squares), (result.astype(jnp.bfloat16), pulled[0].astype(jnp.bfloat16)))
    initial = (tuple((jnp.zeros_like(value) for value in params)), jnp.zeros((4,), jnp.float32))
    (gradients, squares), (outputs, input_grads) = lax.scan(one_round, initial, (inputs, cotangents, prefixes))
    sublayer_rms = jnp.sqrt(squares / (TOKENS * D))
    return (outputs.reshape(TOKENS, D), input_grads.reshape(TOKENS, D), gradients[0], gradients[1], gradients[2], gradients[3], gradients[4], gradients[5], gradients[6], gradients[7], gradients[8], gradients[9], gradients[10], gradients[11], sublayer_rms)
```

```python
from functools import partial

import jax
import jax.numpy as jnp
from jax import lax
from jax.experimental import pallas as pl
from jax.experimental.pallas import tpu as pltpu
from jax.sharding import PartitionSpec as P

HEADS = 16
PREFIX_MOST = 512

epsilon = 1e-05
BF = jnp.bfloat16
F32 = jnp.float32
NT = (((1,), (1,)), ((), ()))
NN = (((1,), (0,)), ((), ()))
TN = (((0,), (0,)), ((), ()))


def dot(a, b, dims):
    return lax.dot_general(a, b, dims, preferred_element_type=F32)


def after(value, *others):
    return lax.optimization_barrier((value,) + others)[0]


def norm_parts(values):
    center = jnp.mean(values, axis=-1, keepdims=True)
    deviation = values - center
    variance = jnp.mean(deviation * deviation, axis=-1, keepdims=True)
    rstd = lax.rsqrt(variance + epsilon)
    return deviation * rstd, rstd


def norm_backward(values, gain, upstream):
    unit, rstd = norm_parts(values)
    scaled = upstream * gain
    grad = rstd * (
        scaled
        - jnp.mean(scaled, axis=-1, keepdims=True)
        - unit * jnp.mean(scaled * unit, axis=-1, keepdims=True)
    )
    return grad, jnp.sum(upstream * unit, axis=0), jnp.sum(upstream, axis=0)


def split3(value):
    high = value.astype(BF).astype(F32)
    rest = value - high
    mid = rest.astype(BF).astype(F32)
    return high, mid, rest - mid


def place(lane, base, items):
    out = jnp.zeros(lane.shape, F32)
    for i, item in enumerate(items):
        out = jnp.where(lane == base + i, item, out)
    return out


def causal_end(row_block, size, length):
    return min(max((row_block + 1) * size, min(PREFIX_MOST, length)), length)


def fill_masks(masks, prefix, size, blocks, transposed):
    shape = (size, size)
    for index, (row_block, col_block) in enumerate(blocks):
        rows = row_block * size + lax.broadcasted_iota(jnp.int32, shape, 1 if transposed else 0)
        cols = col_block * size + lax.broadcasted_iota(jnp.int32, shape, 0 if transposed else 1)
        allowed = (cols <= rows) | ((cols < prefix) & (rows < prefix))
        beyond = jnp.maximum(cols - rows, 0).astype(F32)
        masks[index] = jnp.where(allowed, -2.0 * beyond, -1e30)


def special_blocks(length, size):
    out = []
    for row_block in range(length // size):
        for col_block in range(causal_end(row_block, size, length) // size):
            if col_block >= row_block:
                out.append((row_block, col_block))
    return out


def attend_forward_kernel(size, prefix_ref, slope_ref, joined_ref, context_ref, total_ref, masks):
    length = joined_ref.shape[0]
    pair = pl.program_id(0)
    blocks = special_blocks(length, size)

    @pl.when(pair == 0)
    def _():
        fill_masks(masks, prefix_ref[0], size, blocks, False)

    lane = lax.broadcasted_iota(jnp.int32, (length, 128), 1)
    low = lane < 64
    position = lax.broadcasted_iota(jnp.int32, (length, 1), 0).astype(F32)
    tiles = [joined_ref[:, i * 128 : (i + 1) * 128].astype(F32) for i in range(3)]
    rolled0 = pltpu.roll(tiles[0], 64, 1)
    rolled1 = pltpu.roll(tiles[1], 64, 1)
    sides = []
    for head in range(2):
        slope = slope_ref[pair * 2 + head]
        own = jnp.logical_not(low) if head == 0 else low
        base = 0 if head == 0 else 64
        query = jnp.where(own, (rolled0 if head == 0 else rolled1) * 0.125, place(lane, base, (1.0, 1.0, 1.0)))
        keys = jnp.where(own, tiles[0] if head == 0 else tiles[2], place(lane, base, split3(slope * position)))
        value = jnp.where(low, tiles[1], 1.0) if head == 0 else jnp.where(low, 1.0, tiles[2])
        sides.append((slope, query.astype(BF), keys.astype(BF), value.astype(BF)))
    low_block = low[:size]
    lane_block = lane[:size]
    for row_block in range(length // size):
        end = causal_end(row_block, size, length)
        rows = slice(row_block * size, (row_block + 1) * size)
        results = []
        for head in range(2):
            slope, query, keys, value = sides[head]
            scores = dot(query[rows], keys[:end], NT)
            columns = []
            for col_block in range(end // size):
                piece = scores[:, col_block * size : (col_block + 1) * size]
                if col_block >= row_block:
                    piece = piece + slope * masks[blocks.index((row_block, col_block))]
                columns.append(piece)
            highest = columns[0]
            for piece in columns[1:]:
                highest = jnp.maximum(highest, piece)
            highest = jnp.max(highest, axis=-1, keepdims=True)
            powered = jnp.concatenate([jnp.exp(piece - highest).astype(BF) for piece in columns], axis=1)
            gathered = dot(powered, value[:end], NN)
            total = gathered[:, 64:65] if head == 0 else gathered[:, 0:1]
            results.append((gathered / total, highest + jnp.log(total)))
        context_ref[rows, :] = jnp.where(low_block, results[0][0], results[1][0]).astype(BF)
        total_ref[rows, :] = jnp.where(lane_block == 0, results[0][1], results[1][1])


def attend_forward(joined, prefix, slopes, size=256):
    length, columns = joined.shape
    pairs = columns // 384
    count = len(special_blocks(length, size))
    return pl.pallas_call(
        partial(attend_forward_kernel, size),
        grid_spec=pltpu.PrefetchScalarGridSpec(
            num_scalar_prefetch=2,
            grid=(pairs,),
            in_specs=[pl.BlockSpec((length, 384), lambda p, *_: (0, p))],
            out_specs=[
                pl.BlockSpec((length, 128), lambda p, *_: (0, p)),
                pl.BlockSpec((length, 128), lambda p, *_: (0, p)),
            ],
            scratch_shapes=[pltpu.VMEM((count, size, size), F32)],
        ),
        out_shape=[
            jax.ShapeDtypeStruct((length, pairs * 128), BF),
            jax.ShapeDtypeStruct((length, pairs * 128), F32),
        ],
        compiler_params=pltpu.CompilerParams(vmem_limit_bytes=40 * 1024 * 1024),
        cost_estimate=pl.CostEstimate(flops=pairs * 2 * 2 * 2 * length * length * 128, bytes_accessed=4 * 1024 * 1024, transcendentals=0),
        name="attend_forward",
    )(prefix, slopes, joined)


def attend_backward_kernel(size, prefix_ref, slope_ref, joined_ref, total_ref, context_ref, grad_ref, out_ref, masks, query_sum):
    length = joined_ref.shape[0]
    pair = pl.program_id(0)
    blocks = special_blocks(length, size)

    @pl.when(pair == 0)
    def _():
        fill_masks(masks, prefix_ref[0], size, blocks, True)

    lane = lax.broadcasted_iota(jnp.int32, (length, 128), 1)
    low = lane < 64
    position = lax.broadcasted_iota(jnp.int32, (length, 1), 0).astype(F32)
    tiles = [joined_ref[:, i * 128 : (i + 1) * 128].astype(F32) for i in range(3)]
    rolled = [pltpu.roll(tile, 64, 1) for tile in tiles]
    grad = grad_ref[...].astype(F32)
    product = grad * context_ref[...].astype(F32)
    grad_low = grad.astype(BF)
    rolled_low = [tile.astype(BF) for tile in rolled]
    sides = []
    for head in range(2):
        slope = slope_ref[pair * 2 + head]
        own = jnp.logical_not(low) if head == 0 else low
        base = 0 if head == 0 else 64
        log_total = total_ref[:, head : head + 1]
        query = jnp.where(
            own, rolled[head] * 0.125, place(lane, base, (1.0, 1.0, 1.0) + split3(log_total))
        )
        keys = jnp.where(
            own, tiles[0] if head == 0 else tiles[2], place(lane, base, split3(slope * position) + (-1.0, -1.0, -1.0))
        )
        head_lanes = low if head == 0 else jnp.logical_not(low)
        inner = jnp.sum(jnp.where(head_lanes, product, 0.0), axis=1, keepdims=True)
        base = 64 - base
        value = jnp.where(head_lanes, tiles[1] if head == 0 else tiles[2], place(lane, 64 if head == 0 else 0, (-1.0, -1.0, -1.0)))
        upstream = jnp.where(head_lanes, grad, place(lane, 64 if head == 0 else 0, split3(inner)))
        sides.append((slope, query.astype(BF), keys.astype(BF), value.astype(BF), upstream.astype(BF)))
    low_block = low[:size]
    for col_block in range(length // size):
        first = col_block if col_block * size >= PREFIX_MOST else 0
        cols = slice(col_block * size, (col_block + 1) * size)
        start = first * size
        results = []
        for head in range(2):
            slope, query, keys, value, upstream = sides[head]
            scores = dot(keys[cols], query[start:], NT)
            prob_grad = dot(value[cols], upstream[start:], NT)
            weights, score_grads = [], []
            for row_block in range(first, length // size):
                at = slice((row_block - first) * size, (row_block - first + 1) * size)
                piece = scores[:, at]
                if col_block >= row_block:
                    piece = piece + slope * masks[blocks.index((row_block, col_block))]
                powered = jnp.exp(piece)
                weights.append(powered.astype(BF))
                score_grads.append((powered * prob_grad[:, at]).astype(BF))
            weights = jnp.concatenate(weights, axis=1)
            score_grads = jnp.concatenate(score_grads, axis=1)
            value_grad = dot(weights, grad_low[start:], NN)
            key_grad = dot(score_grads, rolled_low[head][start:], NN) * 0.125
            query_grad = dot(score_grads, rolled_low[0 if head == 0 else 2][cols], TN)
            if col_block == 0:
                query_sum[head] = query_grad
            else:
                query_sum[head, start:] = query_sum[head, start:] + query_grad
            results.append((key_grad, value_grad))
        (key0, value0), (key1, value1) = results
        out_ref[cols, 0:128] = key0.astype(BF)
        out_ref[cols, 128:256] = value0.astype(BF)
        out_ref[cols, 256:384] = jnp.where(low_block, key1, value1).astype(BF)
    out_ref[:, 0:128] = jnp.where(low, query_sum[0] * 0.125, out_ref[:, 0:128].astype(F32)).astype(BF)
    out_ref[:, 128:256] = jnp.where(low, out_ref[:, 128:256].astype(F32), query_sum[1] * 0.125).astype(BF)


def attend_backward(joined, log_totals, context, context_grad, prefix, slopes, size=256):
    length, columns = joined.shape
    pairs = columns // 384
    count = len(special_blocks(length, size))
    return pl.pallas_call(
        partial(attend_backward_kernel, size),
        grid_spec=pltpu.PrefetchScalarGridSpec(
            num_scalar_prefetch=2,
            grid=(pairs,),
            in_specs=[
                pl.BlockSpec((length, 384), lambda p, *_: (0, p)),
                pl.BlockSpec((length, 128), lambda p, *_: (0, p)),
                pl.BlockSpec((length, 128), lambda p, *_: (0, p)),
                pl.BlockSpec((length, 128), lambda p, *_: (0, p)),
            ],
            out_specs=pl.BlockSpec((length, 384), lambda p, *_: (0, p)),
            scratch_shapes=[pltpu.VMEM((count, size, size), F32), pltpu.VMEM((2, length, 128), F32)],
        ),
        out_shape=jax.ShapeDtypeStruct((length, columns), BF),
        compiler_params=pltpu.CompilerParams(vmem_limit_bytes=48 * 1024 * 1024),
        cost_estimate=pl.CostEstimate(flops=pairs * 2 * 5 * 2 * length * length * 128, bytes_accessed=6 * 1024 * 1024, transcendentals=0),
        name="attend_backward",
    )(prefix, slopes, joined, log_totals, context, context_grad)


def tensor_send(value, flip):
    return lax.ppermute(value, "tensor", [(i, i ^ flip) for i in range(4)])


def gather_blocks(value, gate=()):
    if gate:
        value = after(value, *gate)
    over_core = tensor_send(value, 1)
    over_x = tensor_send(value, 2)
    return [value, over_core, over_x, tensor_send(over_x, 1)]


def in_order(blocks, me):
    rows = blocks[0].shape[0]
    out = jnp.zeros((4 * rows, blocks[0].shape[1]), blocks[0].dtype)
    for flip, block in enumerate(blocks):
        out = lax.dynamic_update_slice_in_dim(out, block, (me ^ flip) * rows, 0)
    return out


def scatter_sum(block_of):
    over = tensor_send(block_of(3).astype(BF), 1)
    chip = (block_of(2) + over.astype(F32)).astype(BF)
    far = tensor_send(chip, 2)
    near = tensor_send(block_of(1).astype(BF), 1)
    return block_of(0) + near.astype(F32) + far.astype(F32)


def add_low(a, b):
    return (a.astype(F32) + b.astype(F32)).astype(BF)


def chain_sum(value, count, inner, place_of):
    def send(v, pairs):
        return lax.ppermute(v, "dp", [(a * inner + i, b * inner + i) for a, b in pairs for i in range(inner)])

    if count == 1:
        return value
    half = count // 2
    for step in range(half - 1):
        value = add_low(value, send(value, [(step, step + 1), (count - 1 - step, count - 2 - step)]))
    value = add_low(value, send(value, [(half - 1, half), (half, half - 1)]))
    for step in reversed(range(half - 1)):
        came = send(value, [(step + 1, step), (count - 2 - step, count - 1 - step)])
        value = jnp.where((place_of <= step) | (place_of >= count - 1 - step), came, value)
    return value


def dp_sum(term_of, rows, chunks, dp):
    inner = 2
    outer = dp // inner
    index = lax.axis_index("dp")
    mine, place_of = index % inner, index // inner
    pairs = [(i, i ^ 1) for i in range(dp)]
    size = rows // chunks
    half = size // 2
    pieces = []
    for chunk in range(chunks):
        sent = term_of(chunk * size + (1 - mine) * half, half).astype(BF)
        came = lax.ppermute(sent, "dp", pairs)
        value = (term_of(chunk * size + mine * half, half) + came.astype(F32)).astype(BF)
        value = chain_sum(value, outer, inner, place_of)
        other = lax.ppermute(value, "dp", pairs)
        first = jnp.where(mine == 0, value, other)
        second = jnp.where(mine == 0, other, value)
        pieces += [first, second]
    return jnp.concatenate(pieces, axis=0).astype(F32)


def small_sum(value, dp, axes):
    if "dp" in axes:
        step = 1
        while step < dp:
            value = value + lax.ppermute(value, "dp", [(i, i ^ step) for i in range(dp)])
            step *= 2
    if "tensor" in axes:
        for step in (1, 2):
            value = value + tensor_send(value, step)
    return value


def local(
    dp,
    hidden_in,
    out_grad,
    prefix_len,
    qkv_weight,
    qv_bias,
    dense_weight,
    dense_bias,
    norm1_gain,
    norm1_shift,
    norm2_gain,
    norm2_shift,
    fc1_weight,
    fc1_bias,
    fc2_weight,
    fc2_bias,
):
    rows_here, features = hidden_in.shape
    heads_here, _, head_size = qv_bias.shape
    me = lax.axis_index("tensor")
    slopes = 2.0 ** (-8.0 * (me * heads_here + 1 + lax.iota(jnp.int32, heads_here)).astype(F32) / HEADS)

    hidden_blocks = gather_blocks(hidden_in)
    dense_blocks = gather_blocks(dense_weight, (hidden_blocks[2],))
    grad_blocks = gather_blocks(out_grad, (dense_blocks[2],))

    residual_all = in_order(hidden_blocks, me).astype(F32)
    residual = hidden_in.astype(F32)
    length = residual_all.shape[0]
    normed1_all = (norm_parts(residual_all)[0] * norm1_gain + norm1_shift).astype(BF)
    bias_full = jnp.stack(
        [qv_bias[:, 0], jnp.zeros_like(qv_bias[:, 0]), qv_bias[:, 1]], axis=1
    ).reshape(-1)
    joined = (dot(normed1_all, qkv_weight, NN) + bias_full).astype(BF)
    context, log_totals = attend_forward(joined, prefix_len, slopes)
    context_blocks = gather_blocks(context)
    context_cat = jnp.concatenate(context_blocks, axis=1)
    dense_cat = jnp.concatenate(dense_blocks, axis=0)
    attn_all = dot(context_cat, dense_cat, NN) + dense_bias
    middle_all = residual_all + attn_all
    normed2_all = (norm_parts(middle_all)[0] * norm2_gain + norm2_shift).astype(BF)
    attn_out = lax.dynamic_slice_in_dim(attn_all, me * rows_here, rows_here, 0)
    middle = lax.dynamic_slice_in_dim(middle_all, me * rows_here, rows_here, 0)
    pre = dot(normed2_all, fc1_weight, NN) + fc1_bias
    cubic = 0.7978845608028654
    inner = jnp.tanh(cubic * (pre + 0.044715 * pre * pre * pre))
    activated = (0.5 * pre * (1.0 + inner)).astype(BF)
    slope_pre = 0.5 * (1.0 + inner) + 0.5 * pre * (1.0 - inner * inner) * cubic * (1.0 + 3 * 0.044715 * pre * pre)

    grad_all = in_order(grad_blocks, me)
    act_grad = dot(grad_all, fc2_weight, NT)
    pre_grad = (act_grad * slope_pre).astype(BF)

    def columns_of(array):
        return lambda first, count: lax.dynamic_slice_in_dim(array, first, count, 1)

    act_cols, pre_cols, normed2_cols = columns_of(activated), columns_of(pre_grad), columns_of(normed2_all)
    fc2_weight_grad = dp_sum(lambda a, n: dot(act_cols(a, n), grad_all, TN), activated.shape[1], 4, dp)
    fc1_weight_grad = dp_sum(lambda a, n: dot(normed2_cols(a, n), pre_grad, TN), features, 4, dp)

    def rows_of(array):
        return lambda flip: lax.dynamic_slice_in_dim(array, (me ^ flip) * rows_here, rows_here, 0)

    pre_rows, act_rows = rows_of(pre_grad), rows_of(activated)
    normed2_grad = scatter_sum(lambda flip: dot(pre_rows(flip), fc1_weight, NT))

    gout = out_grad.astype(F32)
    middle_norm_grad, norm2_gain_grad, norm2_shift_grad = norm_backward(middle, norm2_gain, normed2_grad)
    middle_grad = gout + middle_norm_grad
    middle_low = middle_grad.astype(BF)
    context_grads = [dot(middle_low, weight, NT).astype(BF) for weight in dense_blocks]
    arrived = [context_grads[0]] + [tensor_send(context_grads[flip], flip) for flip in (1, 2, 3)]
    context_grad = in_order(arrived, me)
    middle_all_low = in_order(gather_blocks(middle_low, (context_grad,)), me)
    context_cols = columns_of(context)
    dense_weight_grad = dp_sum(lambda a, n: dot(context_cols(a, n), middle_all_low, TN), context.shape[1], 1, dp)

    mlp_out = scatter_sum(lambda flip: dot(act_rows(flip), fc2_weight, NN)) + fc2_bias
    final = middle + mlp_out

    joined_grad = attend_backward(joined, log_totals, context, context_grad, prefix_len, slopes)
    normed1_cols = columns_of(normed1_all)
    qkv_weight_grad = dp_sum(lambda a, n: dot(normed1_cols(a, n), joined_grad, TN), features, 4, dp)
    joined_rows = rows_of(joined_grad)
    normed1_grad = scatter_sum(lambda flip: dot(joined_rows(flip), qkv_weight, NT))
    input_norm_grad, norm1_gain_grad, norm1_shift_grad = norm_backward(residual, norm1_gain, normed1_grad)
    hidden_grad = (middle_grad + input_norm_grad).astype(BF)

    joined_sums = jnp.sum(joined_grad.astype(F32), axis=0).reshape(heads_here, 3, head_size)
    qv_sums = jnp.stack([joined_sums[:, 0], joined_sums[:, 2]], axis=1).reshape(-1)
    squares = jnp.stack(
        [
            jnp.sum(residual * residual),
            jnp.sum(attn_out * attn_out),
            jnp.sum(mlp_out * mlp_out),
            jnp.sum(final * final),
        ]
    )
    by_dp = small_sum(
        jnp.stack(
            [
                jnp.sum(pre_grad.astype(F32), axis=0),
                jnp.pad(qv_sums, (0, features - qv_sums.shape[0])),
                jnp.pad(squares, (0, features - 4)),
                jnp.sum(middle_grad, axis=0),
                norm1_gain_grad,
                norm1_shift_grad,
                norm2_gain_grad,
                norm2_shift_grad,
                jnp.sum(gout, axis=0),
            ]
        ),
        dp,
        ("dp",),
    )
    by_all = small_sum(by_dp[2:], dp, ("tensor",))
    fc1_bias_grad = by_dp[0]
    qv_bias_grad = by_dp[1, : qv_sums.shape[0]].reshape(heads_here, 2, head_size)
    entry_count = rows_here * features * dp * 4
    sublayer_rms = jnp.sqrt(by_all[0, :4] / float(entry_count))
    return (
        final.astype(BF),
        hidden_grad,
        qkv_weight_grad,
        qv_bias_grad,
        dense_weight_grad,
        by_all[1],
        by_all[2],
        by_all[3],
        by_all[4],
        by_all[5],
        fc1_weight_grad,
        fc1_bias_grad,
        fc2_weight_grad,
        by_all[6],
        sublayer_rms,
    )


def solution(mesh):
    return jax.shard_map(
        partial(local, mesh.shape["dp"]),
        mesh=mesh,
        in_specs=(
            P(("dp", "tensor"), None),
            P(("dp", "tensor"), None),
            P("dp"),
            P(None, "tensor"),
            P("tensor", None, None),
            P("tensor", None),
            P(),
            P(),
            P(),
            P(),
            P(),
            P(None, "tensor"),
            P("tensor"),
            P("tensor", None),
            P(),
        ),
        out_specs=(
            P(("dp", "tensor"), None),
            P(("dp", "tensor"), None),
            P(None, "tensor"),
            P("tensor", None, None),
            P("tensor", None),
            P(),
            P(),
            P(),
            P(),
            P(),
            P(None, "tensor"),
            P("tensor"),
            P("tensor", None),
            P(),
            P(),
        ),
        check_vma=False,
    )
```

```python
from functools import partial

import jax
import jax.numpy as jnp
from jax import lax
from jax.experimental import pallas as pl
from jax.experimental.pallas import tpu as pltpu
from jax.sharding import PartitionSpec as P

HEADS = 16
PREFIX_MOST = 512

epsilon = 1e-05
BF = jnp.bfloat16
F32 = jnp.float32
NT = (((1,), (1,)), ((), ()))
NN = (((1,), (0,)), ((), ()))
TN = (((0,), (0,)), ((), ()))


def dot(a, b, dims):
    return lax.dot_general(a, b, dims, preferred_element_type=F32)


def after(value, *others):
    return lax.optimization_barrier((value,) + others)[0]


def norm_parts(values):
    center = jnp.mean(values, axis=-1, keepdims=True)
    deviation = values - center
    variance = jnp.mean(deviation * deviation, axis=-1, keepdims=True)
    rstd = lax.rsqrt(variance + epsilon)
    return deviation * rstd, rstd


def norm_backward(values, gain, upstream):
    unit, rstd = norm_parts(values)
    scaled = upstream * gain
    grad = rstd * (
        scaled
        - jnp.mean(scaled, axis=-1, keepdims=True)
        - unit * jnp.mean(scaled * unit, axis=-1, keepdims=True)
    )
    return grad, jnp.sum(upstream * unit, axis=0), jnp.sum(upstream, axis=0)


def split3(value):
    high = value.astype(BF).astype(F32)
    rest = value - high
    mid = rest.astype(BF).astype(F32)
    return high, mid, rest - mid


def place(lane, base, items):
    out = jnp.zeros(lane.shape, F32)
    for i, item in enumerate(items):
        out = jnp.where(lane == base + i, item, out)
    return out


def causal_end(row_block, size, length):
    return min(max((row_block + 1) * size, min(PREFIX_MOST, length)), length)


def fill_masks(masks, prefix, size, blocks, transposed):
    shape = (size, size)
    for index, (row_block, col_block) in enumerate(blocks):
        rows = row_block * size + lax.broadcasted_iota(jnp.int32, shape, 1 if transposed else 0)
        cols = col_block * size + lax.broadcasted_iota(jnp.int32, shape, 0 if transposed else 1)
        allowed = (cols <= rows) | ((cols < prefix) & (rows < prefix))
        beyond = jnp.maximum(cols - rows, 0).astype(F32)
        masks[index] = jnp.where(allowed, -2.0 * beyond, -1e30)


def special_blocks(length, size):
    out = []
    for row_block in range(length // size):
        for col_block in range(causal_end(row_block, size, length) // size):
            if col_block >= row_block:
                out.append((row_block, col_block))
    return out


def load_order(me_ref, near_ref, far_ref, joined_ref):
    half = near_ref.shape[0]
    chip = me_ref[0] >> 1
    joined_ref[pl.ds(pl.multiple_of(chip * half, half), half), :] = near_ref[...]
    joined_ref[pl.ds(pl.multiple_of((1 - chip) * half, half), half), :] = far_ref[...]


def attend_forward_kernel(size, prefix_ref, slope_ref, me_ref, near_ref, far_ref, context_ref, total_ref, masks, joined_ref):
    length = joined_ref.shape[0]
    pair = pl.program_id(0)
    load_order(me_ref, near_ref, far_ref, joined_ref)
    blocks = special_blocks(length, size)

    @pl.when(pair == 0)
    def _():
        fill_masks(masks, prefix_ref[0], size, blocks, False)

    lane = lax.broadcasted_iota(jnp.int32, (length, 128), 1)
    low = lane < 64
    position = lax.broadcasted_iota(jnp.int32, (length, 1), 0).astype(F32)
    tiles = [joined_ref[:, i * 128 : (i + 1) * 128].astype(F32) for i in range(3)]
    rolled0 = pltpu.roll(tiles[0], 64, 1)
    rolled1 = pltpu.roll(tiles[1], 64, 1)
    sides = []
    for head in range(2):
        slope = slope_ref[pair * 2 + head]
        own = jnp.logical_not(low) if head == 0 else low
        base = 0 if head == 0 else 64
        query = jnp.where(own, (rolled0 if head == 0 else rolled1) * 0.125, place(lane, base, (1.0, 1.0, 1.0)))
        keys = jnp.where(own, tiles[0] if head == 0 else tiles[2], place(lane, base, split3(slope * position)))
        value = jnp.where(low, tiles[1], 1.0) if head == 0 else jnp.where(low, 1.0, tiles[2])
        sides.append((slope, query.astype(BF), keys.astype(BF), value.astype(BF)))
    low_block = low[:size]
    lane_block = lane[:size]
    for row_block in range(length // size):
        end = causal_end(row_block, size, length)
        rows = slice(row_block * size, (row_block + 1) * size)
        results = []
        for head in range(2):
            slope, query, keys, value = sides[head]
            scores = dot(query[rows], keys[:end], NT)
            columns = []
            for col_block in range(end // size):
                piece = scores[:, col_block * size : (col_block + 1) * size]
                if col_block >= row_block:
                    piece = piece + slope * masks[blocks.index((row_block, col_block))]
                columns.append(piece)
            highest = columns[0]
            for piece in columns[1:]:
                highest = jnp.maximum(highest, piece)
            highest = jnp.max(highest, axis=-1, keepdims=True)
            powered = jnp.concatenate([jnp.exp(piece - highest).astype(BF) for piece in columns], axis=1)
            gathered = dot(powered, value[:end], NN)
            total = gathered[:, 64:65] if head == 0 else gathered[:, 0:1]
            results.append((gathered / total, highest + jnp.log(total)))
        context_ref[rows, :] = jnp.where(low_block, results[0][0], results[1][0]).astype(BF)
        total_ref[rows, :] = jnp.where(lane_block == 0, results[0][1], results[1][1])


def attend_forward(near, far, prefix, slopes, me, pair, size=256):
    length = 2 * near.shape[0]
    count = len(special_blocks(length, size))
    tile = pl.BlockSpec((length, 128), lambda p, *_: (0, 0))
    return pl.pallas_call(
        partial(attend_forward_kernel, size),
        grid_spec=pltpu.PrefetchScalarGridSpec(
            num_scalar_prefetch=3,
            grid=(1,),
            in_specs=[pl.BlockSpec((length // 2, 384), lambda p, *_: (0, pair))] * 2,
            out_specs=[tile, tile],
            scratch_shapes=[pltpu.VMEM((count, size, size), F32), pltpu.VMEM((length, 384), BF)],
        ),
        out_shape=[jax.ShapeDtypeStruct((length, 128), BF), jax.ShapeDtypeStruct((length, 128), F32)],
        compiler_params=pltpu.CompilerParams(vmem_limit_bytes=40 * 1024 * 1024),
        cost_estimate=pl.CostEstimate(flops=2 * 2 * 2 * length * length * 128, bytes_accessed=2 * 1024 * 1024, transcendentals=0),
        name="attend_forward",
    )(prefix, slopes[2 * pair : 2 * pair + 2], me, near, far)


def attend_backward_kernel(
    size, prefix_ref, slope_ref, me_ref, near_ref, far_ref, total_ref, context_ref, g0, g1, g2, g3,
    final_ref, masks, query_sum, grad_ref, joined_ref, out_ref,
):
    length = joined_ref.shape[0]
    pair = pl.program_id(0)
    load_order(me_ref, near_ref, far_ref, joined_ref)
    rows = g0.shape[0]
    for flip, ref in enumerate((g0, g1, g2, g3)):
        grad_ref[pl.ds(pl.multiple_of((me_ref[0] ^ flip) * rows, rows), rows), :] = ref[...]
    totals = total_ref[...]
    blocks = special_blocks(length, size)

    @pl.when(pair == 0)
    def _():
        fill_masks(masks, prefix_ref[0], size, blocks, True)

    lane = lax.broadcasted_iota(jnp.int32, (length, 128), 1)
    low = lane < 64
    position = lax.broadcasted_iota(jnp.int32, (length, 1), 0).astype(F32)
    tiles = [joined_ref[:, i * 128 : (i + 1) * 128].astype(F32) for i in range(3)]
    rolled = [pltpu.roll(tile, 64, 1) for tile in tiles]
    grad = grad_ref[...].astype(F32)
    product = grad * context_ref[...].astype(F32)
    grad_low = grad.astype(BF)
    rolled_low = [tile.astype(BF) for tile in rolled]
    sides = []
    for head in range(2):
        slope = slope_ref[pair * 2 + head]
        own = jnp.logical_not(low) if head == 0 else low
        base = 0 if head == 0 else 64
        log_total = totals[:, head : head + 1]
        query = jnp.where(
            own, rolled[head] * 0.125, place(lane, base, (1.0, 1.0, 1.0) + split3(log_total))
        )
        keys = jnp.where(
            own, tiles[0] if head == 0 else tiles[2], place(lane, base, split3(slope * position) + (-1.0, -1.0, -1.0))
        )
        head_lanes = low if head == 0 else jnp.logical_not(low)
        inner = jnp.sum(jnp.where(head_lanes, product, 0.0), axis=1, keepdims=True)
        base = 64 - base
        value = jnp.where(head_lanes, tiles[1] if head == 0 else tiles[2], place(lane, 64 if head == 0 else 0, (-1.0, -1.0, -1.0)))
        upstream = jnp.where(head_lanes, grad, place(lane, 64 if head == 0 else 0, split3(inner)))
        sides.append((slope, query.astype(BF), keys.astype(BF), value.astype(BF), upstream.astype(BF)))
    low_block = low[:size]
    for col_block in range(length // size):
        first = col_block if col_block * size >= PREFIX_MOST else 0
        cols = slice(col_block * size, (col_block + 1) * size)
        start = first * size
        results = []
        for head in range(2):
            slope, query, keys, value, upstream = sides[head]
            scores = dot(keys[cols], query[start:], NT)
            prob_grad = dot(value[cols], upstream[start:], NT)
            weights, score_grads = [], []
            for row_block in range(first, length // size):
                at = slice((row_block - first) * size, (row_block - first + 1) * size)
                piece = scores[:, at]
                if col_block >= row_block:
                    piece = piece + slope * masks[blocks.index((row_block, col_block))]
                powered = jnp.exp(piece)
                weights.append(powered.astype(BF))
                score_grads.append((powered * prob_grad[:, at]).astype(BF))
            weights = jnp.concatenate(weights, axis=1)
            score_grads = jnp.concatenate(score_grads, axis=1)
            value_grad = dot(weights, grad_low[start:], NN)
            key_grad = dot(score_grads, rolled_low[head][start:], NN) * 0.125
            query_grad = dot(score_grads, rolled_low[0 if head == 0 else 2][cols], TN)
            if col_block == 0:
                query_sum[head] = query_grad
            else:
                query_sum[head, start:] = query_sum[head, start:] + query_grad
            results.append((key_grad, value_grad))
        (key0, value0), (key1, value1) = results
        out_ref[cols, 0:128] = key0.astype(BF)
        out_ref[cols, 128:256] = value0.astype(BF)
        out_ref[cols, 256:384] = jnp.where(low_block, key1, value1).astype(BF)
    out_ref[:, 0:128] = jnp.where(low, query_sum[0] * 0.125, out_ref[:, 0:128].astype(F32)).astype(BF)
    out_ref[:, 128:256] = jnp.where(low, out_ref[:, 128:256].astype(F32), query_sum[1] * 0.125).astype(BF)
    half = length // 2
    chip = me_ref[0] >> 1
    final_ref[0:half, :] = out_ref[pl.ds(pl.multiple_of(chip * half, half), half), :]
    final_ref[half:, :] = out_ref[pl.ds(pl.multiple_of((1 - chip) * half, half), half), :]


def attend_backward(near, far, totals, context, grads, prefix, slopes, me, pair, size=256):
    length = 2 * near.shape[0]
    count = len(special_blocks(length, size))
    rows = grads[0].shape[0]
    tile = pl.BlockSpec((length, 128), lambda p, *_: (0, 0))
    return pl.pallas_call(
        partial(attend_backward_kernel, size),
        grid_spec=pltpu.PrefetchScalarGridSpec(
            num_scalar_prefetch=3,
            grid=(1,),
            in_specs=[pl.BlockSpec((length // 2, 384), lambda p, *_: (0, pair))] * 2
            + [tile, tile]
            + [pl.BlockSpec((rows, 128), lambda p, *_: (0, pair))] * 4,
            out_specs=pl.BlockSpec((length, 384), lambda p, *_: (0, 0)),
            scratch_shapes=[
                pltpu.VMEM((count, size, size), F32),
                pltpu.VMEM((2, length, 128), F32),
                pltpu.VMEM((length, 128), BF),
                pltpu.VMEM((length, 384), BF),
                pltpu.VMEM((length, 384), BF),
            ],
        ),
        out_shape=jax.ShapeDtypeStruct((length, 384), BF),
        compiler_params=pltpu.CompilerParams(vmem_limit_bytes=48 * 1024 * 1024),
        cost_estimate=pl.CostEstimate(flops=2 * 5 * 2 * length * length * 256, bytes_accessed=3 * 1024 * 1024, transcendentals=0),
        name="attend_backward",
    )(prefix, slopes[2 * pair : 2 * pair + 2], me, near, far, totals, context, *grads)


MIB = 1024 * 1024


def whole(shape):
    return pl.BlockSpec(shape, lambda *_: (0,) * len(shape))


def once(shape):
    return pl.BlockSpec(shape, lambda *_: (0,) * len(shape), pipeline_mode=pl.Buffered(1))


def project_kernel(me_ref, own_ref, near_ref, weight_ref, bias_ref, gain_ref, shift_ref, normed_ref, joined_ref):
    block = jnp.where(pl.program_id(0) == 0, own_ref[...].astype(F32), near_ref[...].astype(F32))
    normed = (norm_parts(block)[0] * gain_ref[...] + shift_ref[...]).astype(BF)
    normed_ref[...] = normed
    joined_ref[...] = (dot(normed, weight_ref[...], NN) + bias_ref[...]).astype(BF)


def project(me, blocks, weight, bias, gain, shift):
    rows, features = blocks[0].shape
    columns = weight.shape[1]
    return pl.pallas_call(
        project_kernel,
        grid_spec=pltpu.PrefetchScalarGridSpec(
            num_scalar_prefetch=1,
            grid=(2,),
            in_specs=[once((rows, features))] * 2
            + [once((features, columns)), once((1, columns)), once((1, features)), once((1, features))],
            out_specs=[
                pl.BlockSpec((rows, features), lambda g, me: ((me[0] & 1) ^ g, 0)),
                pl.BlockSpec((rows, columns), lambda g, me: ((me[0] & 1) ^ g, 0)),
            ],
        ),
        out_shape=[
            jax.ShapeDtypeStruct((2 * rows, features), BF),
            jax.ShapeDtypeStruct((2 * rows, columns), BF),
        ],
        compiler_params=pltpu.CompilerParams(vmem_limit_bytes=32 * 1024 * 1024),
        cost_estimate=pl.CostEstimate(flops=2 * 2 * rows * features * columns, bytes_accessed=6 * MIB, transcendentals=0),
        name="project",
    )(me, *blocks, weight, bias, gain, shift)


def middle_kernel(me_ref, *refs):
    (c0, c1, d0, d1, e0, e1, f0, f1, w0, w1, w2, w3, h0, h1, h2, h3, g0, g1, g2, g3, fc1_ref, fc2_ref, fc1_bias_ref,
     dense_bias_ref, gain_ref, shift_ref) = refs[:26]
    (normed_ref, act_ref, pre_ref, grad_ref, middle_ref, bias_sum_ref, squares_ref,
     part3_ref, part2_ref, part1_ref, part0_ref, hidden_ref) = refs[26:]
    step = pl.program_id(0)
    for at, (grad, hidden) in enumerate(((g3, h3), (g2, h2), (g1, h1), (g0, h0))):
        @pl.when(step == at)
        def _():
            grad_ref[...] = grad[...]
            hidden_ref[...] = hidden[...]
    grad = grad_ref[...]
    attn = dense_bias_ref[...]
    for halves, weight in (((c0, c1), w0), ((d0, d1), w1), ((e0, e1), w2), ((f0, f1), w3)):
        both = jnp.concatenate([half[...] for half in halves], axis=1)
        attn = attn + dot(both, weight[...], NN)
    middle = hidden_ref[...].astype(F32) + attn
    normed = (norm_parts(middle)[0] * gain_ref[...] + shift_ref[...]).astype(BF)
    normed_ref[...] = normed
    middle_ref[...] = middle
    squares_ref[...] = jnp.sum(attn * attn, axis=0, keepdims=True)
    pre = dot(normed, fc1_ref[...], NN) + fc1_bias_ref[...]
    act_grad = dot(grad, fc2_ref[...], NT)
    cubic = 0.7978845608028654
    square = pre * pre
    inner = jnp.tanh(pre * (cubic + cubic * 0.044715 * square))
    half = 0.5 + 0.5 * inner
    act = pre * half
    act_ref[...] = act.astype(BF)
    slope = half + act * (1.0 - inner) * (cubic + cubic * 3 * 0.044715 * square)
    pre_grad = (act_grad * slope).astype(BF)
    pre_ref[...] = pre_grad
    sums = jnp.sum(pre_grad.astype(F32), axis=0, keepdims=True)
    part = dot(pre_grad, fc1_ref[...], NT)

    @pl.when(step == 0)
    def _():
        bias_sum_ref[...] = sums

    @pl.when(step != 0)
    def _():
        bias_sum_ref[...] += sums

    for at, ref in enumerate((part3_ref, part2_ref, part1_ref, part0_ref)):
        @pl.when(step == at)
        def _():
            ref[...] = part.astype(ref.dtype)


def middle_part(me, contexts, weights, hidden, grads, fc1, fc2, fc1_bias, dense_bias, gain, shift):
    rows = hidden[0].shape[0]
    features, hidden_units = fc1.shape
    flip = lambda g, me: (3 - g, 0)
    placed = lambda g, me: (me[0] ^ (3 - g), 0)
    columns = contexts[0].shape[1]
    return pl.pallas_call(
        middle_kernel,
        grid_spec=pltpu.PrefetchScalarGridSpec(
            num_scalar_prefetch=1,
            grid=(4,),
            in_specs=[pl.BlockSpec((rows, columns), placed)] * 8
            + [once(w.shape) for w in weights]
            + [once((rows, features))] * 8
            + [once(fc1.shape), once(fc2.shape), once((1, hidden_units))] + [once((1, features))] * 3,
            out_specs=[
                pl.BlockSpec((rows, features), flip),
                pl.BlockSpec((rows, hidden_units), flip),
                pl.BlockSpec((rows, hidden_units), flip),
                pl.BlockSpec((rows, features), flip),
                whole((rows, features)),
                whole((1, hidden_units)),
                whole((1, features)),
            ]
            + [whole((rows, features))] * 4,
            scratch_shapes=[pltpu.VMEM((rows, features), BF)],
        ),
        out_shape=[
            jax.ShapeDtypeStruct((4 * rows, features), BF),
            jax.ShapeDtypeStruct((4 * rows, hidden_units), BF),
            jax.ShapeDtypeStruct((4 * rows, hidden_units), BF),
            jax.ShapeDtypeStruct((4 * rows, features), BF),
            jax.ShapeDtypeStruct((rows, features), F32),
            jax.ShapeDtypeStruct((1, hidden_units), F32),
            jax.ShapeDtypeStruct((1, features), F32),
        ]
        + [jax.ShapeDtypeStruct((rows, features), kind) for kind in (BF, F32, BF, F32)],
        compiler_params=pltpu.CompilerParams(vmem_limit_bytes=56 * 1024 * 1024),
        cost_estimate=pl.CostEstimate(flops=2 * 4 * rows * features * (features + 3 * hidden_units), bytes_accessed=14 * MIB, transcendentals=0),
        name="middle_part",
    )(me, *contexts, *weights, *hidden, *grads, fc1, fc2, fc1_bias, dense_bias, gain, shift)


def turn_kernel(part_ref, near_ref, far_ref, middle_ref, out_grad_ref, gain_ref, w0, w1, w2, w3,
                grad_ref, low_ref, g0, g1, g2, g3, sums_ref):
    upstream = part_ref[...] + near_ref[...].astype(F32) + far_ref[...].astype(F32)
    unit, rstd = norm_parts(middle_ref[...])
    scaled = upstream * gain_ref[...]
    grad = rstd * (
        scaled
        - jnp.mean(scaled, axis=-1, keepdims=True)
        - unit * jnp.mean(scaled * unit, axis=-1, keepdims=True)
    )
    out_grad = out_grad_ref[...].astype(F32)
    grad = grad + out_grad
    low = grad.astype(BF)
    grad_ref[...] = grad
    low_ref[...] = low
    for weight, ref in ((w0, g0), (w1, g1), (w2, g2), (w3, g3)):
        ref[...] = dot(low, weight[...], NT).astype(BF)
    sums_ref[0:1, :] = jnp.sum(grad, axis=0, keepdims=True)
    sums_ref[1:2, :] = jnp.sum(upstream * unit, axis=0, keepdims=True)
    sums_ref[2:3, :] = jnp.sum(upstream, axis=0, keepdims=True)
    sums_ref[3:4, :] = jnp.sum(out_grad, axis=0, keepdims=True)
    sums_ref[4:8, :] = jnp.zeros((4, grad.shape[1]), F32)


def turn(part, near, far, middle, out_grad, gain, weights):
    rows, features = middle.shape
    heads = weights[0].shape[0]
    return pl.pallas_call(
        turn_kernel,
        out_shape=[
            jax.ShapeDtypeStruct((rows, features), F32),
            jax.ShapeDtypeStruct((rows, features), BF),
        ]
        + [jax.ShapeDtypeStruct((rows, heads), BF)] * 4
        + [jax.ShapeDtypeStruct((8, features), F32)],
        compiler_params=pltpu.CompilerParams(vmem_limit_bytes=32 * 1024 * 1024),
        cost_estimate=pl.CostEstimate(flops=2 * 4 * rows * features * heads, bytes_accessed=7 * MIB, transcendentals=0),
        name="turn",
    )(part, near, far, middle, out_grad, gain, *weights)


def first_part_kernel(me_ref, grad_ref, weight_ref, part3_ref, part2_ref, part1_ref, part0_ref):
    step = pl.program_id(0)
    part = dot(grad_ref[...], weight_ref[...], NT)
    for at, ref in enumerate((part3_ref, part2_ref, part1_ref, part0_ref)):
        @pl.when(step == at)
        def _():
            ref[...] = part.astype(ref.dtype)


def first_part(me, grad, weight):
    rows, features = grad.shape[0] // 4, weight.shape[0]
    return pl.pallas_call(
        first_part_kernel,
        grid_spec=pltpu.PrefetchScalarGridSpec(
            num_scalar_prefetch=1,
            grid=(4,),
            in_specs=[pl.BlockSpec((rows, grad.shape[1]), lambda g, me: ((me[0] & 1) ^ (3 - g), 0)), once(weight.shape)],
            out_specs=[whole((rows, features))] * 4,
        ),
        out_shape=[jax.ShapeDtypeStruct((rows, features), kind) for kind in (BF, F32, BF, F32)],
        compiler_params=pltpu.CompilerParams(vmem_limit_bytes=32 * 1024 * 1024),
        cost_estimate=pl.CostEstimate(flops=2 * 4 * rows * features * grad.shape[1], bytes_accessed=6 * MIB, transcendentals=0),
        name="first_part",
    )(me, grad, weight)


def last_kernel(part_ref, near_ref, far_ref, hidden_ref, middle_grad_ref, gain_ref, out_ref, sums_ref):
    upstream = part_ref[...] + near_ref[...].astype(F32) + far_ref[...].astype(F32)
    unit, rstd = norm_parts(hidden_ref[...].astype(F32))
    scaled = upstream * gain_ref[...]
    grad = rstd * (
        scaled
        - jnp.mean(scaled, axis=-1, keepdims=True)
        - unit * jnp.mean(scaled * unit, axis=-1, keepdims=True)
    )
    out_ref[...] = (grad + middle_grad_ref[...]).astype(BF)
    sums_ref[0:1, :] = jnp.sum(upstream * unit, axis=0, keepdims=True)
    sums_ref[1:2, :] = jnp.sum(upstream, axis=0, keepdims=True)
    sums_ref[2:8, :] = jnp.zeros((6, grad.shape[1]), F32)


def last_norm(part, near, far, hidden, middle_grad, gain):
    rows, features = hidden.shape
    return pl.pallas_call(
        last_kernel,
        out_shape=[jax.ShapeDtypeStruct((rows, features), BF), jax.ShapeDtypeStruct((8, features), F32)],
        compiler_params=pltpu.CompilerParams(vmem_limit_bytes=32 * 1024 * 1024),
        cost_estimate=pl.CostEstimate(flops=2 * rows * features * 16, bytes_accessed=5 * MIB, transcendentals=0),
        name="last_norm",
    )(part, near, far, hidden, middle_grad, gain)


def tensor_send(value, flip):
    return lax.ppermute(value, "tensor", [(i, i ^ flip) for i in range(4)])


def add_low(a, b):
    return (a.astype(F32) + b.astype(F32)).astype(BF)


class Ladder:
    def __init__(self, dp, array):
        self.inner, self.outer = 2, dp // 2
        index = lax.axis_index("dp")
        self.mine, self.place_of = index % 2, index // 2
        self.pairs = [(i, i ^ 1) for i in range(dp)]
        self.array, self.half = array, array.shape[0] // 2
        half = self.outer // 2
        count = self.outer
        self.steps = [("in", s) for s in range(half - 1)] + ([("mid", 0)] if count > 1 else [])
        self.steps += [("out", s) for s in reversed(range(half - 1))]
        self.stages = len(self.steps) + 2
        self.stage = 0
        self.came = self.value = None
        self.open = False

    def along(self, pairs):
        return [(a * self.inner + i, b * self.inner + i) for a, b in pairs for i in range(self.inner)]

    def part(self, which):
        return lax.dynamic_slice_in_dim(self.array, which * self.half, self.half, 0)

    def send(self, *gate):
        count, half = self.outer, self.outer // 2
        if self.stage == 0:
            self.sent, pairs = self.part(1 - self.mine), self.pairs
        elif self.stage == self.stages - 1:
            self.sent, pairs = self.value, self.pairs
        else:
            kind, step = self.steps[self.stage - 1]
            self.sent = self.value
            if kind == "in":
                pairs = [(step, step + 1), (count - 1 - step, count - 2 - step)]
            elif kind == "mid":
                pairs = [(half - 1, half), (half, half - 1)]
            else:
                pairs = [(step + 1, step), (count - 2 - step, count - 1 - step)]
            pairs = self.along(pairs)
        if gate:
            self.sent = after(self.sent, *gate)
        self.came = lax.ppermute(self.sent, "dp", pairs)
        self.open = True
        return self

    def take(self, *gate):
        count = self.outer
        if gate and self.value is not None:
            self.value = after(self.value, *gate)
        if self.stage == 0:
            own = self.part(self.mine)
            if gate:
                own = after(own, *gate)
            self.value = add_low(own, self.came)
        elif self.stage < self.stages - 1:
            kind, step = self.steps[self.stage - 1]
            if kind == "out":
                outside = (self.place_of <= step) | (self.place_of >= count - 1 - step)
                self.value = jnp.where(outside, self.came, self.value)
            else:
                self.value = add_low(self.value, self.came)
        self.stage += 1
        self.open = False
        return self

    def finish(self):
        if self.came is not None and self.open:
            self.take()
        while self.stage < self.stages:
            self.send().take()
        return self

    def rows(self):
        lower = self.mine == 0
        return [jnp.where(lower, self.value, self.came), jnp.where(lower, self.came, self.value)]


class Spread:
    def __init__(self, dp, array):
        self.lines = [[a * 2 + i for a in range(dp // 2)] for i in range(2)]
        self.pairs = [(i, i ^ 1) for i in range(dp)]
        self.mine = lax.axis_index("dp") % 2
        self.array = array
        self.blocks = array.reshape(dp // 2, 2, array.shape[0] // dp, array.shape[1])

    def send(self):
        self.came = lax.ppermute(lax.dynamic_index_in_dim(self.blocks, 1 - self.mine, 1, False), "dp", self.pairs)

    def take(self, *gate):
        self.value = add_low(after(lax.dynamic_index_in_dim(self.blocks, self.mine, 1, False), *gate), self.came)
        return self

    def trade(self):
        self.terms = lax.all_to_all(self.value, "dp", 0, 0, axis_index_groups=self.lines, tiled=True)

    def add(self, *gate):
        self.value = jnp.sum(after(self.terms, *gate).astype(F32), axis=0).astype(BF)
        return self

    def gather(self):
        self.all = lax.all_gather(self.value, "dp", axis=0, tiled=True)


def joined_rows(ladders):
    return jnp.concatenate([piece for ladder in ladders for piece in ladder.rows()], axis=0).astype(F32)


def small_sum(value, dp, axes):
    if "dp" in axes:
        step = 1
        while step < dp:
            value = value + lax.ppermute(value, "dp", [(i, i ^ step) for i in range(dp)])
            step *= 2
    if "tensor" in axes:
        for step in (1, 2):
            value = value + tensor_send(value, step)
    return value


def local(
    dp,
    hidden_in,
    out_grad,
    prefix_len,
    qkv_weight,
    qv_bias,
    dense_weight,
    dense_bias,
    norm1_gain,
    norm1_shift,
    norm2_gain,
    norm2_shift,
    fc1_weight,
    fc1_bias,
    fc2_weight,
    fc2_bias,
):
    rows_here, features = hidden_in.shape
    heads_here, _, head_size = qv_bias.shape
    tensor_index = lax.axis_index("tensor")
    me = tensor_index.reshape(1)
    slopes = 2.0 ** (-8.0 * (tensor_index * heads_here + 1 + lax.iota(jnp.int32, heads_here)).astype(F32) / HEADS)
    bias_full = jnp.stack(
        [qv_bias[:, 0], jnp.zeros_like(qv_bias[:, 0]), qv_bias[:, 1]], axis=1
    ).reshape(1, -1)
    row = lambda v: v.reshape(1, -1)

    norm1 = (qkv_weight, bias_full, row(norm1_gain), row(norm1_shift))
    hidden_x = tensor_send(hidden_in, 2)
    hidden_c = tensor_send(hidden_in, 1)
    dense_c = tensor_send(dense_weight, 1)
    normed_near, joined_near = project(me, (hidden_in, hidden_c), *norm1)
    share = dense_weight.shape[0] // 2
    parity = lax.axis_index("dp") % 2
    dense_share = lax.dynamic_slice_in_dim(dense_weight, parity * share, share, 0)
    hidden_xc = tensor_send(after(hidden_x, joined_near), 1)
    dense_half = tensor_send(after(dense_share, hidden_x, joined_near), 2)
    normed_far, joined_far = project(me, (hidden_x, hidden_xc), *norm1)
    grad_c = tensor_send(after(out_grad, hidden_c), 1)
    context0, totals0 = attend_forward(joined_near, joined_far, prefix_len, slopes, me, 0)
    context0_x = tensor_send(context0, 2)
    context0_c = tensor_send(context0, 1)
    grad_x = tensor_send(after(out_grad, dense_half, context0), 2)
    dense_other = lax.ppermute(after(dense_half, context0), "dp", [(i, i ^ 1) for i in range(dp)])
    context1, totals1 = attend_forward(after(joined_near, context0_c), joined_far, prefix_len, slopes, me, 1)
    context1_x = tensor_send(context1, 2)
    context1_c = tensor_send(context1, 1)
    dense_x = jnp.where(
        parity == 0,
        jnp.concatenate([dense_half, dense_other], axis=0),
        jnp.concatenate([dense_other, dense_half], axis=0),
    )
    dense_xc = tensor_send(dense_x, 1)
    dense_blocks = [dense_weight, dense_c, dense_x, dense_xc]
    grad_xc = tensor_send(grad_x, 1)
    context0_xc = tensor_send(context0_x, 1)
    context1_xc = tensor_send(context1_x, 1)

    contexts = [context0, context1, context0_c, context1_c, context0_x, context1_x, context0_xc, context1_xc]
    (normed2_all, activated, pre_grad, grad_all, middle, fc1_bias_sum, attn_squares, part3, part2, part1, part0) = middle_part(
        me, contexts, dense_blocks, (hidden_in, hidden_c, hidden_x, hidden_xc), (out_grad, grad_c, grad_x, grad_xc),
        fc1_weight, fc2_weight, row(fc1_bias), row(dense_bias), row(norm2_gain), row(norm2_shift),
    )

    over = tensor_send(part3, 1)
    near = tensor_send(part1, 1)
    half = features // 2
    fc1_term = dot(normed2_all, pre_grad, TN).astype(BF)
    b1, b2 = Ladder(dp, fc1_term[:half]), Ladder(dp, fc1_term[half:])
    b1.send()
    chip = (after(part2, b1.sent) + over.astype(F32)).astype(BF)
    far = tensor_send(chip, 2)
    fc2_term = dot(after(activated, chip), grad_all, TN).astype(BF)
    a1, a2 = Ladder(dp, fc2_term[:half]), Ladder(dp, fc2_term[half:])
    b2.send(fc2_term)
    b1.take(b2.sent).send()
    middle_grad, middle_low, *context_grads, turn_sums = turn(
        after(part0, b1.value), near, far, middle, out_grad, row(norm2_gain), dense_blocks
    )
    arrived = [context_grads[0]] + [tensor_send(context_grads[flip], flip) for flip in (2, 3, 1)]
    arrived = [arrived[0], arrived[3], arrived[1], arrived[2]]
    b1.take(middle_low).send()
    b2.take(b1.value).send()
    joined_grad0 = attend_backward(
        after(joined_near, b2.value), joined_far, totals0, context0, arrived, prefix_len, slopes, me, 0
    )
    a1.send(joined_grad0)
    middle_x = tensor_send(after(middle_low, joined_grad0), 2)
    normed1_all = jnp.concatenate([after(normed_near, joined_grad0), normed_far], axis=0)
    b1.take(a1.sent).send()
    b2.take(b1.value).send()
    middle_c = tensor_send(after(middle_low, b2.value), 1)
    joined_grad1 = attend_backward(
        after(joined_near, b2.value, normed1_all), joined_far, totals1, context1, arrived, prefix_len, slopes, me, 1
    )
    a1.take(joined_grad1).send()
    a2.send(a1.value)
    middle_xc = tensor_send(after(middle_x, joined_grad1), 1)
    c1 = Ladder(dp, dot(after(normed1_all, a2.sent), joined_grad0, TN).astype(BF))
    b1.take(c1.array).send()
    b2.take(b1.value).send()
    a1.take(b2.value).send()
    a2.take(a1.value).send()
    c1.send(a2.value)
    qkv_term = dot(after(normed1_all, c1.sent), joined_grad1, TN).astype(BF)
    middle_all = jnp.concatenate([after(middle_low, c1.sent), middle_c, middle_x, middle_xc], axis=0)
    context = jnp.concatenate([context0, context1], axis=1)
    context_flip = jnp.concatenate(
        [lax.dynamic_slice_in_dim(context, (tensor_index ^ flip) * rows_here, rows_here, 0) for flip in range(4)], axis=0
    )
    dense_term = dot(after(middle_all, qkv_term), context_flip, TN).astype(BF)
    c2 = Ladder(dp, jnp.concatenate([qkv_term, dense_term], axis=1))
    b1.take(c2.array)
    b2.take(b1.value).send()
    a1.take(b2.value).send()
    a2.take(a1.value).send()
    c1.take(a2.value).send()
    c2.send(c1.value)
    joined_grad = jnp.concatenate([joined_grad0, joined_grad1], axis=1)
    last3, last2, last1, last0 = first_part(me, after(joined_grad, c2.sent), qkv_weight)
    b2.take(last0)
    a1.take(b2.value).send()
    a2.take(a1.value).send()
    c1.take(a2.value).send()
    c2.take(c1.value).send()
    last_over = tensor_send(after(last3, c2.value), 1)
    last_near = tensor_send(after(last1, c2.value), 1)
    late = after(activated, c2.value)
    mlp3, mlp2, mlp1, mlp0 = (
        dot(late[flip * rows_here : (flip + 1) * rows_here], fc2_weight, NN) for flip in (3, 2, 1, 0)
    )
    last_chip = (after(last2, mlp0) + last_over.astype(F32)).astype(BF)
    last_far = tensor_send(last_chip, 2)
    a1.take(last_chip)
    a2.take(a1.value).send()
    c1.take(a2.value).send()
    c2.take(c1.value).send()
    mlp_over = tensor_send(after(mlp3, c2.value).astype(BF), 1)
    mlp_near = tensor_send(after(mlp1, c2.value).astype(BF), 1)
    fc1_sum = joined_rows([b1, b2])
    hidden_grad, last_sums = last_norm(
        after(last0, c2.value), last_near, last_far, hidden_in, middle_grad, row(norm1_gain)
    )
    mlp_chip = (after(mlp2, hidden_grad) + mlp_over.astype(F32)).astype(BF)
    mlp_far = tensor_send(mlp_chip, 2)
    a2.take(mlp_chip)
    c1.take(a2.value).send()
    c2.take(c1.value).send()
    fc2_sum = joined_rows([a1, a2])
    mlp_out = after(mlp0, c2.value) + mlp_near.astype(F32) + mlp_far.astype(F32) + fc2_bias
    final = middle + mlp_out
    residual = hidden_in.astype(F32)
    c1.take(final)
    c2.take(c1.value).send()
    last_sums = after(last_sums, c2.value)
    c2.finish()
    last_sum = joined_rows([c2])

    joined_sums = jnp.sum(joined_grad.astype(F32), axis=0).reshape(heads_here, 3, head_size)
    qv_sums = jnp.stack([joined_sums[:, 0], joined_sums[:, 2]], axis=1).reshape(1, -1)
    squares = jnp.stack(
        [jnp.sum(residual * residual), jnp.sum(attn_squares), jnp.sum(mlp_out * mlp_out), jnp.sum(final * final)]
    ).reshape(1, -1)
    widen = lambda v: jnp.pad(v, ((0, 0), (0, features - v.shape[1])))
    by_dp = small_sum(
        jnp.concatenate(
            [fc1_bias_sum, widen(qv_sums), widen(squares), turn_sums[:4], last_sums[:2]], axis=0
        ),
        dp,
        ("dp",),
    )
    by_all = small_sum(by_dp[2:], dp, ("tensor",))
    qv_bias_grad = by_dp[1, : qv_sums.shape[1]].reshape(heads_here, 2, head_size)
    entry_count = rows_here * features * dp * 4
    sublayer_rms = jnp.sqrt(by_all[0, :4] / float(entry_count))
    return (
        final.astype(BF),
        hidden_grad,
        jnp.concatenate([joined_rows([c1]), last_sum[:, : qkv_term.shape[1]]], axis=1),
        qv_bias_grad,
        last_sum[:, qkv_term.shape[1] :].T,
        by_all[1],
        by_all[5],
        by_all[6],
        by_all[2],
        by_all[3],
        fc1_sum.astype(F32),
        by_dp[0],
        fc2_sum.astype(F32),
        by_all[4],
        sublayer_rms,
    )


def solution(mesh):
    return jax.shard_map(
        partial(local, mesh.shape["dp"]),
        mesh=mesh,
        in_specs=(
            P(("dp", "tensor"), None),
            P(("dp", "tensor"), None),
            P("dp"),
            P(None, "tensor"),
            P("tensor", None, None),
            P("tensor", None),
            P(),
            P(),
            P(),
            P(),
            P(),
            P(None, "tensor"),
            P("tensor"),
            P("tensor", None),
            P(),
        ),
        out_specs=(
            P(("dp", "tensor"), None),
            P(("dp", "tensor"), None),
            P(None, "tensor"),
            P("tensor", None, None),
            P("tensor", None),
            P(),
            P(),
            P(),
            P(),
            P(),
            P(None, "tensor"),
            P("tensor"),
            P("tensor", None),
            P(),
            P(),
        ),
        check_vma=False,
    )
```

```python
from functools import partial

import jax
import jax.numpy as jnp
from jax import lax
from jax.experimental import pallas as pl
from jax.experimental.pallas import tpu as pltpu
from jax.sharding import PartitionSpec as P

HEADS = 16
PREFIX_MOST = 512

epsilon = 1e-05
BF = jnp.bfloat16
F32 = jnp.float32
NT = (((1,), (1,)), ((), ()))
NN = (((1,), (0,)), ((), ()))
TN = (((0,), (0,)), ((), ()))


def dot(a, b, dims):
    return lax.dot_general(a, b, dims, preferred_element_type=F32)


def after(value, *others):
    return lax.optimization_barrier((value,) + others)[0]


def norm_parts(values):
    center = jnp.mean(values, axis=-1, keepdims=True)
    deviation = values - center
    variance = jnp.mean(deviation * deviation, axis=-1, keepdims=True)
    rstd = lax.rsqrt(variance + epsilon)
    return deviation * rstd, rstd


def norm_backward(values, gain, upstream):
    unit, rstd = norm_parts(values)
    scaled = upstream * gain
    grad = rstd * (
        scaled
        - jnp.mean(scaled, axis=-1, keepdims=True)
        - unit * jnp.mean(scaled * unit, axis=-1, keepdims=True)
    )
    return grad, jnp.sum(upstream * unit, axis=0), jnp.sum(upstream, axis=0)


def split3(value):
    high = value.astype(BF).astype(F32)
    rest = value - high
    mid = rest.astype(BF).astype(F32)
    return high, mid, rest - mid


def place(lane, base, items):
    out = jnp.zeros(lane.shape, F32)
    for i, item in enumerate(items):
        out = jnp.where(lane == base + i, item, out)
    return out


def causal_end(row_block, size, length):
    return min(max((row_block + 1) * size, min(PREFIX_MOST, length)), length)


def fill_masks(masks, prefix, size, blocks, transposed):
    shape = (size, size)
    for index, (row_block, col_block) in enumerate(blocks):
        rows = row_block * size + lax.broadcasted_iota(jnp.int32, shape, 1 if transposed else 0)
        cols = col_block * size + lax.broadcasted_iota(jnp.int32, shape, 0 if transposed else 1)
        allowed = (cols <= rows) | ((cols < prefix) & (rows < prefix))
        beyond = jnp.maximum(cols - rows, 0).astype(F32)
        masks[index] = jnp.where(allowed, -2.0 * beyond, -1e30)


def special_blocks(length, size):
    out = []
    for row_block in range(length // size):
        for col_block in range(causal_end(row_block, size, length) // size):
            if col_block >= row_block:
                out.append((row_block, col_block))
    return out


def load_order(me_ref, near_ref, far_ref, joined_ref):
    half = near_ref.shape[0]
    chip = me_ref[0] >> 1
    joined_ref[pl.ds(pl.multiple_of(chip * half, half), half), :] = near_ref[...]
    joined_ref[pl.ds(pl.multiple_of((1 - chip) * half, half), half), :] = far_ref[...]


def attend_forward_kernel(size, prefix_ref, slope_ref, me_ref, near_ref, far_ref, context_ref, total_ref, masks, joined_ref):
    length = joined_ref.shape[0]
    pair = pl.program_id(0)
    load_order(me_ref, near_ref, far_ref, joined_ref)
    blocks = special_blocks(length, size)

    @pl.when(pair == 0)
    def _():
        fill_masks(masks, prefix_ref[0], size, blocks, False)

    lane = lax.broadcasted_iota(jnp.int32, (length, 128), 1)
    low = lane < 64
    position = lax.broadcasted_iota(jnp.int32, (length, 1), 0).astype(F32)
    tiles = [joined_ref[:, i * 128 : (i + 1) * 128].astype(F32) for i in range(3)]
    rolled0 = pltpu.roll(tiles[0], 64, 1)
    rolled1 = pltpu.roll(tiles[1], 64, 1)
    sides = []
    for head in range(2):
        slope = slope_ref[pair * 2 + head]
        own = jnp.logical_not(low) if head == 0 else low
        base = 0 if head == 0 else 64
        query = jnp.where(own, (rolled0 if head == 0 else rolled1) * 0.125, place(lane, base, (1.0, 1.0, 1.0)))
        keys = jnp.where(own, tiles[0] if head == 0 else tiles[2], place(lane, base, split3(slope * position)))
        value = jnp.where(low, tiles[1], 1.0) if head == 0 else jnp.where(low, 1.0, tiles[2])
        sides.append((slope, query.astype(BF), keys.astype(BF), value.astype(BF)))
    low_block = low[:size]
    lane_block = lane[:size]
    for row_block in range(length // size):
        end = causal_end(row_block, size, length)
        rows = slice(row_block * size, (row_block + 1) * size)
        results = []
        for head in range(2):
            slope, query, keys, value = sides[head]
            scores = dot(query[rows], keys[:end], NT)
            columns = []
            for col_block in range(end // size):
                piece = scores[:, col_block * size : (col_block + 1) * size]
                if col_block >= row_block:
                    piece = piece + slope * masks[blocks.index((row_block, col_block))]
                columns.append(piece)
            highest = columns[0]
            for piece in columns[1:]:
                highest = jnp.maximum(highest, piece)
            highest = jnp.max(highest, axis=-1, keepdims=True)
            powered = jnp.concatenate([jnp.exp(piece - highest).astype(BF) for piece in columns], axis=1)
            gathered = dot(powered, value[:end], NN)
            total = gathered[:, 64:65] if head == 0 else gathered[:, 0:1]
            results.append((gathered / total, highest + jnp.log(total)))
        context_ref[rows, :] = jnp.where(low_block, results[0][0], results[1][0]).astype(BF)
        total_ref[rows, :] = jnp.where(lane_block == 0, results[0][1], results[1][1])


def attend_forward(near, far, prefix, slopes, me, size=256):
    length, columns = 2 * near.shape[0], near.shape[1]
    pairs = columns // 384
    count = len(special_blocks(length, size))
    tile = pl.BlockSpec((length, 128), lambda p, *_: (0, p))
    return pl.pallas_call(
        partial(attend_forward_kernel, size),
        grid_spec=pltpu.PrefetchScalarGridSpec(
            num_scalar_prefetch=3,
            grid=(pairs,),
            in_specs=[pl.BlockSpec((length // 2, 384), lambda p, *_: (0, p))] * 2,
            out_specs=[tile, tile],
            scratch_shapes=[pltpu.VMEM((count, size, size), F32), pltpu.VMEM((length, 384), BF)],
        ),
        out_shape=[
            jax.ShapeDtypeStruct((length, pairs * 128), BF),
            jax.ShapeDtypeStruct((length, pairs * 128), F32),
        ],
        compiler_params=pltpu.CompilerParams(vmem_limit_bytes=40 * 1024 * 1024),
        cost_estimate=pl.CostEstimate(flops=4 * 2 * 2 * length * length * 128, bytes_accessed=4 * 1024 * 1024, transcendentals=0),
        name="attend_forward",
    )(prefix, slopes, me, near, far)


def attend_backward_kernel(
    size, prefix_ref, slope_ref, me_ref, near_ref, far_ref, total_ref, context_ref, g0, g1, g2, g3,
    final_ref, masks, query_sum, grad_ref, joined_ref, out_ref,
):
    length = joined_ref.shape[0]
    pair = pl.program_id(0)
    load_order(me_ref, near_ref, far_ref, joined_ref)
    rows = g0.shape[0]
    for flip, ref in enumerate((g0, g1, g2, g3)):
        grad_ref[pl.ds(pl.multiple_of((me_ref[0] ^ flip) * rows, rows), rows), :] = ref[...]
    totals = total_ref[...]
    blocks = special_blocks(length, size)

    @pl.when(pair == 0)
    def _():
        fill_masks(masks, prefix_ref[0], size, blocks, True)

    lane = lax.broadcasted_iota(jnp.int32, (length, 128), 1)
    low = lane < 64
    position = lax.broadcasted_iota(jnp.int32, (length, 1), 0).astype(F32)
    tiles = [joined_ref[:, i * 128 : (i + 1) * 128].astype(F32) for i in range(3)]
    rolled = [pltpu.roll(tile, 64, 1) for tile in tiles]
    grad = grad_ref[...].astype(F32)
    product = grad * context_ref[...].astype(F32)
    grad_low = grad.astype(BF)
    rolled_low = [tile.astype(BF) for tile in rolled]
    sides = []
    for head in range(2):
        slope = slope_ref[pair * 2 + head]
        own = jnp.logical_not(low) if head == 0 else low
        base = 0 if head == 0 else 64
        log_total = totals[:, head : head + 1]
        query = jnp.where(
            own, rolled[head] * 0.125, place(lane, base, (1.0, 1.0, 1.0) + split3(log_total))
        )
        keys = jnp.where(
            own, tiles[0] if head == 0 else tiles[2], place(lane, base, split3(slope * position) + (-1.0, -1.0, -1.0))
        )
        head_lanes = low if head == 0 else jnp.logical_not(low)
        inner = jnp.sum(jnp.where(head_lanes, product, 0.0), axis=1, keepdims=True)
        base = 64 - base
        value = jnp.where(head_lanes, tiles[1] if head == 0 else tiles[2], place(lane, 64 if head == 0 else 0, (-1.0, -1.0, -1.0)))
        upstream = jnp.where(head_lanes, grad, place(lane, 64 if head == 0 else 0, split3(inner)))
        sides.append((slope, query.astype(BF), keys.astype(BF), value.astype(BF), upstream.astype(BF)))
    low_block = low[:size]
    for col_block in range(length // size):
        first = col_block if col_block * size >= PREFIX_MOST else 0
        cols = slice(col_block * size, (col_block + 1) * size)
        start = first * size
        results = []
        for head in range(2):
            slope, query, keys, value, upstream = sides[head]
            scores = dot(keys[cols], query[start:], NT)
            prob_grad = dot(value[cols], upstream[start:], NT)
            weights, score_grads = [], []
            for row_block in range(first, length // size):
                at = slice((row_block - first) * size, (row_block - first + 1) * size)
                piece = scores[:, at]
                if col_block >= row_block:
                    piece = piece + slope * masks[blocks.index((row_block, col_block))]
                powered = jnp.exp(piece)
                weights.append(powered.astype(BF))
                score_grads.append((powered * prob_grad[:, at]).astype(BF))
            weights = jnp.concatenate(weights, axis=1)
            score_grads = jnp.concatenate(score_grads, axis=1)
            value_grad = dot(weights, grad_low[start:], NN)
            key_grad = dot(score_grads, rolled_low[head][start:], NN) * 0.125
            query_grad = dot(score_grads, rolled_low[0 if head == 0 else 2][cols], TN)
            if col_block == 0:
                query_sum[head] = query_grad
            else:
                query_sum[head, start:] = query_sum[head, start:] + query_grad
            results.append((key_grad, value_grad))
        (key0, value0), (key1, value1) = results
        out_ref[cols, 0:128] = key0.astype(BF)
        out_ref[cols, 128:256] = value0.astype(BF)
        out_ref[cols, 256:384] = jnp.where(low_block, key1, value1).astype(BF)
    out_ref[:, 0:128] = jnp.where(low, query_sum[0] * 0.125, out_ref[:, 0:128].astype(F32)).astype(BF)
    out_ref[:, 128:256] = jnp.where(low, out_ref[:, 128:256].astype(F32), query_sum[1] * 0.125).astype(BF)
    half = length // 2
    chip = me_ref[0] >> 1
    final_ref[0:half, :] = out_ref[pl.ds(pl.multiple_of(chip * half, half), half), :]
    final_ref[half:, :] = out_ref[pl.ds(pl.multiple_of((1 - chip) * half, half), half), :]


def attend_backward(near, far, totals, context, grads, prefix, slopes, me, pair, size=256):
    length = 2 * near.shape[0]
    count = len(special_blocks(length, size))
    rows = grads[0].shape[0]
    return pl.pallas_call(
        partial(attend_backward_kernel, size),
        grid_spec=pltpu.PrefetchScalarGridSpec(
            num_scalar_prefetch=3,
            grid=(1,),
            in_specs=[pl.BlockSpec((length // 2, 384), lambda p, *_: (0, pair))] * 2
            + [pl.BlockSpec((length, 128), lambda p, *_: (0, pair))] * 2
            + [pl.BlockSpec((rows, 128), lambda p, *_: (0, pair))] * 4,
            out_specs=pl.BlockSpec((length, 384), lambda p, *_: (0, 0)),
            scratch_shapes=[
                pltpu.VMEM((count, size, size), F32),
                pltpu.VMEM((2, length, 128), F32),
                pltpu.VMEM((length, 128), BF),
                pltpu.VMEM((length, 384), BF),
                pltpu.VMEM((length, 384), BF),
            ],
        ),
        out_shape=jax.ShapeDtypeStruct((length, 384), BF),
        compiler_params=pltpu.CompilerParams(vmem_limit_bytes=48 * 1024 * 1024),
        cost_estimate=pl.CostEstimate(flops=2 * 5 * 2 * length * length * 256, bytes_accessed=3 * 1024 * 1024, transcendentals=0),
        name="attend_backward",
    )(prefix, slopes[2 * pair : 2 * pair + 2], me, near, far, totals, context, *grads)


MIB = 1024 * 1024


def whole(shape):
    return pl.BlockSpec(shape, lambda *_: (0,) * len(shape))


def once(shape):
    return pl.BlockSpec(shape, lambda *_: (0,) * len(shape), pipeline_mode=pl.Buffered(1))


def project_kernel(me_ref, own_ref, near_ref, weight_ref, bias_ref, gain_ref, shift_ref, normed_ref, joined_ref):
    block = jnp.where(pl.program_id(0) == 0, own_ref[...].astype(F32), near_ref[...].astype(F32))
    normed = (norm_parts(block)[0] * gain_ref[...] + shift_ref[...]).astype(BF)
    normed_ref[...] = normed
    joined_ref[...] = (dot(normed, weight_ref[...], NN) + bias_ref[...]).astype(BF)


def project(me, blocks, weight, bias, gain, shift):
    rows, features = blocks[0].shape
    columns = weight.shape[1]
    return pl.pallas_call(
        project_kernel,
        grid_spec=pltpu.PrefetchScalarGridSpec(
            num_scalar_prefetch=1,
            grid=(2,),
            in_specs=[once((rows, features))] * 2
            + [once((features, columns)), once((1, columns)), once((1, features)), once((1, features))],
            out_specs=[
                pl.BlockSpec((rows, features), lambda g, me: ((me[0] & 1) ^ g, 0)),
                pl.BlockSpec((rows, columns), lambda g, me: ((me[0] & 1) ^ g, 0)),
            ],
        ),
        out_shape=[
            jax.ShapeDtypeStruct((2 * rows, features), BF),
            jax.ShapeDtypeStruct((2 * rows, columns), BF),
        ],
        compiler_params=pltpu.CompilerParams(vmem_limit_bytes=32 * 1024 * 1024),
        cost_estimate=pl.CostEstimate(flops=2 * 2 * rows * features * columns, bytes_accessed=6 * MIB, transcendentals=0),
        name="project",
    )(me, *blocks, weight, bias, gain, shift)


def middle_kernel(me_ref, *refs):
    (c0, c1, c2, c3, w0, w1, w2, w3, hidden_ref, grad_ref, fc1_ref, fc2_ref, fc1_bias_ref,
     dense_bias_ref, gain_ref, shift_ref) = refs[:16]
    (normed_ref, act_ref, pre_ref, middle_ref, bias_sum_ref, squares_ref,
     part3_ref, part2_ref, part1_ref, part0_ref) = refs[16:]
    step = pl.program_id(0)
    grad = grad_ref[...]
    attn = dense_bias_ref[...]
    for context_ref, weight in ((c0, w0), (c1, w1), (c2, w2), (c3, w3)):
        attn = attn + dot(context_ref[...], weight[...], NN)
    middle = hidden_ref[...].astype(F32) + attn
    normed = (norm_parts(middle)[0] * gain_ref[...] + shift_ref[...]).astype(BF)
    normed_ref[...] = normed
    middle_ref[...] = middle
    squares_ref[...] = jnp.sum(attn * attn, axis=0, keepdims=True)
    pre = dot(normed, fc1_ref[...], NN) + fc1_bias_ref[...]
    act_grad = dot(grad, fc2_ref[...], NT)
    cubic = 0.7978845608028654
    square = pre * pre
    inner = jnp.tanh(pre * (cubic + cubic * 0.044715 * square))
    half = 0.5 + 0.5 * inner
    act = pre * half
    act_ref[...] = act.astype(BF)
    slope = half + act * (1.0 - inner) * (cubic + cubic * 3 * 0.044715 * square)
    pre_grad = (act_grad * slope).astype(BF)
    pre_ref[...] = pre_grad
    sums = jnp.sum(pre_grad.astype(F32), axis=0, keepdims=True)
    part = dot(pre_grad, fc1_ref[...], NT)

    @pl.when(step == 0)
    def _():
        bias_sum_ref[...] = sums

    @pl.when(step != 0)
    def _():
        bias_sum_ref[...] += sums

    for at, ref in enumerate((part3_ref, part2_ref, part1_ref, part0_ref)):
        @pl.when(step == at)
        def _():
            ref[...] = part.astype(ref.dtype)


def middle_part(me, contexts, weights, hidden, grad, fc1, fc2, fc1_bias, dense_bias, gain, shift):
    rows = hidden.shape[0] // 4
    features, hidden_units = fc1.shape
    flip = lambda g, me: (3 - g, 0)
    placed = lambda g, me: (me[0] ^ (3 - g), 0)
    columns = contexts[0].shape[1]
    return pl.pallas_call(
        middle_kernel,
        grid_spec=pltpu.PrefetchScalarGridSpec(
            num_scalar_prefetch=1,
            grid=(4,),
            in_specs=[pl.BlockSpec((rows, columns), placed)] * 4
            + [once(w.shape) for w in weights]
            + [pl.BlockSpec((rows, features), flip)] * 2
            + [once(fc1.shape), once(fc2.shape), once((1, hidden_units))] + [once((1, features))] * 3,
            out_specs=[
                pl.BlockSpec((rows, features), flip),
                pl.BlockSpec((rows, hidden_units), flip),
                pl.BlockSpec((rows, hidden_units), flip),
                whole((rows, features)),
                whole((1, hidden_units)),
                whole((1, features)),
            ]
            + [whole((rows, features))] * 4,
        ),
        out_shape=[
            jax.ShapeDtypeStruct((4 * rows, features), BF),
            jax.ShapeDtypeStruct((4 * rows, hidden_units), BF),
            jax.ShapeDtypeStruct((4 * rows, hidden_units), BF),
            jax.ShapeDtypeStruct((rows, features), F32),
            jax.ShapeDtypeStruct((1, hidden_units), F32),
            jax.ShapeDtypeStruct((1, features), F32),
        ]
        + [jax.ShapeDtypeStruct((rows, features), kind) for kind in (BF, F32, BF, F32)],
        compiler_params=pltpu.CompilerParams(vmem_limit_bytes=48 * 1024 * 1024),
        cost_estimate=pl.CostEstimate(flops=2 * 4 * rows * features * (features + 3 * hidden_units), bytes_accessed=14 * MIB, transcendentals=0),
        name="middle_part",
    )(me, *contexts, *weights, hidden, grad, fc1, fc2, fc1_bias, dense_bias, gain, shift)


def turn_kernel(part_ref, near_ref, far_ref, middle_ref, out_grad_ref, gain_ref, w0, w1, w2, w3,
                grad_ref, low_ref, g0, g1, g2, g3, sums_ref):
    upstream = part_ref[...] + near_ref[...].astype(F32) + far_ref[...].astype(F32)
    unit, rstd = norm_parts(middle_ref[...])
    scaled = upstream * gain_ref[...]
    grad = rstd * (
        scaled
        - jnp.mean(scaled, axis=-1, keepdims=True)
        - unit * jnp.mean(scaled * unit, axis=-1, keepdims=True)
    )
    out_grad = out_grad_ref[...].astype(F32)
    grad = grad + out_grad
    low = grad.astype(BF)
    grad_ref[...] = grad
    low_ref[...] = low
    for weight, ref in ((w0, g0), (w1, g1), (w2, g2), (w3, g3)):
        ref[...] = dot(low, weight[...], NT).astype(BF)
    sums_ref[0:1, :] = jnp.sum(grad, axis=0, keepdims=True)
    sums_ref[1:2, :] = jnp.sum(upstream * unit, axis=0, keepdims=True)
    sums_ref[2:3, :] = jnp.sum(upstream, axis=0, keepdims=True)
    sums_ref[3:4, :] = jnp.sum(out_grad, axis=0, keepdims=True)
    sums_ref[4:8, :] = jnp.zeros((4, grad.shape[1]), F32)


def turn(part, near, far, middle, out_grad, gain, weights):
    rows, features = middle.shape
    heads = weights[0].shape[0]
    return pl.pallas_call(
        turn_kernel,
        out_shape=[
            jax.ShapeDtypeStruct((rows, features), F32),
            jax.ShapeDtypeStruct((rows, features), BF),
        ]
        + [jax.ShapeDtypeStruct((rows, heads), BF)] * 4
        + [jax.ShapeDtypeStruct((8, features), F32)],
        compiler_params=pltpu.CompilerParams(vmem_limit_bytes=32 * 1024 * 1024),
        cost_estimate=pl.CostEstimate(flops=2 * 4 * rows * features * heads, bytes_accessed=7 * MIB, transcendentals=0),
        name="turn",
    )(part, near, far, middle, out_grad, gain, *weights)


def rows_kernel(dims, me_ref, left_ref, weight_ref, part3_ref, part2_ref, part1_ref, part0_ref):
    step = pl.program_id(0)
    part = dot(left_ref[...], weight_ref[...], dims)
    for at, ref in enumerate((part3_ref, part2_ref, part1_ref, part0_ref)):
        @pl.when(step == at)
        def _():
            ref[...] = part.astype(ref.dtype)


def rows_product(me, left, weight, dims, order):
    rows = left.shape[0] // 4
    features = weight.shape[1] if dims is NN else weight.shape[0]
    return pl.pallas_call(
        partial(rows_kernel, dims),
        grid_spec=pltpu.PrefetchScalarGridSpec(
            num_scalar_prefetch=1,
            grid=(4,),
            in_specs=[pl.BlockSpec((rows, left.shape[1]), lambda g, me: (order(3 - g, me), 0)), once(weight.shape)],
            out_specs=[whole((rows, features))] * 4,
        ),
        out_shape=[jax.ShapeDtypeStruct((rows, features), kind) for kind in (BF, F32, BF, F32)],
        compiler_params=pltpu.CompilerParams(vmem_limit_bytes=32 * 1024 * 1024),
        cost_estimate=pl.CostEstimate(flops=2 * 4 * rows * features * left.shape[1], bytes_accessed=6 * MIB, transcendentals=0),
        name="rows_product",
    )(me, left, weight)


def last_kernel(part_ref, near_ref, far_ref, hidden_ref, middle_grad_ref, gain_ref, out_ref):
    upstream = part_ref[...] + near_ref[...].astype(F32) + far_ref[...].astype(F32)
    unit, rstd = norm_parts(hidden_ref[...].astype(F32))
    scaled = upstream * gain_ref[...]
    grad = rstd * (
        scaled
        - jnp.mean(scaled, axis=-1, keepdims=True)
        - unit * jnp.mean(scaled * unit, axis=-1, keepdims=True)
    )
    out_ref[...] = (grad + middle_grad_ref[...]).astype(BF)


def last_norm(part, near, far, hidden, middle_grad, gain):
    rows, features = hidden.shape
    return pl.pallas_call(
        last_kernel,
        out_shape=jax.ShapeDtypeStruct((rows, features), BF),
        compiler_params=pltpu.CompilerParams(vmem_limit_bytes=32 * 1024 * 1024),
        cost_estimate=pl.CostEstimate(flops=2 * rows * features * 16, bytes_accessed=5 * MIB, transcendentals=0),
        name="last_norm",
    )(part, near, far, hidden, middle_grad, gain)


def last_product_kernel(me_ref, left_ref, hidden_ref, weight_ref, part3_ref, part2_ref, part1_ref, part0_ref, sums_ref, bias_ref):
    step = pl.program_id(0)
    left = left_ref[...]
    part = dot(left, weight_ref[...], NT)
    for at, ref in enumerate((part3_ref, part2_ref, part1_ref, part0_ref)):
        @pl.when(step == at)
        def _():
            ref[...] = part.astype(ref.dtype)
    unit, _ = norm_parts(hidden_ref[...].astype(F32))
    gain_sum = jnp.sum(part * unit, axis=0, keepdims=True)
    shift_sum = jnp.sum(part, axis=0, keepdims=True)
    bias_sum = jnp.sum(left.astype(F32), axis=0, keepdims=True)

    @pl.when(step == 0)
    def _():
        sums_ref[0:1, :] = gain_sum
        sums_ref[1:2, :] = shift_sum
        bias_ref[...] = bias_sum

    @pl.when(step != 0)
    def _():
        sums_ref[0:1, :] += gain_sum
        sums_ref[1:2, :] += shift_sum
        bias_ref[...] += bias_sum


def last_product(me, left, hidden, weight):
    rows, features, columns = left.shape[0] // 4, weight.shape[0], left.shape[1]
    return pl.pallas_call(
        last_product_kernel,
        grid_spec=pltpu.PrefetchScalarGridSpec(
            num_scalar_prefetch=1,
            grid=(4,),
            in_specs=[
                pl.BlockSpec((rows, columns), lambda g, me: ((me[0] & 1) ^ (3 - g), 0)),
                pl.BlockSpec((rows, features), lambda g, me: (3 - g, 0)),
                once(weight.shape),
            ],
            out_specs=[whole((rows, features))] * 4 + [whole((2, features)), whole((1, columns))],
        ),
        out_shape=[jax.ShapeDtypeStruct((rows, features), kind) for kind in (BF, F32, BF, F32)]
        + [jax.ShapeDtypeStruct((2, features), F32), jax.ShapeDtypeStruct((1, columns), F32)],
        compiler_params=pltpu.CompilerParams(vmem_limit_bytes=32 * 1024 * 1024),
        cost_estimate=pl.CostEstimate(flops=2 * 4 * rows * features * columns, bytes_accessed=6 * MIB, transcendentals=0),
        name="last_product",
    )(me, left, hidden, weight)


def finish_kernel(rows, parity_ref, c1_value, c1_came, c2_value, c2_came, qkv_ref, dense_ref, small_ref):
    first = pl.program_id(0) == parity_ref[0]

    def put(one, two):
        width = two.shape[1]
        qkv_ref[:, 0:width] = one[:, 0:width].astype(F32)
        qkv_ref[:, width : 2 * width] = two[0:rows, :].astype(F32)
        dense_ref[...] = one[:, width:].astype(F32).T
        small_ref[...] = two[rows:, :].astype(F32)

    @pl.when(first)
    def _():
        put(c1_value, c2_value)

    @pl.when(jnp.logical_not(first))
    def _():
        put(c1_came, c2_came)


def finish(parity, c1, c2):
    half, both = c1.value.shape
    full, width = c2.value.shape
    extra, more = both - width, full - half
    return pl.pallas_call(
        partial(finish_kernel, half),
        grid_spec=pltpu.PrefetchScalarGridSpec(
            num_scalar_prefetch=1,
            grid=(2,),
            in_specs=[once((half, both))] * 2 + [once((full, width))] * 2,
            out_specs=[
                pl.BlockSpec((half, 2 * width), lambda g, *_: (g, 0)),
                pl.BlockSpec((extra, half), lambda g, *_: (0, g)),
                pl.BlockSpec((more, width), lambda g, *_: (g, 0)),
            ],
        ),
        out_shape=[
            jax.ShapeDtypeStruct((2 * half, 2 * width), F32),
            jax.ShapeDtypeStruct((extra, 2 * half), F32),
            jax.ShapeDtypeStruct((2 * more, width), F32),
        ],
        compiler_params=pltpu.CompilerParams(vmem_limit_bytes=32 * 1024 * 1024),
        cost_estimate=pl.CostEstimate(flops=1024, bytes_accessed=6 * MIB, transcendentals=0),
        name="finish",
    )(parity, c1.value, c1.came, c2.value, c2.came)


def tensor_send(value, flip):
    return lax.ppermute(value, "tensor", [(i, i ^ flip) for i in range(4)])


def add_low(a, b):
    return (a.astype(F32) + b.astype(F32)).astype(BF)


class Ladder:
    def __init__(self, dp, array):
        self.inner, self.outer = 2, dp // 2
        index = lax.axis_index("dp")
        self.mine, self.place_of = index % 2, index // 2
        self.pairs = [(i, i ^ 1) for i in range(dp)]
        self.array, self.half = array, array.shape[0] // 2
        half = self.outer // 2
        count = self.outer
        self.steps = [("in", s) for s in range(half - 1)] + ([("mid", 0)] if count > 1 else [])
        self.steps += [("out", s) for s in reversed(range(half - 1))]
        self.stages = len(self.steps) + 2
        self.stage = 0
        self.came = self.value = None
        self.open = False

    def along(self, pairs):
        return [(a * self.inner + i, b * self.inner + i) for a, b in pairs for i in range(self.inner)]

    def part(self, which):
        return lax.dynamic_slice_in_dim(self.array, which * self.half, self.half, 0)

    def send(self, *gate):
        count, half = self.outer, self.outer // 2
        if self.stage == 0:
            self.sent, pairs = self.part(1 - self.mine), self.pairs
        elif self.stage == self.stages - 1:
            self.sent, pairs = self.value, self.pairs
        else:
            kind, step = self.steps[self.stage - 1]
            self.sent = self.value
            if kind == "in":
                pairs = [(step, step + 1), (count - 1 - step, count - 2 - step)]
            elif kind == "mid":
                pairs = [(half - 1, half), (half, half - 1)]
            else:
                pairs = [(step + 1, step), (count - 2 - step, count - 1 - step)]
            pairs = self.along(pairs)
        if gate:
            self.sent = after(self.sent, *gate)
        self.came = lax.ppermute(self.sent, "dp", pairs)
        self.open = True
        return self

    def take(self, *gate):
        count = self.outer
        if gate and self.value is not None:
            self.value = after(self.value, *gate)
        if self.stage == 0:
            own = self.part(self.mine)
            if gate:
                own = after(own, *gate)
            self.value = add_low(own, self.came)
        elif self.stage < self.stages - 1:
            kind, step = self.steps[self.stage - 1]
            if kind == "out":
                outside = (self.place_of <= step) | (self.place_of >= count - 1 - step)
                self.value = jnp.where(outside, self.came, self.value)
            else:
                self.value = add_low(self.value, self.came)
        self.stage += 1
        self.open = False
        return self

    def finish(self):
        if self.came is not None and self.open:
            self.take()
        while self.stage < self.stages:
            self.send().take()
        return self

    def rows(self):
        lower = self.mine == 0
        return [jnp.where(lower, self.value, self.came), jnp.where(lower, self.came, self.value)]


class Spread:
    def __init__(self, dp, array):
        self.lines = [[a * 2 + i for a in range(dp // 2)] for i in range(2)]
        self.pairs = [(i, i ^ 1) for i in range(dp)]
        self.mine = lax.axis_index("dp") % 2
        self.array = array
        self.blocks = array.reshape(dp // 2, 2, array.shape[0] // dp, array.shape[1])

    def send(self):
        self.came = lax.ppermute(lax.dynamic_index_in_dim(self.blocks, 1 - self.mine, 1, False), "dp", self.pairs)

    def take(self, *gate):
        self.value = add_low(after(lax.dynamic_index_in_dim(self.blocks, self.mine, 1, False), *gate), self.came)
        return self

    def trade(self):
        self.terms = lax.all_to_all(self.value, "dp", 0, 0, axis_index_groups=self.lines, tiled=True)

    def add(self, *gate):
        self.value = jnp.sum(after(self.terms, *gate).astype(F32), axis=0).astype(BF)
        return self

    def gather(self):
        self.all = lax.all_gather(self.value, "dp", axis=0, tiled=True)


def joined_rows(ladders):
    return jnp.concatenate([piece for ladder in ladders for piece in ladder.rows()], axis=0).astype(F32)


def local(
    dp,
    hidden_in,
    out_grad,
    prefix_len,
    qkv_weight,
    qv_bias,
    dense_weight,
    dense_bias,
    norm1_gain,
    norm1_shift,
    norm2_gain,
    norm2_shift,
    fc1_weight,
    fc1_bias,
    fc2_weight,
    fc2_bias,
):
    rows_here, features = hidden_in.shape
    heads_here, _, head_size = qv_bias.shape
    tensor_index = lax.axis_index("tensor")
    me = tensor_index.reshape(1)
    slopes = 2.0 ** (-8.0 * (tensor_index * heads_here + 1 + lax.iota(jnp.int32, heads_here)).astype(F32) / HEADS)
    bias_full = jnp.stack(
        [qv_bias[:, 0], jnp.zeros_like(qv_bias[:, 0]), qv_bias[:, 1]], axis=1
    ).reshape(1, -1)
    row = lambda v: v.reshape(1, -1)

    norm1 = (qkv_weight, bias_full, row(norm1_gain), row(norm1_shift))
    hidden_x = tensor_send(hidden_in, 2)
    hidden_c = tensor_send(hidden_in, 1)
    dense_c = tensor_send(dense_weight, 1)
    normed_near, joined_near = project(me, (hidden_in, hidden_c), *norm1)
    share = dense_weight.shape[0] // 2
    parity = lax.axis_index("dp") % 2
    dense_share = lax.dynamic_slice_in_dim(dense_weight, parity * share, share, 0)
    hidden_xc = tensor_send(after(hidden_x, joined_near), 1)
    dense_half = tensor_send(after(dense_share, hidden_x, joined_near), 2)
    grad_x = tensor_send(after(out_grad, hidden_x, joined_near), 2)
    normed_far, joined_far = project(me, (hidden_x, hidden_xc), *norm1)
    grad_c = tensor_send(after(out_grad, hidden_c), 1)
    context, totals = attend_forward(joined_near, joined_far, prefix_len, slopes, me)
    context_x = tensor_send(context, 2)
    context_c = tensor_send(context, 1)
    dense_other = lax.ppermute(after(dense_half, context), "dp", [(i, i ^ 1) for i in range(dp)])
    dense_x = jnp.where(
        parity == 0,
        jnp.concatenate([dense_half, dense_other], axis=0),
        jnp.concatenate([dense_other, dense_half], axis=0),
    )
    dense_xc = tensor_send(dense_x, 1)
    dense_blocks = [dense_weight, dense_c, dense_x, dense_xc]
    grad_xc = tensor_send(after(grad_x, context), 1)
    grad_all = jnp.concatenate([out_grad, grad_c, grad_x, grad_xc], axis=0)
    hidden_all = jnp.concatenate([hidden_in, hidden_c, hidden_x, after(hidden_xc, context)], axis=0)
    context_xc = tensor_send(after(context_x, grad_all, hidden_all), 1)

    (normed2_all, activated, pre_grad, middle, fc1_bias_sum, attn_squares, part3, part2, part1, part0) = middle_part(
        me, (context, context_c, context_x, context_xc), dense_blocks, hidden_all, grad_all,
        fc1_weight, fc2_weight, row(fc1_bias), row(dense_bias), row(norm2_gain), row(norm2_shift),
    )

    over = tensor_send(part3, 1)
    near = tensor_send(part1, 1)
    half = features // 2
    fc1_term = dot(normed2_all, pre_grad, TN).astype(BF)
    b1, b2 = Ladder(dp, fc1_term[:half]), Ladder(dp, fc1_term[half:])
    b1.send()
    chip = (after(part2, b1.sent) + over.astype(F32)).astype(BF)
    far = tensor_send(chip, 2)
    fc2_term = dot(after(activated, chip), grad_all, TN).astype(BF)
    a1, a2 = Ladder(dp, fc2_term[:half]), Ladder(dp, fc2_term[half:])
    b2.send(fc2_term)
    mlp3, mlp2, mlp1, mlp0 = rows_product(me, after(activated, b2.sent), fc2_weight, NN, lambda g, me: g)
    b1.take(mlp0).send()
    middle_grad, middle_low, *context_grads, turn_sums = turn(
        after(part0, b1.value), near, far, middle, out_grad, row(norm2_gain), dense_blocks
    )
    arrived = [context_grads[0]] + [tensor_send(context_grads[flip], flip) for flip in (2, 3, 1)]
    arrived = [arrived[0], arrived[3], arrived[1], arrived[2]]
    mlp_over = tensor_send(after(mlp3, arrived[1]), 1)
    mlp_near = tensor_send(after(mlp1, arrived[1]), 1)
    b1.take(arrived[1]).send()
    b2.take(b1.value).send()
    middle_x = tensor_send(after(middle_low, arrived[2]), 2)
    a1.send(b2.value)
    mlp_chip = (after(mlp2, a1.sent) + mlp_over.astype(F32)).astype(BF)
    joined_grad0 = attend_backward(
        after(joined_near, a1.sent, mlp_chip), joined_far, totals, context, arrived, prefix_len, slopes, me, 0
    )
    b1.take(joined_grad0).send()
    b2.take(b1.value).send()
    a1.take(b2.value).send()
    middle_c = tensor_send(after(middle_low, a1.value), 1)
    middle_xc = tensor_send(after(middle_x, a1.value), 1)
    a2.send(middle_xc)
    mlp_far = tensor_send(after(mlp_chip, middle_xc), 2)
    normed1_all = jnp.concatenate([after(normed_near, a2.sent), normed_far], axis=0)
    joined_grad1 = attend_backward(
        after(joined_near, a2.sent), joined_far, totals, context, arrived, prefix_len, slopes, me, 1
    )
    width = joined_grad1.shape[1]
    qkv_term = dot(normed1_all, joined_grad1, TN).astype(BF)
    middle_all = jnp.concatenate([after(middle_low, qkv_term), middle_c, middle_x, middle_xc], axis=0)
    context_flip = jnp.concatenate(
        [
            lax.dynamic_slice_in_dim(after(context, qkv_term), (tensor_index ^ flip) * rows_here, rows_here, 0)
            for flip in range(4)
        ],
        axis=0,
    )
    dense_term = dot(middle_all, context_flip, TN).astype(BF)
    joined_grad = jnp.concatenate([joined_grad0, after(joined_grad1, dense_term)], axis=1)
    last3, last2, last1, last0, last_sums, joined_sums = last_product(me, joined_grad, hidden_all, qkv_weight)
    b1.take(last0).send()
    b2.take(b1.value).send()
    a1.take(b2.value).send()
    a2.take(a1.value).send()
    qkv_first = dot(after(normed1_all, dense_term), joined_grad0, TN).astype(BF)
    c1 = Ladder(dp, jnp.concatenate([qkv_first, after(dense_term, a2.value)], axis=1))
    c1.send()
    mlp_out = after(mlp0, c1.sent) + mlp_near.astype(F32) + mlp_far.astype(F32) + fc2_bias
    final = middle + mlp_out
    residual = hidden_in.astype(F32)
    column_squares = lambda v: jnp.sum(v * v, axis=0, keepdims=True)
    joined_sums = joined_sums.reshape(heads_here, 3, head_size)
    qv_sums = jnp.stack([joined_sums[:, 0], joined_sums[:, 2]], axis=1).reshape(1, -1)
    small = jnp.concatenate(
        [column_squares(residual), attn_squares, column_squares(mlp_out), column_squares(final), turn_sums[:4], last_sums],
        axis=0,
    )
    small = small + tensor_send(small, 1)
    small = small + tensor_send(small, 2)
    small = jnp.concatenate(
        [fc1_bias_sum, jnp.pad(qv_sums, ((0, 0), (0, features - qv_sums.shape[1]))), small], axis=0
    )
    small = jnp.pad(small, ((0, 16 - small.shape[0]), (0, 4 * width - features))).astype(BF)
    small_blocks = [small[:, i * width : (i + 1) * width] for i in range(4)]
    b1.take(small)
    c2 = Ladder(dp, jnp.concatenate([qkv_term[:half], *small_blocks[:2], qkv_term[half:], *small_blocks[2:]], axis=0))
    c2.send(b1.came)
    b2.take(c2.sent).send()
    a1.take(b2.value).send()
    a2.take(a1.value).send()
    c1.take(a2.value).send()
    b2.take(c1.value)
    last_over = tensor_send(after(last3, b2.came), 1)
    last_near = tensor_send(after(last1, b2.came), 1)
    a1.take(b2.came).send()
    a2.take(a1.value).send()
    c1.take(a2.value).send()
    c2.take(c1.value).send()
    last_chip = (after(last2, c2.value) + last_over.astype(F32)).astype(BF)
    last_far = tensor_send(last_chip, 2)
    fc1_sum = after(joined_rows([b1, b2]), last_chip)
    a1.take(fc1_sum)
    a2.take(a1.came).send()
    c1.take(a2.value).send()
    c2.take(c1.value).send()
    hidden_grad = last_norm(after(last0, c2.value), last_near, last_far, hidden_in, middle_grad, row(norm1_gain))
    a2.take(hidden_grad)
    c1.take(a2.came).send()
    c2.take(c1.value).send()
    fc2_sum = after(joined_rows([a1, a2]), c2.value)
    c1.take(fc2_sum)
    c2.take(c1.came).send()
    c2.finish()
    qkv_sum, dense_sum, small_sum = finish(parity.reshape(1), c1, c2)
    by_dp = jnp.concatenate([small_sum[i * 16 : (i + 1) * 16] for i in range(4)], axis=1)[:, :features]
    by_all = by_dp[5:]
    qv_bias_grad = by_dp[1, : qv_sums.shape[1]].reshape(heads_here, 2, head_size)
    entry_count = rows_here * features * dp * 4
    sublayer_rms = jnp.sqrt(jnp.sum(by_dp[2:6], axis=1) / float(entry_count))
    return (
        final.astype(BF),
        hidden_grad,
        qkv_sum,
        qv_bias_grad,
        dense_sum,
        by_all[1],
        by_all[5],
        by_all[6],
        by_all[2],
        by_all[3],
        fc1_sum.astype(F32),
        by_dp[0],
        fc2_sum.astype(F32),
        by_all[4],
        sublayer_rms,
    )


def solution(mesh):
    return jax.shard_map(
        partial(local, mesh.shape["dp"]),
        mesh=mesh,
        in_specs=(
            P(("dp", "tensor"), None),
            P(("dp", "tensor"), None),
            P("dp"),
            P(None, "tensor"),
            P("tensor", None, None),
            P("tensor", None),
            P(),
            P(),
            P(),
            P(),
            P(),
            P(None, "tensor"),
            P("tensor"),
            P("tensor", None),
            P(),
        ),
        out_specs=(
            P(("dp", "tensor"), None),
            P(("dp", "tensor"), None),
            P(None, "tensor"),
            P("tensor", None, None),
            P("tensor", None),
            P(),
            P(),
            P(),
            P(),
            P(),
            P(None, "tensor"),
            P("tensor"),
            P("tensor", None),
            P(),
            P(),
        ),
        check_vma=False,
    )
```

```python
from functools import partial

import jax
import jax.numpy as jnp
from jax import lax
from jax.experimental import pallas as pl
from jax.experimental.pallas import tpu as pltpu
from jax.sharding import PartitionSpec as P

HEADS = 16
PREFIX_MOST = 512

epsilon = 1e-05
BF = jnp.bfloat16
F32 = jnp.float32
NT = (((1,), (1,)), ((), ()))
NN = (((1,), (0,)), ((), ()))
TN = (((0,), (0,)), ((), ()))


def dot(a, b, dims):
    return lax.dot_general(a, b, dims, preferred_element_type=F32)


def after(value, *others):
    return lax.optimization_barrier((value,) + others)[0]


def norm_parts(values):
    center = jnp.mean(values, axis=-1, keepdims=True)
    deviation = values - center
    variance = jnp.mean(deviation * deviation, axis=-1, keepdims=True)
    rstd = lax.rsqrt(variance + epsilon)
    return deviation * rstd, rstd


def norm_backward(values, gain, upstream):
    unit, rstd = norm_parts(values)
    scaled = upstream * gain
    grad = rstd * (
        scaled
        - jnp.mean(scaled, axis=-1, keepdims=True)
        - unit * jnp.mean(scaled * unit, axis=-1, keepdims=True)
    )
    return grad, jnp.sum(upstream * unit, axis=0), jnp.sum(upstream, axis=0)


def split3(value):
    high = value.astype(BF).astype(F32)
    rest = value - high
    mid = rest.astype(BF).astype(F32)
    return high, mid, rest - mid


def place(lane, base, items):
    out = jnp.zeros(lane.shape, F32)
    for i, item in enumerate(items):
        out = jnp.where(lane == base + i, item, out)
    return out


def causal_end(row_block, size, length):
    return min(max((row_block + 1) * size, min(PREFIX_MOST, length)), length)


def fill_masks(masks, prefix, size, blocks, transposed):
    shape = (size, size)
    for index, (row_block, col_block) in enumerate(blocks):
        rows = row_block * size + lax.broadcasted_iota(jnp.int32, shape, 1 if transposed else 0)
        cols = col_block * size + lax.broadcasted_iota(jnp.int32, shape, 0 if transposed else 1)
        allowed = (cols <= rows) | ((cols < prefix) & (rows < prefix))
        beyond = jnp.maximum(cols - rows, 0).astype(F32)
        masks[index] = jnp.where(allowed, -2.0 * beyond, -1e30)


def special_blocks(length, size):
    out = []
    for row_block in range(length // size):
        for col_block in range(causal_end(row_block, size, length) // size):
            if col_block >= row_block:
                out.append((row_block, col_block))
    return out


def load_order(me_ref, near_ref, far_ref, joined_ref):
    half = near_ref.shape[0]
    chip = me_ref[0] >> 1
    joined_ref[pl.ds(pl.multiple_of(chip * half, half), half), :] = near_ref[...]
    joined_ref[pl.ds(pl.multiple_of((1 - chip) * half, half), half), :] = far_ref[...]


def attend_forward_kernel(size, prefix_ref, slope_ref, me_ref, near_ref, far_ref, context_ref, total_ref, masks, joined_ref):
    length = joined_ref.shape[0]
    pair = pl.program_id(0)
    load_order(me_ref, near_ref, far_ref, joined_ref)
    blocks = special_blocks(length, size)

    @pl.when(pair == 0)
    def _():
        fill_masks(masks, prefix_ref[0], size, blocks, False)

    lane = lax.broadcasted_iota(jnp.int32, (length, 128), 1)
    low = lane < 64
    position = lax.broadcasted_iota(jnp.int32, (length, 1), 0).astype(F32)
    tiles = [joined_ref[:, i * 128 : (i + 1) * 128].astype(F32) for i in range(3)]
    rolled0 = pltpu.roll(tiles[0], 64, 1)
    rolled1 = pltpu.roll(tiles[1], 64, 1)
    sides = []
    for head in range(2):
        slope = slope_ref[pair * 2 + head]
        own = jnp.logical_not(low) if head == 0 else low
        base = 0 if head == 0 else 64
        query = jnp.where(own, (rolled0 if head == 0 else rolled1) * 0.125, place(lane, base, (1.0, 1.0, 1.0)))
        keys = jnp.where(own, tiles[0] if head == 0 else tiles[2], place(lane, base, split3(slope * position)))
        value = jnp.where(low, tiles[1], 1.0) if head == 0 else jnp.where(low, 1.0, tiles[2])
        sides.append((slope, query.astype(BF), keys.astype(BF), value.astype(BF)))
    low_block = low[:size]
    lane_block = lane[:size]
    for row_block in range(length // size):
        end = causal_end(row_block, size, length)
        rows = slice(row_block * size, (row_block + 1) * size)
        results = []
        for head in range(2):
            slope, query, keys, value = sides[head]
            scores = dot(query[rows], keys[:end], NT)
            columns = []
            for col_block in range(end // size):
                piece = scores[:, col_block * size : (col_block + 1) * size]
                if col_block >= row_block:
                    piece = piece + slope * masks[blocks.index((row_block, col_block))]
                columns.append(piece)
            highest = columns[0]
            for piece in columns[1:]:
                highest = jnp.maximum(highest, piece)
            highest = jnp.max(highest, axis=-1, keepdims=True)
            powered = jnp.concatenate([jnp.exp(piece - highest).astype(BF) for piece in columns], axis=1)
            gathered = dot(powered, value[:end], NN)
            total = gathered[:, 64:65] if head == 0 else gathered[:, 0:1]
            results.append((gathered / total, highest + jnp.log(total)))
        context_ref[rows, :] = jnp.where(low_block, results[0][0], results[1][0]).astype(BF)
        total_ref[rows, :] = jnp.where(lane_block == 0, results[0][1], results[1][1])


def attend_forward(near, far, prefix, slopes, me, size=256):
    length, columns = 2 * near.shape[0], near.shape[1]
    pairs = columns // 384
    count = len(special_blocks(length, size))
    tile = pl.BlockSpec((length, 128), lambda p, *_: (0, p))
    return pl.pallas_call(
        partial(attend_forward_kernel, size),
        grid_spec=pltpu.PrefetchScalarGridSpec(
            num_scalar_prefetch=3,
            grid=(pairs,),
            in_specs=[pl.BlockSpec((length // 2, 384), lambda p, *_: (0, p))] * 2,
            out_specs=[tile, tile],
            scratch_shapes=[pltpu.VMEM((count, size, size), F32), pltpu.VMEM((length, 384), BF)],
        ),
        out_shape=[
            jax.ShapeDtypeStruct((length, pairs * 128), BF),
            jax.ShapeDtypeStruct((length, pairs * 128), F32),
        ],
        compiler_params=pltpu.CompilerParams(vmem_limit_bytes=40 * 1024 * 1024),
        cost_estimate=pl.CostEstimate(flops=4 * 2 * 2 * length * length * 128, bytes_accessed=4 * 1024 * 1024, transcendentals=0),
        name="attend_forward",
    )(prefix, slopes, me, near, far)


def attend_backward_kernel(
    size, prefix_ref, slope_ref, me_ref, near_ref, far_ref, total_ref, context_ref, g0, g1, g2, g3,
    final_ref, masks, query_sum, grad_ref, joined_ref, out_ref,
):
    length = joined_ref.shape[0]
    pair = pl.program_id(0)
    load_order(me_ref, near_ref, far_ref, joined_ref)
    rows = g0.shape[0]
    for flip, ref in enumerate((g0, g1, g2, g3)):
        grad_ref[pl.ds(pl.multiple_of((me_ref[0] ^ flip) * rows, rows), rows), :] = ref[...]
    totals = total_ref[...]
    blocks = special_blocks(length, size)

    @pl.when(pair == 0)
    def _():
        fill_masks(masks, prefix_ref[0], size, blocks, True)

    lane = lax.broadcasted_iota(jnp.int32, (length, 128), 1)
    low = lane < 64
    position = lax.broadcasted_iota(jnp.int32, (length, 1), 0).astype(F32)
    tiles = [joined_ref[:, i * 128 : (i + 1) * 128].astype(F32) for i in range(3)]
    rolled = [pltpu.roll(tile, 64, 1) for tile in tiles]
    grad = grad_ref[...].astype(F32)
    product = grad * context_ref[...].astype(F32)
    grad_low = grad.astype(BF)
    rolled_low = [tile.astype(BF) for tile in rolled]
    sides = []
    for head in range(2):
        slope = slope_ref[pair * 2 + head]
        own = jnp.logical_not(low) if head == 0 else low
        base = 0 if head == 0 else 64
        log_total = totals[:, head : head + 1]
        query = jnp.where(
            own, rolled[head] * 0.125, place(lane, base, (1.0, 1.0, 1.0) + split3(log_total))
        )
        keys = jnp.where(
            own, tiles[0] if head == 0 else tiles[2], place(lane, base, split3(slope * position) + (-1.0, -1.0, -1.0))
        )
        head_lanes = low if head == 0 else jnp.logical_not(low)
        inner = jnp.sum(jnp.where(head_lanes, product, 0.0), axis=1, keepdims=True)
        base = 64 - base
        value = jnp.where(head_lanes, tiles[1] if head == 0 else tiles[2], place(lane, 64 if head == 0 else 0, (-1.0, -1.0, -1.0)))
        upstream = jnp.where(head_lanes, grad, place(lane, 64 if head == 0 else 0, split3(inner)))
        sides.append((slope, query.astype(BF), keys.astype(BF), value.astype(BF), upstream.astype(BF)))
    low_block = low[:size]
    for col_block in range(length // size):
        first = col_block if col_block * size >= PREFIX_MOST else 0
        cols = slice(col_block * size, (col_block + 1) * size)
        start = first * size
        results = []
        for head in range(2):
            slope, query, keys, value, upstream = sides[head]
            scores = dot(keys[cols], query[start:], NT)
            prob_grad = dot(value[cols], upstream[start:], NT)
            weights, score_grads = [], []
            for row_block in range(first, length // size):
                at = slice((row_block - first) * size, (row_block - first + 1) * size)
                piece = scores[:, at]
                if col_block >= row_block:
                    piece = piece + slope * masks[blocks.index((row_block, col_block))]
                powered = jnp.exp(piece)
                weights.append(powered.astype(BF))
                score_grads.append((powered * prob_grad[:, at]).astype(BF))
            weights = jnp.concatenate(weights, axis=1)
            score_grads = jnp.concatenate(score_grads, axis=1)
            value_grad = dot(weights, grad_low[start:], NN)
            key_grad = dot(score_grads, rolled_low[head][start:], NN) * 0.125
            query_grad = dot(score_grads, rolled_low[0 if head == 0 else 2][cols], TN)
            if col_block == 0:
                query_sum[head] = query_grad
            else:
                query_sum[head, start:] = query_sum[head, start:] + query_grad
            results.append((key_grad, value_grad))
        (key0, value0), (key1, value1) = results
        out_ref[cols, 0:128] = key0.astype(BF)
        out_ref[cols, 128:256] = value0.astype(BF)
        out_ref[cols, 256:384] = jnp.where(low_block, key1, value1).astype(BF)
    out_ref[:, 0:128] = jnp.where(low, query_sum[0] * 0.125, out_ref[:, 0:128].astype(F32)).astype(BF)
    out_ref[:, 128:256] = jnp.where(low, out_ref[:, 128:256].astype(F32), query_sum[1] * 0.125).astype(BF)
    half = length // 2
    chip = me_ref[0] >> 1
    final_ref[0:half, :] = out_ref[pl.ds(pl.multiple_of(chip * half, half), half), :]
    final_ref[half:, :] = out_ref[pl.ds(pl.multiple_of((1 - chip) * half, half), half), :]


def attend_backward(near, far, totals, context, grads, prefix, slopes, me, pair, size=256):
    length = 2 * near.shape[0]
    count = len(special_blocks(length, size))
    rows = grads[0].shape[0]
    return pl.pallas_call(
        partial(attend_backward_kernel, size),
        grid_spec=pltpu.PrefetchScalarGridSpec(
            num_scalar_prefetch=3,
            grid=(1,),
            in_specs=[pl.BlockSpec((length // 2, 384), lambda p, *_: (0, pair))] * 2
            + [pl.BlockSpec((length, 128), lambda p, *_: (0, pair))] * 2
            + [pl.BlockSpec((rows, 128), lambda p, *_: (0, pair))] * 4,
            out_specs=pl.BlockSpec((length, 384), lambda p, *_: (0, 0)),
            scratch_shapes=[
                pltpu.VMEM((count, size, size), F32),
                pltpu.VMEM((2, length, 128), F32),
                pltpu.VMEM((length, 128), BF),
                pltpu.VMEM((length, 384), BF),
                pltpu.VMEM((length, 384), BF),
            ],
        ),
        out_shape=jax.ShapeDtypeStruct((length, 384), BF),
        compiler_params=pltpu.CompilerParams(vmem_limit_bytes=48 * 1024 * 1024),
        cost_estimate=pl.CostEstimate(flops=2 * 5 * 2 * length * length * 256, bytes_accessed=3 * 1024 * 1024, transcendentals=0),
        name="attend_backward",
    )(prefix, slopes[2 * pair : 2 * pair + 2], me, near, far, totals, context, *grads)


MIB = 1024 * 1024


def whole(shape):
    return pl.BlockSpec(shape, lambda *_: (0,) * len(shape))


def once(shape):
    return pl.BlockSpec(shape, lambda *_: (0,) * len(shape), pipeline_mode=pl.Buffered(1))


def project_kernel(me_ref, own_ref, near_ref, weight_ref, bias_ref, gain_ref, shift_ref, normed_ref, joined_ref):
    block = jnp.where(pl.program_id(0) == 0, own_ref[...].astype(F32), near_ref[...].astype(F32))
    normed = (norm_parts(block)[0] * gain_ref[...] + shift_ref[...]).astype(BF)
    normed_ref[...] = normed
    joined_ref[...] = (dot(normed, weight_ref[...], NN) + bias_ref[...]).astype(BF)


def project(me, blocks, weight, bias, gain, shift):
    rows, features = blocks[0].shape
    columns = weight.shape[1]
    return pl.pallas_call(
        project_kernel,
        grid_spec=pltpu.PrefetchScalarGridSpec(
            num_scalar_prefetch=1,
            grid=(2,),
            in_specs=[once((rows, features))] * 2
            + [once((features, columns)), once((1, columns)), once((1, features)), once((1, features))],
            out_specs=[
                pl.BlockSpec((rows, features), lambda g, me: ((me[0] & 1) ^ g, 0)),
                pl.BlockSpec((rows, columns), lambda g, me: ((me[0] & 1) ^ g, 0)),
            ],
        ),
        out_shape=[
            jax.ShapeDtypeStruct((2 * rows, features), BF),
            jax.ShapeDtypeStruct((2 * rows, columns), BF),
        ],
        compiler_params=pltpu.CompilerParams(vmem_limit_bytes=32 * 1024 * 1024),
        cost_estimate=pl.CostEstimate(flops=2 * 2 * rows * features * columns, bytes_accessed=6 * MIB, transcendentals=0),
        name="project",
    )(me, *blocks, weight, bias, gain, shift)


def middle_kernel(me_ref, *refs):
    (c0, c1, c2, c3, w0, w1, w2, w3, hidden_ref, grad_ref, fc1_ref, fc2_ref, fc1_bias_ref,
     dense_bias_ref, gain_ref, shift_ref) = refs[:16]
    (normed_ref, act_ref, pre_ref, middle_ref, bias_sum_ref, squares_ref,
     part3_ref, part2_ref, part1_ref, part0_ref) = refs[16:]
    step = pl.program_id(0)
    grad = grad_ref[...]
    attn = dense_bias_ref[...]
    for context_ref, weight in ((c0, w0), (c1, w1), (c2, w2), (c3, w3)):
        attn = attn + dot(context_ref[...], weight[...], NN)
    middle = hidden_ref[...].astype(F32) + attn
    normed = (norm_parts(middle)[0] * gain_ref[...] + shift_ref[...]).astype(BF)
    normed_ref[...] = normed
    middle_ref[...] = middle
    squares_ref[...] = jnp.sum(attn * attn, axis=0, keepdims=True)
    pre = dot(normed, fc1_ref[...], NN) + fc1_bias_ref[...]
    act_grad = dot(grad, fc2_ref[...], NT)
    cubic = 0.7978845608028654
    square = pre * pre
    inner = jnp.tanh(pre * (cubic + cubic * 0.044715 * square))
    half = 0.5 + 0.5 * inner
    act = pre * half
    act_ref[...] = act.astype(BF)
    slope = half + act * (1.0 - inner) * (cubic + cubic * 3 * 0.044715 * square)
    pre_grad = (act_grad * slope).astype(BF)
    pre_ref[...] = pre_grad
    sums = jnp.sum(pre_grad.astype(F32), axis=0, keepdims=True)
    part = dot(pre_grad, fc1_ref[...], NT)

    @pl.when(step == 0)
    def _():
        bias_sum_ref[...] = sums

    @pl.when(step != 0)
    def _():
        bias_sum_ref[...] += sums

    for at, ref in enumerate((part3_ref, part2_ref, part1_ref, part0_ref)):
        @pl.when(step == at)
        def _():
            ref[...] = part.astype(ref.dtype)


def middle_part(me, contexts, weights, hidden, grad, fc1, fc2, fc1_bias, dense_bias, gain, shift):
    rows = hidden.shape[0] // 4
    features, hidden_units = fc1.shape
    flip = lambda g, me: (3 - g, 0)
    placed = lambda g, me: (me[0] ^ (3 - g), 0)
    columns = contexts[0].shape[1]
    return pl.pallas_call(
        middle_kernel,
        grid_spec=pltpu.PrefetchScalarGridSpec(
            num_scalar_prefetch=1,
            grid=(4,),
            in_specs=[pl.BlockSpec((rows, columns), placed)] * 4
            + [once(w.shape) for w in weights]
            + [pl.BlockSpec((rows, features), flip)] * 2
            + [once(fc1.shape), once(fc2.shape), once((1, hidden_units))] + [once((1, features))] * 3,
            out_specs=[
                pl.BlockSpec((rows, features), flip),
                pl.BlockSpec((rows, hidden_units), flip),
                pl.BlockSpec((rows, hidden_units), flip),
                whole((rows, features)),
                whole((1, hidden_units)),
                whole((1, features)),
            ]
            + [whole((rows, features))] * 4,
        ),
        out_shape=[
            jax.ShapeDtypeStruct((4 * rows, features), BF),
            jax.ShapeDtypeStruct((4 * rows, hidden_units), BF),
            jax.ShapeDtypeStruct((4 * rows, hidden_units), BF),
            jax.ShapeDtypeStruct((rows, features), F32),
            jax.ShapeDtypeStruct((1, hidden_units), F32),
            jax.ShapeDtypeStruct((1, features), F32),
        ]
        + [jax.ShapeDtypeStruct((rows, features), kind) for kind in (BF, F32, BF, F32)],
        compiler_params=pltpu.CompilerParams(vmem_limit_bytes=48 * 1024 * 1024),
        cost_estimate=pl.CostEstimate(flops=2 * 4 * rows * features * (features + 3 * hidden_units), bytes_accessed=14 * MIB, transcendentals=0),
        name="middle_part",
    )(me, *contexts, *weights, hidden, grad, fc1, fc2, fc1_bias, dense_bias, gain, shift)


def turn_kernel(part_ref, near_ref, far_ref, middle_ref, out_grad_ref, gain_ref, w0, w1, w2, w3,
                grad_ref, low_ref, g0, g1, g2, g3, sums_ref):
    upstream = part_ref[...] + near_ref[...].astype(F32) + far_ref[...].astype(F32)
    unit, rstd = norm_parts(middle_ref[...])
    scaled = upstream * gain_ref[...]
    grad = rstd * (
        scaled
        - jnp.mean(scaled, axis=-1, keepdims=True)
        - unit * jnp.mean(scaled * unit, axis=-1, keepdims=True)
    )
    out_grad = out_grad_ref[...].astype(F32)
    grad = grad + out_grad
    low = grad.astype(BF)
    grad_ref[...] = grad
    low_ref[...] = low
    for weight, ref in ((w0, g0), (w1, g1), (w2, g2), (w3, g3)):
        ref[...] = dot(low, weight[...], NT).astype(BF)
    sums_ref[0:1, :] = jnp.sum(grad, axis=0, keepdims=True)
    sums_ref[1:2, :] = jnp.sum(upstream * unit, axis=0, keepdims=True)
    sums_ref[2:3, :] = jnp.sum(upstream, axis=0, keepdims=True)
    sums_ref[3:4, :] = jnp.sum(out_grad, axis=0, keepdims=True)
    sums_ref[4:8, :] = jnp.zeros((4, grad.shape[1]), F32)


def turn(part, near, far, middle, out_grad, gain, weights):
    rows, features = middle.shape
    heads = weights[0].shape[0]
    return pl.pallas_call(
        turn_kernel,
        out_shape=[
            jax.ShapeDtypeStruct((rows, features), F32),
            jax.ShapeDtypeStruct((rows, features), BF),
        ]
        + [jax.ShapeDtypeStruct((rows, heads), BF)] * 4
        + [jax.ShapeDtypeStruct((8, features), F32)],
        compiler_params=pltpu.CompilerParams(vmem_limit_bytes=32 * 1024 * 1024),
        cost_estimate=pl.CostEstimate(flops=2 * 4 * rows * features * heads, bytes_accessed=7 * MIB, transcendentals=0),
        name="turn",
    )(part, near, far, middle, out_grad, gain, *weights)


def rows_kernel(dims, me_ref, left_ref, weight_ref, part3_ref, part2_ref, part1_ref, part0_ref):
    step = pl.program_id(0)
    part = dot(left_ref[...], weight_ref[...], dims)
    for at, ref in enumerate((part3_ref, part2_ref, part1_ref, part0_ref)):
        @pl.when(step == at)
        def _():
            ref[...] = part.astype(ref.dtype)


def rows_product(me, left, weight, dims, order):
    rows = left.shape[0] // 4
    features = weight.shape[1] if dims is NN else weight.shape[0]
    return pl.pallas_call(
        partial(rows_kernel, dims),
        grid_spec=pltpu.PrefetchScalarGridSpec(
            num_scalar_prefetch=1,
            grid=(4,),
            in_specs=[pl.BlockSpec((rows, left.shape[1]), lambda g, me: (order(3 - g, me), 0)), once(weight.shape)],
            out_specs=[whole((rows, features))] * 4,
        ),
        out_shape=[jax.ShapeDtypeStruct((rows, features), kind) for kind in (BF, F32, BF, F32)],
        compiler_params=pltpu.CompilerParams(vmem_limit_bytes=32 * 1024 * 1024),
        cost_estimate=pl.CostEstimate(flops=2 * 4 * rows * features * left.shape[1], bytes_accessed=6 * MIB, transcendentals=0),
        name="rows_product",
    )(me, left, weight)


def last_kernel(part_ref, near_ref, far_ref, hidden_ref, middle_grad_ref, gain_ref, out_ref):
    upstream = part_ref[...] + near_ref[...].astype(F32) + far_ref[...].astype(F32)
    unit, rstd = norm_parts(hidden_ref[...].astype(F32))
    scaled = upstream * gain_ref[...]
    grad = rstd * (
        scaled
        - jnp.mean(scaled, axis=-1, keepdims=True)
        - unit * jnp.mean(scaled * unit, axis=-1, keepdims=True)
    )
    out_ref[...] = (grad + middle_grad_ref[...]).astype(BF)


def last_norm(part, near, far, hidden, middle_grad, gain):
    rows, features = hidden.shape
    return pl.pallas_call(
        last_kernel,
        out_shape=jax.ShapeDtypeStruct((rows, features), BF),
        compiler_params=pltpu.CompilerParams(vmem_limit_bytes=32 * 1024 * 1024),
        cost_estimate=pl.CostEstimate(flops=2 * rows * features * 16, bytes_accessed=5 * MIB, transcendentals=0),
        name="last_norm",
    )(part, near, far, hidden, middle_grad, gain)


def last_product_kernel(me_ref, left_ref, hidden_ref, weight_ref, part3_ref, part2_ref, part1_ref, part0_ref, sums_ref, bias_ref):
    step = pl.program_id(0)
    left = left_ref[...]
    part = dot(left, weight_ref[...], NT)
    for at, ref in enumerate((part3_ref, part2_ref, part1_ref, part0_ref)):
        @pl.when(step == at)
        def _():
            ref[...] = part.astype(ref.dtype)
    unit, _ = norm_parts(hidden_ref[...].astype(F32))
    gain_sum = jnp.sum(part * unit, axis=0, keepdims=True)
    shift_sum = jnp.sum(part, axis=0, keepdims=True)
    bias_sum = jnp.sum(left.astype(F32), axis=0, keepdims=True)

    @pl.when(step == 0)
    def _():
        sums_ref[0:1, :] = gain_sum
        sums_ref[1:2, :] = shift_sum
        bias_ref[...] = bias_sum

    @pl.when(step != 0)
    def _():
        sums_ref[0:1, :] += gain_sum
        sums_ref[1:2, :] += shift_sum
        bias_ref[...] += bias_sum


def last_product(me, left, hidden, weight):
    rows, features, columns = left.shape[0] // 4, weight.shape[0], left.shape[1]
    return pl.pallas_call(
        last_product_kernel,
        grid_spec=pltpu.PrefetchScalarGridSpec(
            num_scalar_prefetch=1,
            grid=(4,),
            in_specs=[
                pl.BlockSpec((rows, columns), lambda g, me: ((me[0] & 1) ^ (3 - g), 0)),
                pl.BlockSpec((rows, features), lambda g, me: (3 - g, 0)),
                once(weight.shape),
            ],
            out_specs=[whole((rows, features))] * 4 + [whole((2, features)), whole((1, columns))],
        ),
        out_shape=[jax.ShapeDtypeStruct((rows, features), kind) for kind in (BF, F32, BF, F32)]
        + [jax.ShapeDtypeStruct((2, features), F32), jax.ShapeDtypeStruct((1, columns), F32)],
        compiler_params=pltpu.CompilerParams(vmem_limit_bytes=32 * 1024 * 1024),
        cost_estimate=pl.CostEstimate(flops=2 * 4 * rows * features * columns, bytes_accessed=6 * MIB, transcendentals=0),
        name="last_product",
    )(me, left, hidden, weight)


def finish_kernel(rows, width, parity_ref, c1_value, c1_came, c2_value, c2_came, qkv_ref, dense_ref, small_ref):
    first = pl.program_id(0) == parity_ref[0]

    def put(one, two):
        extra = one.shape[1] - width
        qkv_ref[:, 0:width] = one[:, 0:width].astype(F32)
        qkv_ref[:, width : 2 * width] = two[0:rows, 0:width].astype(F32)
        dense_ref[0:extra, :] = one[:, width:].astype(F32).T
        dense_ref[extra : 2 * extra, :] = two[0:rows, width:].astype(F32).T
        small_ref[...] = two[rows:, :].astype(F32)

    @pl.when(first)
    def _():
        put(c1_value, c2_value)

    @pl.when(jnp.logical_not(first))
    def _():
        put(c1_came, c2_came)


def finish(parity, width, c1, c2):
    half, both = c1.value.shape
    full = c2.value.shape[0]
    extra, more = both - width, full - half
    return pl.pallas_call(
        partial(finish_kernel, half, width),
        grid_spec=pltpu.PrefetchScalarGridSpec(
            num_scalar_prefetch=1,
            grid=(2,),
            in_specs=[once((half, both))] * 2 + [once((full, both))] * 2,
            out_specs=[
                pl.BlockSpec((half, 2 * width), lambda g, *_: (g, 0)),
                pl.BlockSpec((2 * extra, half), lambda g, *_: (0, g)),
                pl.BlockSpec((more, both), lambda g, *_: (g, 0)),
            ],
        ),
        out_shape=[
            jax.ShapeDtypeStruct((2 * half, 2 * width), F32),
            jax.ShapeDtypeStruct((2 * extra, 2 * half), F32),
            jax.ShapeDtypeStruct((2 * more, both), F32),
        ],
        compiler_params=pltpu.CompilerParams(vmem_limit_bytes=32 * 1024 * 1024),
        cost_estimate=pl.CostEstimate(flops=1024, bytes_accessed=6 * MIB, transcendentals=0),
        name="finish",
    )(parity, c1.value, c1.came, c2.value, c2.came)


def tensor_send(value, flip):
    return lax.ppermute(value, "tensor", [(i, i ^ flip) for i in range(4)])


def add_low(a, b):
    return (a.astype(F32) + b.astype(F32)).astype(BF)


class Ladder:
    def __init__(self, dp, array):
        self.inner, self.outer = 2, dp // 2
        index = lax.axis_index("dp")
        self.mine, self.place_of = index % 2, index // 2
        self.pairs = [(i, i ^ 1) for i in range(dp)]
        self.array, self.half = array, array.shape[0] // 2
        half = self.outer // 2
        count = self.outer
        self.steps = [("in", s) for s in range(half - 1)] + ([("mid", 0)] if count > 1 else [])
        self.steps += [("out", s) for s in reversed(range(half - 1))]
        self.stages = len(self.steps) + 2
        self.stage = 0
        self.came = self.value = None
        self.open = False

    def along(self, pairs):
        return [(a * self.inner + i, b * self.inner + i) for a, b in pairs for i in range(self.inner)]

    def part(self, which):
        return lax.dynamic_slice_in_dim(self.array, which * self.half, self.half, 0)

    def send(self, *gate):
        count, half = self.outer, self.outer // 2
        if self.stage == 0:
            self.sent, pairs = self.part(1 - self.mine), self.pairs
        elif self.stage == self.stages - 1:
            self.sent, pairs = self.value, self.pairs
        else:
            kind, step = self.steps[self.stage - 1]
            self.sent = self.value
            if kind == "in":
                pairs = [(step, step + 1), (count - 1 - step, count - 2 - step)]
            elif kind == "mid":
                pairs = [(half - 1, half), (half, half - 1)]
            else:
                pairs = [(step + 1, step), (count - 2 - step, count - 1 - step)]
            pairs = self.along(pairs)
        if gate:
            self.sent = after(self.sent, *gate)
        self.came = lax.ppermute(self.sent, "dp", pairs)
        self.open = True
        return self

    def take(self, *gate):
        count = self.outer
        if gate and self.value is not None:
            self.value = after(self.value, *gate)
        if self.stage == 0:
            own = self.part(self.mine)
            if gate:
                own = after(own, *gate)
            self.value = add_low(own, self.came)
        elif self.stage < self.stages - 1:
            kind, step = self.steps[self.stage - 1]
            if kind == "out":
                outside = (self.place_of <= step) | (self.place_of >= count - 1 - step)
                self.value = jnp.where(outside, self.came, self.value)
            else:
                self.value = add_low(self.value, self.came)
        self.stage += 1
        self.open = False
        return self

    def finish(self):
        if self.came is not None and self.open:
            self.take()
        while self.stage < self.stages:
            self.send().take()
        return self

    def rows(self):
        lower = self.mine == 0
        return [jnp.where(lower, self.value, self.came), jnp.where(lower, self.came, self.value)]


class Spread:
    def __init__(self, dp, array):
        self.lines = [[a * 2 + i for a in range(dp // 2)] for i in range(2)]
        self.pairs = [(i, i ^ 1) for i in range(dp)]
        self.mine = lax.axis_index("dp") % 2
        self.array = array
        self.blocks = array.reshape(dp // 2, 2, array.shape[0] // dp, array.shape[1])

    def send(self):
        self.came = lax.ppermute(lax.dynamic_index_in_dim(self.blocks, 1 - self.mine, 1, False), "dp", self.pairs)

    def take(self, *gate):
        self.value = add_low(after(lax.dynamic_index_in_dim(self.blocks, self.mine, 1, False), *gate), self.came)
        return self

    def trade(self):
        self.terms = lax.all_to_all(self.value, "dp", 0, 0, axis_index_groups=self.lines, tiled=True)

    def add(self, *gate):
        self.value = jnp.sum(after(self.terms, *gate).astype(F32), axis=0).astype(BF)
        return self

    def gather(self):
        self.all = lax.all_gather(self.value, "dp", axis=0, tiled=True)


def joined_rows(ladders):
    return jnp.concatenate([piece for ladder in ladders for piece in ladder.rows()], axis=0).astype(F32)


def local(
    dp,
    hidden_in,
    out_grad,
    prefix_len,
    qkv_weight,
    qv_bias,
    dense_weight,
    dense_bias,
    norm1_gain,
    norm1_shift,
    norm2_gain,
    norm2_shift,
    fc1_weight,
    fc1_bias,
    fc2_weight,
    fc2_bias,
):
    rows_here, features = hidden_in.shape
    heads_here, _, head_size = qv_bias.shape
    tensor_index = lax.axis_index("tensor")
    me = tensor_index.reshape(1)
    slopes = 2.0 ** (-8.0 * (tensor_index * heads_here + 1 + lax.iota(jnp.int32, heads_here)).astype(F32) / HEADS)
    bias_full = jnp.stack(
        [qv_bias[:, 0], jnp.zeros_like(qv_bias[:, 0]), qv_bias[:, 1]], axis=1
    ).reshape(1, -1)
    row = lambda v: v.reshape(1, -1)

    norm1 = (qkv_weight, bias_full, row(norm1_gain), row(norm1_shift))
    hidden_x = tensor_send(hidden_in, 2)
    hidden_c = tensor_send(hidden_in, 1)
    dense_c = tensor_send(dense_weight, 1)
    normed_near, joined_near = project(me, (hidden_in, hidden_c), *norm1)
    share = dense_weight.shape[0] // 2
    parity = lax.axis_index("dp") % 2
    dense_share = lax.dynamic_slice_in_dim(dense_weight, parity * share, share, 0)
    hidden_xc = tensor_send(after(hidden_x, joined_near), 1)
    dense_half = tensor_send(after(dense_share, hidden_x, joined_near), 2)
    grad_x = tensor_send(after(out_grad, hidden_x, joined_near), 2)
    normed_far, joined_far = project(me, (hidden_x, hidden_xc), *norm1)
    grad_c = tensor_send(after(out_grad, hidden_c), 1)
    context, totals = attend_forward(joined_near, joined_far, prefix_len, slopes, me)
    context_x = tensor_send(context, 2)
    context_c = tensor_send(context, 1)
    dense_other = lax.ppermute(after(dense_half, context), "dp", [(i, i ^ 1) for i in range(dp)])
    dense_x = jnp.where(
        parity == 0,
        jnp.concatenate([dense_half, dense_other], axis=0),
        jnp.concatenate([dense_other, dense_half], axis=0),
    )
    dense_xc = tensor_send(dense_x, 1)
    dense_blocks = [dense_weight, dense_c, dense_x, dense_xc]
    grad_xc = tensor_send(after(grad_x, context), 1)
    grad_all = jnp.concatenate([out_grad, grad_c, grad_x, grad_xc], axis=0)
    hidden_all = jnp.concatenate([hidden_in, hidden_c, hidden_x, after(hidden_xc, context)], axis=0)
    context_xc = tensor_send(after(context_x, grad_all, hidden_all), 1)

    (normed2_all, activated, pre_grad, middle, fc1_bias_sum, attn_squares, part3, part2, part1, part0) = middle_part(
        me, (context, context_c, context_x, context_xc), dense_blocks, hidden_all, grad_all,
        fc1_weight, fc2_weight, row(fc1_bias), row(dense_bias), row(norm2_gain), row(norm2_shift),
    )

    over = tensor_send(part3, 1)
    near = tensor_send(part1, 1)
    half = features // 2
    fc1_term = dot(normed2_all, pre_grad, TN).astype(BF)
    b1, b2 = Ladder(dp, fc1_term[:half]), Ladder(dp, fc1_term[half:])
    b1.send()
    chip = (after(part2, b1.sent) + over.astype(F32)).astype(BF)
    far = tensor_send(chip, 2)
    fc2_term = dot(after(activated, chip), grad_all, TN).astype(BF)
    a1, a2 = Ladder(dp, fc2_term[:half]), Ladder(dp, fc2_term[half:])
    b2.send(fc2_term)
    mlp3, mlp2, mlp1, mlp0 = rows_product(me, after(activated, b2.sent), fc2_weight, NN, lambda g, me: g)
    b1.take(mlp0).send()
    middle_grad, middle_low, *context_grads, turn_sums = turn(
        after(part0, b1.value), near, far, middle, out_grad, row(norm2_gain), dense_blocks
    )
    arrived = [context_grads[0]] + [tensor_send(context_grads[flip], flip) for flip in (2, 3, 1)]
    arrived = [arrived[0], arrived[3], arrived[1], arrived[2]]
    mlp_over = tensor_send(after(mlp3, arrived[1]), 1)
    mlp_near = tensor_send(after(mlp1, arrived[1]), 1)
    b1.take(arrived[1]).send()
    b2.take(b1.value).send()
    middle_x = tensor_send(after(middle_low, arrived[2]), 2)
    a1.send(b2.value)
    mlp_chip = (after(mlp2, a1.sent) + mlp_over.astype(F32)).astype(BF)
    joined_grad0 = attend_backward(
        after(joined_near, a1.sent, mlp_chip), joined_far, totals, context, arrived, prefix_len, slopes, me, 0
    )
    b1.take(joined_grad0).send()
    b2.take(b1.value).send()
    a1.take(b2.value).send()
    middle_c = tensor_send(after(middle_low, a1.value), 1)
    middle_xc = tensor_send(after(middle_x, a1.value), 1)
    a2.send(middle_xc)
    mlp_far = tensor_send(after(mlp_chip, middle_xc), 2)
    normed1_all = jnp.concatenate([after(normed_near, a2.sent), normed_far], axis=0)
    joined_grad1 = attend_backward(
        after(joined_near, a2.sent), joined_far, totals, context, arrived, prefix_len, slopes, me, 1
    )
    width, extra = joined_grad1.shape[1], context.shape[1] // 2
    wide = width + extra
    qkv_term = dot(normed1_all, joined_grad1, TN).astype(BF)
    middle_all = jnp.concatenate([after(middle_low, qkv_term), middle_c, middle_x, middle_xc], axis=0)
    context_flip = jnp.concatenate(
        [
            lax.dynamic_slice_in_dim(after(context, qkv_term), (tensor_index ^ flip) * rows_here, rows_here, 0)
            for flip in range(4)
        ],
        axis=0,
    )
    dense_term = dot(middle_all, context_flip, TN).astype(BF)
    joined_grad = jnp.concatenate([joined_grad0, after(joined_grad1, dense_term)], axis=1)
    last3, last2, last1, last0, last_sums, joined_sums = last_product(me, joined_grad, hidden_all, qkv_weight)
    b1.take(last0).send()
    b2.take(b1.value).send()
    a1.take(b2.value).send()
    a2.take(a1.value).send()
    qkv_first = dot(after(normed1_all, dense_term), joined_grad0, TN).astype(BF)
    c1 = Ladder(dp, jnp.concatenate([qkv_first, after(dense_term, a2.value)[:, :extra]], axis=1))
    c1.send()
    mlp_out = after(mlp0, c1.sent) + mlp_near.astype(F32) + mlp_far.astype(F32) + fc2_bias
    final = middle + mlp_out
    residual = hidden_in.astype(F32)
    column_squares = lambda v: jnp.sum(v * v, axis=0, keepdims=True)
    joined_sums = joined_sums.reshape(heads_here, 3, head_size)
    qv_sums = jnp.stack([joined_sums[:, 0], joined_sums[:, 2]], axis=1).reshape(1, -1)
    small = jnp.concatenate(
        [column_squares(residual), attn_squares, column_squares(mlp_out), column_squares(final), turn_sums[:4], last_sums],
        axis=0,
    )
    small = small + tensor_send(small, 1)
    small = small + tensor_send(small, 2)
    small = jnp.concatenate(
        [fc1_bias_sum, jnp.pad(qv_sums, ((0, 0), (0, features - qv_sums.shape[1]))), small], axis=0
    )
    small = jnp.pad(small, ((0, 16 - small.shape[0]), (0, 2 * wide - features))).astype(BF)
    c2_term = jnp.concatenate([qkv_term, dense_term[:, extra:]], axis=1)
    b1.take(small)
    c2 = Ladder(dp, jnp.concatenate([c2_term[:half], small[:, :wide], c2_term[half:], small[:, wide:]], axis=0))
    c2.send(b1.came)
    b2.take(c2.sent).send()
    a1.take(b2.value).send()
    a2.take(a1.value).send()
    c1.take(a2.value).send()
    b2.take(c1.value)
    last_over = tensor_send(after(last3, b2.came), 1)
    last_near = tensor_send(after(last1, b2.came), 1)
    a1.take(b2.came).send()
    a2.take(a1.value).send()
    c1.take(a2.value).send()
    c2.take(c1.value).send()
    last_chip = (after(last2, c2.value) + last_over.astype(F32)).astype(BF)
    last_far = tensor_send(last_chip, 2)
    fc1_sum = after(joined_rows([b1, b2]), last_chip)
    a1.take(fc1_sum)
    a2.take(a1.came).send()
    c1.take(a2.value).send()
    c2.take(c1.value).send()
    hidden_grad = last_norm(after(last0, c2.value), last_near, last_far, hidden_in, middle_grad, row(norm1_gain))
    a2.take(hidden_grad)
    c1.take(a2.came).send()
    c2.take(c1.value).send()
    fc2_sum = after(joined_rows([a1, a2]), c2.value)
    c1.take(fc2_sum)
    c2.take(c1.came).send()
    c2.finish()
    qkv_sum, dense_sum, small_sum = finish(parity.reshape(1), width, c1, c2)
    by_dp = jnp.concatenate([small_sum[:16], small_sum[16:]], axis=1)[:, :features]
    by_all = by_dp[5:]
    qv_bias_grad = by_dp[1, : qv_sums.shape[1]].reshape(heads_here, 2, head_size)
    entry_count = rows_here * features * dp * 4
    sublayer_rms = jnp.sqrt(jnp.sum(by_dp[2:6], axis=1) / float(entry_count))
    return (
        final.astype(BF),
        hidden_grad,
        qkv_sum,
        qv_bias_grad,
        dense_sum,
        by_all[1],
        by_all[5],
        by_all[6],
        by_all[2],
        by_all[3],
        fc1_sum.astype(F32),
        by_dp[0],
        fc2_sum.astype(F32),
        by_all[4],
        sublayer_rms,
    )


def solution(mesh):
    return jax.shard_map(
        partial(local, mesh.shape["dp"]),
        mesh=mesh,
        in_specs=(
            P(("dp", "tensor"), None),
            P(("dp", "tensor"), None),
            P("dp"),
            P(None, "tensor"),
            P("tensor", None, None),
            P("tensor", None),
            P(),
            P(),
            P(),
            P(),
            P(),
            P(None, "tensor"),
            P("tensor"),
            P("tensor", None),
            P(),
        ),
        out_specs=(
            P(("dp", "tensor"), None),
            P(("dp", "tensor"), None),
            P(None, "tensor"),
            P("tensor", None, None),
            P("tensor", None),
            P(),
            P(),
            P(),
            P(),
            P(),
            P(None, "tensor"),
            P("tensor"),
            P("tensor", None),
            P(),
            P(),
        ),
        check_vma=False,
    )
```

```python
from functools import partial

import jax
import jax.numpy as jnp
from jax import lax
from jax.experimental import pallas as pl
from jax.experimental.pallas import tpu as pltpu
from jax.sharding import PartitionSpec as P

HEADS = 16
PREFIX_MOST = 512

epsilon = 1e-05
BF = jnp.bfloat16
F32 = jnp.float32
NT = (((1,), (1,)), ((), ()))
NN = (((1,), (0,)), ((), ()))
TN = (((0,), (0,)), ((), ()))


def dot(a, b, dims):
    return lax.dot_general(a, b, dims, preferred_element_type=F32)


def after(value, *others):
    return lax.optimization_barrier((value,) + others)[0]


def norm_parts(values):
    center = jnp.mean(values, axis=-1, keepdims=True)
    deviation = values - center
    variance = jnp.mean(deviation * deviation, axis=-1, keepdims=True)
    rstd = lax.rsqrt(variance + epsilon)
    return deviation * rstd, rstd


def norm_backward(values, gain, upstream):
    unit, rstd = norm_parts(values)
    scaled = upstream * gain
    grad = rstd * (
        scaled
        - jnp.mean(scaled, axis=-1, keepdims=True)
        - unit * jnp.mean(scaled * unit, axis=-1, keepdims=True)
    )
    return grad, jnp.sum(upstream * unit, axis=0), jnp.sum(upstream, axis=0)


def split3(value):
    high = value.astype(BF).astype(F32)
    rest = value - high
    mid = rest.astype(BF).astype(F32)
    return high, mid, rest - mid


def place(lane, base, items):
    out = jnp.zeros(lane.shape, F32)
    for i, item in enumerate(items):
        out = jnp.where(lane == base + i, item, out)
    return out


def causal_end(row_block, size, length):
    return min(max((row_block + 1) * size, min(PREFIX_MOST, length)), length)


def fill_masks(masks, prefix, size, blocks, transposed):
    shape = (size, size)
    for index, (row_block, col_block) in enumerate(blocks):
        rows = row_block * size + lax.broadcasted_iota(jnp.int32, shape, 1 if transposed else 0)
        cols = col_block * size + lax.broadcasted_iota(jnp.int32, shape, 0 if transposed else 1)
        allowed = (cols <= rows) | ((cols < prefix) & (rows < prefix))
        beyond = jnp.maximum(cols - rows, 0).astype(F32)
        masks[index] = jnp.where(allowed, -2.0 * beyond, -1e30)


def special_blocks(length, size):
    out = []
    for row_block in range(length // size):
        for col_block in range(causal_end(row_block, size, length) // size):
            if col_block >= row_block:
                out.append((row_block, col_block))
    return out


def load_order(me_ref, near_ref, far_ref, joined_ref):
    half = near_ref.shape[0]
    chip = me_ref[0] >> 1
    joined_ref[pl.ds(pl.multiple_of(chip * half, half), half), :] = near_ref[...]
    joined_ref[pl.ds(pl.multiple_of((1 - chip) * half, half), half), :] = far_ref[...]


def attend_forward_kernel(size, prefix_ref, slope_ref, me_ref, near_ref, far_ref, context_ref, total_ref, masks, joined_ref):
    length = joined_ref.shape[0]
    pair = pl.program_id(0)
    load_order(me_ref, near_ref, far_ref, joined_ref)
    blocks = special_blocks(length, size)

    @pl.when(pair == 0)
    def _():
        fill_masks(masks, prefix_ref[0], size, blocks, False)

    lane = lax.broadcasted_iota(jnp.int32, (length, 128), 1)
    low = lane < 64
    position = lax.broadcasted_iota(jnp.int32, (length, 1), 0).astype(F32)
    tiles = [joined_ref[:, i * 128 : (i + 1) * 128].astype(F32) for i in range(3)]
    rolled0 = pltpu.roll(tiles[0], 64, 1)
    rolled1 = pltpu.roll(tiles[1], 64, 1)
    sides = []
    for head in range(2):
        slope = slope_ref[pair * 2 + head]
        own = jnp.logical_not(low) if head == 0 else low
        base = 0 if head == 0 else 64
        query = jnp.where(own, (rolled0 if head == 0 else rolled1) * 0.125, place(lane, base, (1.0, 1.0, 1.0)))
        keys = jnp.where(own, tiles[0] if head == 0 else tiles[2], place(lane, base, split3(slope * position)))
        value = jnp.where(low, tiles[1], 1.0) if head == 0 else jnp.where(low, 1.0, tiles[2])
        sides.append((slope, query.astype(BF), keys.astype(BF), value.astype(BF)))
    low_block = low[:size]
    lane_block = lane[:size]
    for row_block in range(length // size):
        end = causal_end(row_block, size, length)
        rows = slice(row_block * size, (row_block + 1) * size)
        results = []
        for head in range(2):
            slope, query, keys, value = sides[head]
            scores = dot(query[rows], keys[:end], NT)
            columns = []
            for col_block in range(end // size):
                piece = scores[:, col_block * size : (col_block + 1) * size]
                if col_block >= row_block:
                    piece = piece + slope * masks[blocks.index((row_block, col_block))]
                columns.append(piece)
            highest = columns[0]
            for piece in columns[1:]:
                highest = jnp.maximum(highest, piece)
            highest = jnp.max(highest, axis=-1, keepdims=True)
            powered = jnp.concatenate([jnp.exp(piece - highest).astype(BF) for piece in columns], axis=1)
            gathered = dot(powered, value[:end], NN)
            total = gathered[:, 64:65] if head == 0 else gathered[:, 0:1]
            results.append((gathered / total, highest + jnp.log(total)))
        context_ref[rows, :] = jnp.where(low_block, results[0][0], results[1][0]).astype(BF)
        total_ref[rows, :] = jnp.where(lane_block == 0, results[0][1], results[1][1])


def attend_forward(near, far, prefix, slopes, me, size=256):
    length, columns = 2 * near.shape[0], near.shape[1]
    pairs = columns // 384
    count = len(special_blocks(length, size))
    tile = pl.BlockSpec((length, 128), lambda p, *_: (0, p))
    return pl.pallas_call(
        partial(attend_forward_kernel, size),
        grid_spec=pltpu.PrefetchScalarGridSpec(
            num_scalar_prefetch=3,
            grid=(pairs,),
            in_specs=[pl.BlockSpec((length // 2, 384), lambda p, *_: (0, p))] * 2,
            out_specs=[tile, tile],
            scratch_shapes=[pltpu.VMEM((count, size, size), F32), pltpu.VMEM((length, 384), BF)],
        ),
        out_shape=[
            jax.ShapeDtypeStruct((length, pairs * 128), BF),
            jax.ShapeDtypeStruct((length, pairs * 128), F32),
        ],
        compiler_params=pltpu.CompilerParams(vmem_limit_bytes=40 * 1024 * 1024),
        cost_estimate=pl.CostEstimate(flops=4 * 2 * 2 * length * length * 128, bytes_accessed=4 * 1024 * 1024, transcendentals=0),
        name="attend_forward",
    )(prefix, slopes, me, near, far)


def attend_backward_kernel(
    size, prefix_ref, slope_ref, me_ref, near_ref, far_ref, total_ref, context_ref, g0, g1, g2, g3,
    final_ref, masks, query_sum, grad_ref, joined_ref, out_ref,
):
    length = joined_ref.shape[0]
    pair = pl.program_id(0)
    load_order(me_ref, near_ref, far_ref, joined_ref)
    rows = g0.shape[0]
    for flip, ref in enumerate((g0, g1, g2, g3)):
        grad_ref[pl.ds(pl.multiple_of((me_ref[0] ^ flip) * rows, rows), rows), :] = ref[...]
    totals = total_ref[...]
    blocks = special_blocks(length, size)

    @pl.when(pair == 0)
    def _():
        fill_masks(masks, prefix_ref[0], size, blocks, True)

    lane = lax.broadcasted_iota(jnp.int32, (length, 128), 1)
    low = lane < 64
    position = lax.broadcasted_iota(jnp.int32, (length, 1), 0).astype(F32)
    tiles = [joined_ref[:, i * 128 : (i + 1) * 128].astype(F32) for i in range(3)]
    rolled = [pltpu.roll(tile, 64, 1) for tile in tiles]
    grad = grad_ref[...].astype(F32)
    product = grad * context_ref[...].astype(F32)
    grad_low = grad.astype(BF)
    rolled_low = [tile.astype(BF) for tile in rolled]
    sides = []
    for head in range(2):
        slope = slope_ref[pair * 2 + head]
        own = jnp.logical_not(low) if head == 0 else low
        base = 0 if head == 0 else 64
        log_total = totals[:, head : head + 1]
        query = jnp.where(
            own, rolled[head] * 0.125, place(lane, base, (1.0, 1.0, 1.0) + split3(log_total))
        )
        keys = jnp.where(
            own, tiles[0] if head == 0 else tiles[2], place(lane, base, split3(slope * position) + (-1.0, -1.0, -1.0))
        )
        head_lanes = low if head == 0 else jnp.logical_not(low)
        inner = jnp.sum(jnp.where(head_lanes, product, 0.0), axis=1, keepdims=True)
        base = 64 - base
        value = jnp.where(head_lanes, tiles[1] if head == 0 else tiles[2], place(lane, 64 if head == 0 else 0, (-1.0, -1.0, -1.0)))
        upstream = jnp.where(head_lanes, grad, place(lane, 64 if head == 0 else 0, split3(inner)))
        sides.append((slope, query.astype(BF), keys.astype(BF), value.astype(BF), upstream.astype(BF)))
    low_block = low[:size]
    for col_block in range(length // size):
        first = col_block if col_block * size >= PREFIX_MOST else 0
        cols = slice(col_block * size, (col_block + 1) * size)
        start = first * size
        results = []
        for head in range(2):
            slope, query, keys, value, upstream = sides[head]
            scores = dot(keys[cols], query[start:], NT)
            prob_grad = dot(value[cols], upstream[start:], NT)
            weights, score_grads = [], []
            for row_block in range(first, length // size):
                at = slice((row_block - first) * size, (row_block - first + 1) * size)
                piece = scores[:, at]
                if col_block >= row_block:
                    piece = piece + slope * masks[blocks.index((row_block, col_block))]
                powered = jnp.exp(piece)
                weights.append(powered.astype(BF))
                score_grads.append((powered * prob_grad[:, at]).astype(BF))
            weights = jnp.concatenate(weights, axis=1)
            score_grads = jnp.concatenate(score_grads, axis=1)
            value_grad = dot(weights, grad_low[start:], NN)
            key_grad = dot(score_grads, rolled_low[head][start:], NN) * 0.125
            query_grad = dot(score_grads, rolled_low[0 if head == 0 else 2][cols], TN)
            if col_block == 0:
                query_sum[head] = query_grad
            else:
                query_sum[head, start:] = query_sum[head, start:] + query_grad
            results.append((key_grad, value_grad))
        (key0, value0), (key1, value1) = results
        out_ref[cols, 0:128] = key0.astype(BF)
        out_ref[cols, 128:256] = value0.astype(BF)
        out_ref[cols, 256:384] = jnp.where(low_block, key1, value1).astype(BF)
    out_ref[:, 0:128] = jnp.where(low, query_sum[0] * 0.125, out_ref[:, 0:128].astype(F32)).astype(BF)
    out_ref[:, 128:256] = jnp.where(low, out_ref[:, 128:256].astype(F32), query_sum[1] * 0.125).astype(BF)
    half = length // 2
    chip = me_ref[0] >> 1
    final_ref[0:half, :] = out_ref[pl.ds(pl.multiple_of(chip * half, half), half), :]
    final_ref[half:, :] = out_ref[pl.ds(pl.multiple_of((1 - chip) * half, half), half), :]


def attend_backward(near, far, totals, context, grads, prefix, slopes, me, pair, size=256):
    length = 2 * near.shape[0]
    count = len(special_blocks(length, size))
    rows = grads[0].shape[0]
    return pl.pallas_call(
        partial(attend_backward_kernel, size),
        grid_spec=pltpu.PrefetchScalarGridSpec(
            num_scalar_prefetch=3,
            grid=(1,),
            in_specs=[pl.BlockSpec((length // 2, 384), lambda p, *_: (0, pair))] * 2
            + [pl.BlockSpec((length, 128), lambda p, *_: (0, pair))] * 2
            + [pl.BlockSpec((rows, 128), lambda p, *_: (0, pair))] * 4,
            out_specs=pl.BlockSpec((length, 384), lambda p, *_: (0, 0)),
            scratch_shapes=[
                pltpu.VMEM((count, size, size), F32),
                pltpu.VMEM((2, length, 128), F32),
                pltpu.VMEM((length, 128), BF),
                pltpu.VMEM((length, 384), BF),
                pltpu.VMEM((length, 384), BF),
            ],
        ),
        out_shape=jax.ShapeDtypeStruct((length, 384), BF),
        compiler_params=pltpu.CompilerParams(vmem_limit_bytes=48 * 1024 * 1024),
        cost_estimate=pl.CostEstimate(flops=2 * 5 * 2 * length * length * 256, bytes_accessed=3 * 1024 * 1024, transcendentals=0),
        name="attend_backward",
    )(prefix, slopes[2 * pair : 2 * pair + 2], me, near, far, totals, context, *grads)


MIB = 1024 * 1024


def whole(shape):
    return pl.BlockSpec(shape, lambda *_: (0,) * len(shape))


def once(shape):
    return pl.BlockSpec(shape, lambda *_: (0,) * len(shape), pipeline_mode=pl.Buffered(1))


def project_kernel(me_ref, own_ref, near_ref, weight_ref, bias_ref, gain_ref, shift_ref, normed_ref, joined_ref):
    block = jnp.where(pl.program_id(0) == 0, own_ref[...].astype(F32), near_ref[...].astype(F32))
    normed = (norm_parts(block)[0] * gain_ref[...] + shift_ref[...]).astype(BF)
    normed_ref[...] = normed
    joined_ref[...] = (dot(normed, weight_ref[...], NN) + bias_ref[...]).astype(BF)


def project(me, blocks, weight, bias, gain, shift):
    rows, features = blocks[0].shape
    columns = weight.shape[1]
    return pl.pallas_call(
        project_kernel,
        grid_spec=pltpu.PrefetchScalarGridSpec(
            num_scalar_prefetch=1,
            grid=(2,),
            in_specs=[once((rows, features))] * 2
            + [once((features, columns)), once((1, columns)), once((1, features)), once((1, features))],
            out_specs=[
                pl.BlockSpec((rows, features), lambda g, me: ((me[0] & 1) ^ g, 0)),
                pl.BlockSpec((rows, columns), lambda g, me: ((me[0] & 1) ^ g, 0)),
            ],
        ),
        out_shape=[
            jax.ShapeDtypeStruct((2 * rows, features), BF),
            jax.ShapeDtypeStruct((2 * rows, columns), BF),
        ],
        compiler_params=pltpu.CompilerParams(vmem_limit_bytes=32 * 1024 * 1024),
        cost_estimate=pl.CostEstimate(flops=2 * 2 * rows * features * columns, bytes_accessed=6 * MIB, transcendentals=0),
        name="project",
    )(me, *blocks, weight, bias, gain, shift)


def middle_kernel(me_ref, *refs):
    (c0, c1, c2, c3, w0, w1, w2, w3, hidden_ref, grad_ref, fc1_ref, fc2_ref, fc1_bias_ref,
     dense_bias_ref, gain_ref, shift_ref) = refs[:16]
    (normed_ref, act_ref, pre_ref, middle_ref, bias_sum_ref, squares_ref,
     part3_ref, part2_ref, part1_ref, part0_ref) = refs[16:]
    step = pl.program_id(0)
    grad = grad_ref[...]
    attn = dense_bias_ref[...]
    for context_ref, weight in ((c0, w0), (c1, w1), (c2, w2), (c3, w3)):
        attn = attn + dot(context_ref[...], weight[...], NN)
    middle = hidden_ref[...].astype(F32) + attn
    normed = (norm_parts(middle)[0] * gain_ref[...] + shift_ref[...]).astype(BF)
    normed_ref[...] = normed
    middle_ref[...] = middle
    squares_ref[...] = jnp.sum(attn * attn, axis=0, keepdims=True)
    pre = dot(normed, fc1_ref[...], NN) + fc1_bias_ref[...]
    act_grad = dot(grad, fc2_ref[...], NT)
    cubic = 0.7978845608028654
    square = pre * pre
    inner = jnp.tanh(pre * (cubic + cubic * 0.044715 * square))
    half = 0.5 + 0.5 * inner
    act = pre * half
    act_ref[...] = act.astype(BF)
    slope = half + act * (1.0 - inner) * (cubic + cubic * 3 * 0.044715 * square)
    pre_grad = (act_grad * slope).astype(BF)
    pre_ref[...] = pre_grad
    sums = jnp.sum(pre_grad.astype(F32), axis=0, keepdims=True)
    part = dot(pre_grad, fc1_ref[...], NT)

    @pl.when(step == 0)
    def _():
        bias_sum_ref[...] = sums

    @pl.when(step != 0)
    def _():
        bias_sum_ref[...] += sums

    for at, ref in enumerate((part3_ref, part2_ref, part1_ref, part0_ref)):
        @pl.when(step == at)
        def _():
            ref[...] = part.astype(ref.dtype)


def middle_part(me, contexts, weights, hidden, grad, fc1, fc2, fc1_bias, dense_bias, gain, shift):
    rows = hidden.shape[0] // 4
    features, hidden_units = fc1.shape
    flip = lambda g, me: (3 - g, 0)
    placed = lambda g, me: (me[0] ^ (3 - g), 0)
    columns = contexts[0].shape[1]
    return pl.pallas_call(
        middle_kernel,
        grid_spec=pltpu.PrefetchScalarGridSpec(
            num_scalar_prefetch=1,
            grid=(4,),
            in_specs=[pl.BlockSpec((rows, columns), placed)] * 4
            + [once(w.shape) for w in weights]
            + [pl.BlockSpec((rows, features), flip)] * 2
            + [once(fc1.shape), once(fc2.shape), once((1, hidden_units))] + [once((1, features))] * 3,
            out_specs=[
                pl.BlockSpec((rows, features), flip),
                pl.BlockSpec((rows, hidden_units), flip),
                pl.BlockSpec((rows, hidden_units), flip),
                whole((rows, features)),
                whole((1, hidden_units)),
                whole((1, features)),
            ]
            + [whole((rows, features))] * 4,
        ),
        out_shape=[
            jax.ShapeDtypeStruct((4 * rows, features), BF),
            jax.ShapeDtypeStruct((4 * rows, hidden_units), BF),
            jax.ShapeDtypeStruct((4 * rows, hidden_units), BF),
            jax.ShapeDtypeStruct((rows, features), F32),
            jax.ShapeDtypeStruct((1, hidden_units), F32),
            jax.ShapeDtypeStruct((1, features), F32),
        ]
        + [jax.ShapeDtypeStruct((rows, features), kind) for kind in (BF, F32, BF, F32)],
        compiler_params=pltpu.CompilerParams(vmem_limit_bytes=48 * 1024 * 1024),
        cost_estimate=pl.CostEstimate(flops=2 * 4 * rows * features * (features + 3 * hidden_units), bytes_accessed=14 * MIB, transcendentals=0),
        name="middle_part",
    )(me, *contexts, *weights, hidden, grad, fc1, fc2, fc1_bias, dense_bias, gain, shift)


def turn_kernel(part_ref, near_ref, far_ref, middle_ref, out_grad_ref, gain_ref, w0, w1, w2, w3,
                grad_ref, low_ref, g0, g1, g2, g3, sums_ref):
    upstream = part_ref[...] + near_ref[...].astype(F32) + far_ref[...].astype(F32)
    unit, rstd = norm_parts(middle_ref[...])
    scaled = upstream * gain_ref[...]
    grad = rstd * (
        scaled
        - jnp.mean(scaled, axis=-1, keepdims=True)
        - unit * jnp.mean(scaled * unit, axis=-1, keepdims=True)
    )
    out_grad = out_grad_ref[...].astype(F32)
    grad = grad + out_grad
    low = grad.astype(BF)
    grad_ref[...] = grad
    low_ref[...] = low
    for weight, ref in ((w0, g0), (w1, g1), (w2, g2), (w3, g3)):
        ref[...] = dot(low, weight[...], NT).astype(BF)
    sums_ref[0:1, :] = jnp.sum(grad, axis=0, keepdims=True)
    sums_ref[1:2, :] = jnp.sum(upstream * unit, axis=0, keepdims=True)
    sums_ref[2:3, :] = jnp.sum(upstream, axis=0, keepdims=True)
    sums_ref[3:4, :] = jnp.sum(out_grad, axis=0, keepdims=True)
    sums_ref[4:8, :] = jnp.zeros((4, grad.shape[1]), F32)


def turn(part, near, far, middle, out_grad, gain, weights):
    rows, features = middle.shape
    heads = weights[0].shape[0]
    return pl.pallas_call(
        turn_kernel,
        out_shape=[
            jax.ShapeDtypeStruct((rows, features), F32),
            jax.ShapeDtypeStruct((rows, features), BF),
        ]
        + [jax.ShapeDtypeStruct((rows, heads), BF)] * 4
        + [jax.ShapeDtypeStruct((8, features), F32)],
        compiler_params=pltpu.CompilerParams(vmem_limit_bytes=32 * 1024 * 1024),
        cost_estimate=pl.CostEstimate(flops=2 * 4 * rows * features * heads, bytes_accessed=7 * MIB, transcendentals=0),
        name="turn",
    )(part, near, far, middle, out_grad, gain, *weights)


def rows_kernel(dims, me_ref, left_ref, weight_ref, part3_ref, part2_ref, part1_ref, part0_ref):
    step = pl.program_id(0)
    part = dot(left_ref[...], weight_ref[...], dims)
    for at, ref in enumerate((part3_ref, part2_ref, part1_ref, part0_ref)):
        @pl.when(step == at)
        def _():
            ref[...] = part.astype(ref.dtype)


def rows_product(me, left, weight, dims, order):
    rows = left.shape[0] // 4
    features = weight.shape[1] if dims is NN else weight.shape[0]
    return pl.pallas_call(
        partial(rows_kernel, dims),
        grid_spec=pltpu.PrefetchScalarGridSpec(
            num_scalar_prefetch=1,
            grid=(4,),
            in_specs=[pl.BlockSpec((rows, left.shape[1]), lambda g, me: (order(3 - g, me), 0)), once(weight.shape)],
            out_specs=[whole((rows, features))] * 4,
        ),
        out_shape=[jax.ShapeDtypeStruct((rows, features), kind) for kind in (BF, F32, BF, F32)],
        compiler_params=pltpu.CompilerParams(vmem_limit_bytes=32 * 1024 * 1024),
        cost_estimate=pl.CostEstimate(flops=2 * 4 * rows * features * left.shape[1], bytes_accessed=6 * MIB, transcendentals=0),
        name="rows_product",
    )(me, left, weight)


def last_kernel(part_ref, near_ref, far_ref, hidden_ref, middle_grad_ref, gain_ref, out_ref):
    upstream = part_ref[...] + near_ref[...].astype(F32) + far_ref[...].astype(F32)
    unit, rstd = norm_parts(hidden_ref[...].astype(F32))
    scaled = upstream * gain_ref[...]
    grad = rstd * (
        scaled
        - jnp.mean(scaled, axis=-1, keepdims=True)
        - unit * jnp.mean(scaled * unit, axis=-1, keepdims=True)
    )
    out_ref[...] = (grad + middle_grad_ref[...]).astype(BF)


def last_norm(part, near, far, hidden, middle_grad, gain):
    rows, features = hidden.shape
    return pl.pallas_call(
        last_kernel,
        out_shape=jax.ShapeDtypeStruct((rows, features), BF),
        compiler_params=pltpu.CompilerParams(vmem_limit_bytes=32 * 1024 * 1024),
        cost_estimate=pl.CostEstimate(flops=2 * rows * features * 16, bytes_accessed=5 * MIB, transcendentals=0),
        name="last_norm",
    )(part, near, far, hidden, middle_grad, gain)


def last_product_kernel(me_ref, left_ref, hidden_ref, weight_ref, part3_ref, part2_ref, part1_ref, part0_ref, sums_ref, bias_ref):
    step = pl.program_id(0)
    left = left_ref[...]
    part = dot(left, weight_ref[...], NT)
    for at, ref in enumerate((part3_ref, part2_ref, part1_ref, part0_ref)):
        @pl.when(step == at)
        def _():
            ref[...] = part.astype(ref.dtype)
    unit, _ = norm_parts(hidden_ref[...].astype(F32))
    gain_sum = jnp.sum(part * unit, axis=0, keepdims=True)
    shift_sum = jnp.sum(part, axis=0, keepdims=True)
    bias_sum = jnp.sum(left.astype(F32), axis=0, keepdims=True)

    @pl.when(step == 0)
    def _():
        sums_ref[0:1, :] = gain_sum
        sums_ref[1:2, :] = shift_sum
        bias_ref[...] = bias_sum

    @pl.when(step != 0)
    def _():
        sums_ref[0:1, :] += gain_sum
        sums_ref[1:2, :] += shift_sum
        bias_ref[...] += bias_sum


def last_product(me, left, hidden, weight):
    rows, features, columns = left.shape[0] // 4, weight.shape[0], left.shape[1]
    return pl.pallas_call(
        last_product_kernel,
        grid_spec=pltpu.PrefetchScalarGridSpec(
            num_scalar_prefetch=1,
            grid=(4,),
            in_specs=[
                pl.BlockSpec((rows, columns), lambda g, me: ((me[0] & 1) ^ (3 - g), 0)),
                pl.BlockSpec((rows, features), lambda g, me: (3 - g, 0)),
                once(weight.shape),
            ],
            out_specs=[whole((rows, features))] * 4 + [whole((2, features)), whole((1, columns))],
        ),
        out_shape=[jax.ShapeDtypeStruct((rows, features), kind) for kind in (BF, F32, BF, F32)]
        + [jax.ShapeDtypeStruct((2, features), F32), jax.ShapeDtypeStruct((1, columns), F32)],
        compiler_params=pltpu.CompilerParams(vmem_limit_bytes=32 * 1024 * 1024),
        cost_estimate=pl.CostEstimate(flops=2 * 4 * rows * features * columns, bytes_accessed=6 * MIB, transcendentals=0),
        name="last_product",
    )(me, left, hidden, weight)


def finish_kernel(rows, width, parity_ref, c1_value, c1_came, c2_value, c2_came, qkv_ref, dense_ref, small_ref):
    first = pl.program_id(0) == parity_ref[0]

    def put(one, two):
        extra = one.shape[1] - width
        qkv_ref[:, 0:width] = one[:, 0:width].astype(F32)
        qkv_ref[:, width : 2 * width] = two[0:rows, 0:width].astype(F32)
        dense_ref[0:extra, :] = one[:, width:].astype(F32).T
        dense_ref[extra : 2 * extra, :] = two[0:rows, width:].astype(F32).T
        small_ref[...] = two[rows:, :].astype(F32)

    @pl.when(first)
    def _():
        put(c1_value, c2_value)

    @pl.when(jnp.logical_not(first))
    def _():
        put(c1_came, c2_came)


def finish(parity, width, c1, c2):
    half, both = c1.value.shape
    full = c2.value.shape[0]
    extra, more = both - width, full - half
    return pl.pallas_call(
        partial(finish_kernel, half, width),
        grid_spec=pltpu.PrefetchScalarGridSpec(
            num_scalar_prefetch=1,
            grid=(2,),
            in_specs=[once((half, both))] * 2 + [once((full, both))] * 2,
            out_specs=[
                pl.BlockSpec((half, 2 * width), lambda g, *_: (g, 0)),
                pl.BlockSpec((2 * extra, half), lambda g, *_: (0, g)),
                pl.BlockSpec((more, both), lambda g, *_: (g, 0)),
            ],
        ),
        out_shape=[
            jax.ShapeDtypeStruct((2 * half, 2 * width), F32),
            jax.ShapeDtypeStruct((2 * extra, 2 * half), F32),
            jax.ShapeDtypeStruct((2 * more, both), F32),
        ],
        compiler_params=pltpu.CompilerParams(vmem_limit_bytes=32 * 1024 * 1024),
        cost_estimate=pl.CostEstimate(flops=1024, bytes_accessed=6 * MIB, transcendentals=0),
        name="finish",
    )(parity, c1.value, c1.came, c2.value, c2.came)


def tensor_send(value, flip):
    return lax.ppermute(value, "tensor", [(i, i ^ flip) for i in range(4)])


def add_low(a, b):
    return (a.astype(F32) + b.astype(F32)).astype(BF)


class Ladder:
    def __init__(self, dp, array):
        self.inner, self.outer = 2, dp // 2
        index = lax.axis_index("dp")
        self.mine, self.place_of = index % 2, index // 2
        self.pairs = [(i, i ^ 1) for i in range(dp)]
        self.array, self.half = array, array.shape[0] // 2
        half = self.outer // 2
        count = self.outer
        self.steps = [("in", s) for s in range(half - 1)] + ([("mid", 0)] if count > 1 else [])
        self.steps += [("out", s) for s in reversed(range(half - 1))]
        self.stages = len(self.steps) + 2
        self.stage = 0
        self.came = self.value = None
        self.open = False

    def along(self, pairs):
        return [(a * self.inner + i, b * self.inner + i) for a, b in pairs for i in range(self.inner)]

    def part(self, which):
        return lax.dynamic_slice_in_dim(self.array, which * self.half, self.half, 0)

    def send(self, *gate):
        count, half = self.outer, self.outer // 2
        if self.stage == 0:
            self.sent, pairs = self.part(1 - self.mine), self.pairs
        elif self.stage == self.stages - 1:
            self.sent, pairs = self.value, self.pairs
        else:
            kind, step = self.steps[self.stage - 1]
            self.sent = self.value
            if kind == "in":
                pairs = [(step, step + 1), (count - 1 - step, count - 2 - step)]
            elif kind == "mid":
                pairs = [(half - 1, half), (half, half - 1)]
            else:
                pairs = [(step + 1, step), (count - 2 - step, count - 1 - step)]
            pairs = self.along(pairs)
        if gate:
            self.sent = after(self.sent, *gate)
        self.came = lax.ppermute(self.sent, "dp", pairs)
        self.open = True
        return self

    def take(self, *gate):
        count = self.outer
        if gate and self.value is not None:
            self.value = after(self.value, *gate)
        if self.stage == 0:
            own = self.part(self.mine)
            if gate:
                own = after(own, *gate)
            self.value = add_low(own, self.came)
        elif self.stage < self.stages - 1:
            kind, step = self.steps[self.stage - 1]
            if kind == "out":
                outside = (self.place_of <= step) | (self.place_of >= count - 1 - step)
                self.value = jnp.where(outside, self.came, self.value)
            else:
                self.value = add_low(self.value, self.came)
        self.stage += 1
        self.open = False
        return self

    def finish(self):
        if self.came is not None and self.open:
            self.take()
        while self.stage < self.stages:
            self.send().take()
        return self

    def rows(self):
        lower = self.mine == 0
        return [jnp.where(lower, self.value, self.came), jnp.where(lower, self.came, self.value)]


class Spread:
    def __init__(self, dp, array):
        self.lines = [[a * 2 + i for a in range(dp // 2)] for i in range(2)]
        self.pairs = [(i, i ^ 1) for i in range(dp)]
        self.mine = lax.axis_index("dp") % 2
        self.array = array
        self.blocks = array.reshape(dp // 2, 2, array.shape[0] // dp, array.shape[1])

    def send(self):
        self.came = lax.ppermute(lax.dynamic_index_in_dim(self.blocks, 1 - self.mine, 1, False), "dp", self.pairs)

    def take(self, *gate):
        self.value = add_low(after(lax.dynamic_index_in_dim(self.blocks, self.mine, 1, False), *gate), self.came)
        return self

    def trade(self):
        self.terms = lax.all_to_all(self.value, "dp", 0, 0, axis_index_groups=self.lines, tiled=True)

    def add(self, *gate):
        self.value = jnp.sum(after(self.terms, *gate).astype(F32), axis=0).astype(BF)
        return self

    def gather(self):
        self.all = lax.all_gather(self.value, "dp", axis=0, tiled=True)


def joined_rows(ladders):
    return jnp.concatenate([piece for ladder in ladders for piece in ladder.rows()], axis=0).astype(F32)


def local(
    dp,
    hidden_in,
    out_grad,
    prefix_len,
    qkv_weight,
    qv_bias,
    dense_weight,
    dense_bias,
    norm1_gain,
    norm1_shift,
    norm2_gain,
    norm2_shift,
    fc1_weight,
    fc1_bias,
    fc2_weight,
    fc2_bias,
):
    rows_here, features = hidden_in.shape
    heads_here, _, head_size = qv_bias.shape
    tensor_index = lax.axis_index("tensor")
    me = tensor_index.reshape(1)
    slopes = 2.0 ** (-8.0 * (tensor_index * heads_here + 1 + lax.iota(jnp.int32, heads_here)).astype(F32) / HEADS)
    bias_full = jnp.stack(
        [qv_bias[:, 0], jnp.zeros_like(qv_bias[:, 0]), qv_bias[:, 1]], axis=1
    ).reshape(1, -1)
    row = lambda v: v.reshape(1, -1)

    norm1 = (qkv_weight, bias_full, row(norm1_gain), row(norm1_shift))
    hidden_x = tensor_send(hidden_in, 2)
    hidden_c = tensor_send(hidden_in, 1)
    dense_c = tensor_send(dense_weight, 1)
    normed_near, joined_near = project(me, (hidden_in, hidden_c), *norm1)
    share = dense_weight.shape[0] // 2
    parity = lax.axis_index("dp") % 2
    dense_share = lax.dynamic_slice_in_dim(dense_weight, parity * share, share, 0)
    hidden_xc = tensor_send(after(hidden_x, joined_near), 1)
    dense_half = tensor_send(after(dense_share, hidden_x, joined_near), 2)
    grad_x = tensor_send(after(out_grad, hidden_x, joined_near), 2)
    normed_far, joined_far = project(me, (hidden_x, hidden_xc), *norm1)
    grad_c = tensor_send(after(out_grad, hidden_c), 1)
    context, totals = attend_forward(joined_near, joined_far, prefix_len, slopes, me)
    context_x = tensor_send(context, 2)
    context_c = tensor_send(context, 1)
    dense_other = lax.ppermute(after(dense_half, context), "dp", [(i, i ^ 1) for i in range(dp)])
    dense_x = jnp.where(
        parity == 0,
        jnp.concatenate([dense_half, dense_other], axis=0),
        jnp.concatenate([dense_other, dense_half], axis=0),
    )
    dense_xc = tensor_send(dense_x, 1)
    dense_blocks = [dense_weight, dense_c, dense_x, dense_xc]
    grad_xc = tensor_send(after(grad_x, context), 1)
    grad_all = jnp.concatenate([out_grad, grad_c, grad_x, grad_xc], axis=0)
    hidden_all = jnp.concatenate([hidden_in, hidden_c, hidden_x, after(hidden_xc, context)], axis=0)
    context_xc = tensor_send(after(context_x, grad_all, hidden_all), 1)

    (normed2_all, activated, pre_grad, middle, fc1_bias_sum, attn_squares, part3, part2, part1, part0) = middle_part(
        me, (context, context_c, context_x, context_xc), dense_blocks, hidden_all, grad_all,
        fc1_weight, fc2_weight, row(fc1_bias), row(dense_bias), row(norm2_gain), row(norm2_shift),
    )

    over = tensor_send(part3, 1)
    near = tensor_send(part1, 1)
    half = features // 2
    fc1_term = dot(normed2_all, pre_grad, TN).astype(BF)
    b1, b2 = Ladder(dp, fc1_term[:half]), Ladder(dp, fc1_term[half:])
    b1.send()
    chip = (after(part2, b1.sent) + over.astype(F32)).astype(BF)
    far = tensor_send(chip, 2)
    fc2_term = dot(after(activated, chip), grad_all, TN).astype(BF)
    a1, a2 = Ladder(dp, fc2_term[:half]), Ladder(dp, fc2_term[half:])
    b2.send(fc2_term)
    mlp3, mlp2, mlp1, mlp0 = rows_product(me, after(activated, b2.sent), fc2_weight, NN, lambda g, me: g)
    b1.take(mlp0).send()
    middle_grad, middle_low, *context_grads, turn_sums = turn(
        after(part0, b1.value), near, far, middle, out_grad, row(norm2_gain), dense_blocks
    )
    arrived = [context_grads[0]] + [tensor_send(context_grads[flip], flip) for flip in (2, 3, 1)]
    arrived = [arrived[0], arrived[3], arrived[1], arrived[2]]
    mlp_over = tensor_send(after(mlp3, arrived[1]), 1)
    mlp_near = tensor_send(after(mlp1, arrived[1]), 1)
    b1.take(arrived[1]).send()
    b2.take(b1.value).send()
    middle_x = tensor_send(after(middle_low, arrived[2]), 2)
    a1.send(b2.value)
    mlp_chip = (after(mlp2, a1.sent) + mlp_over.astype(F32)).astype(BF)
    joined_grad0 = attend_backward(
        after(joined_near, a1.sent, mlp_chip), joined_far, totals, context, arrived, prefix_len, slopes, me, 0
    )
    b1.take(joined_grad0).send()
    b2.take(b1.value).send()
    a1.take(b2.value).send()
    middle_c = tensor_send(after(middle_low, a1.value), 1)
    middle_xc = tensor_send(after(middle_x, a1.value), 1)
    a2.send(middle_xc)
    mlp_far = tensor_send(after(mlp_chip, middle_xc), 2)
    normed1_all = jnp.concatenate([after(normed_near, a2.sent), normed_far], axis=0)
    joined_grad1 = attend_backward(
        after(joined_near, a2.sent), joined_far, totals, context, arrived, prefix_len, slopes, me, 1
    )
    width, extra = joined_grad1.shape[1], context.shape[1] // 2
    wide = width + extra
    qkv_term = dot(normed1_all, joined_grad1, TN).astype(BF)
    middle_all = jnp.concatenate([after(middle_low, qkv_term), middle_c, middle_x, middle_xc], axis=0)
    context_flip = jnp.concatenate(
        [
            lax.dynamic_slice_in_dim(after(context, qkv_term), (tensor_index ^ flip) * rows_here, rows_here, 0)
            for flip in range(4)
        ],
        axis=0,
    )
    dense_term = dot(middle_all, context_flip, TN).astype(BF)
    joined_grad = jnp.concatenate([joined_grad0, after(joined_grad1, dense_term)], axis=1)
    last3, last2, last1, last0, last_sums, joined_sums = last_product(me, joined_grad, hidden_all, qkv_weight)
    b1.take(last0).send()
    b2.take(b1.value).send()
    a1.take(b2.value).send()
    qkv_first = dot(after(normed1_all, dense_term), joined_grad0, TN).astype(BF)
    c1 = Ladder(dp, jnp.concatenate([qkv_first, after(dense_term, a1.value)[:, :extra]], axis=1))
    c1.send()
    a2.take(c1.sent).send()
    mlp_out = after(mlp0, a2.value) + mlp_near.astype(F32) + mlp_far.astype(F32) + fc2_bias
    final = middle + mlp_out
    residual = hidden_in.astype(F32)
    column_squares = lambda v: jnp.sum(v * v, axis=0, keepdims=True)
    joined_sums = joined_sums.reshape(heads_here, 3, head_size)
    qv_sums = jnp.stack([joined_sums[:, 0], joined_sums[:, 2]], axis=1).reshape(1, -1)
    small = jnp.concatenate(
        [column_squares(residual), attn_squares, column_squares(mlp_out), column_squares(final), turn_sums[:4], last_sums],
        axis=0,
    )
    small = small + tensor_send(small, 1)
    small = small + tensor_send(small, 2)
    small = jnp.concatenate(
        [fc1_bias_sum, jnp.pad(qv_sums, ((0, 0), (0, features - qv_sums.shape[1]))), small], axis=0
    )
    small = jnp.pad(small, ((0, 16 - small.shape[0]), (0, 2 * wide - features))).astype(BF)
    c2_term = jnp.concatenate([qkv_term, dense_term[:, extra:]], axis=1)
    b1.take(small)
    c2 = Ladder(dp, jnp.concatenate([c2_term[:half], small[:, :wide], c2_term[half:], small[:, wide:]], axis=0))
    c2.send(b1.came)
    b2.take(c2.sent).send()
    a1.take(b2.value).send()
    a2.take(a1.value).send()
    c1.take(a2.value).send()
    b2.take(c1.value)
    last_over = tensor_send(after(last3, b2.came), 1)
    last_near = tensor_send(after(last1, b2.came), 1)
    a1.take(b2.came).send()
    a2.take(a1.value).send()
    c1.take(a2.value).send()
    c2.take(c1.value).send()
    last_chip = (after(last2, c2.value) + last_over.astype(F32)).astype(BF)
    last_far = tensor_send(last_chip, 2)
    fc1_sum = after(joined_rows([b1, b2]), last_chip)
    a1.take(fc1_sum)
    a2.take(a1.came).send()
    c1.take(a2.value).send()
    c2.take(c1.value).send()
    hidden_grad = last_norm(after(last0, c2.value), last_near, last_far, hidden_in, middle_grad, row(norm1_gain))
    a2.take(hidden_grad)
    c1.take(a2.came).send()
    c2.take(c1.value).send()
    fc2_sum = after(joined_rows([a1, a2]), c2.value)
    c1.take(fc2_sum)
    c2.take(c1.came).send()
    c2.finish()
    qkv_sum, dense_sum, small_sum = finish(parity.reshape(1), width, c1, c2)
    by_dp = jnp.concatenate([small_sum[:16], small_sum[16:]], axis=1)[:, :features]
    by_all = by_dp[5:]
    qv_bias_grad = by_dp[1, : qv_sums.shape[1]].reshape(heads_here, 2, head_size)
    entry_count = rows_here * features * dp * 4
    sublayer_rms = jnp.sqrt(jnp.sum(by_dp[2:6], axis=1) / float(entry_count))
    return (
        final.astype(BF),
        hidden_grad,
        qkv_sum,
        qv_bias_grad,
        dense_sum,
        by_all[1],
        by_all[5],
        by_all[6],
        by_all[2],
        by_all[3],
        fc1_sum.astype(F32),
        by_dp[0],
        fc2_sum.astype(F32),
        by_all[4],
        sublayer_rms,
    )


def solution(mesh):
    return jax.shard_map(
        partial(local, mesh.shape["dp"]),
        mesh=mesh,
        in_specs=(
            P(("dp", "tensor"), None),
            P(("dp", "tensor"), None),
            P("dp"),
            P(None, "tensor"),
            P("tensor", None, None),
            P("tensor", None),
            P(),
            P(),
            P(),
            P(),
            P(),
            P(None, "tensor"),
            P("tensor"),
            P("tensor", None),
            P(),
        ),
        out_specs=(
            P(("dp", "tensor"), None),
            P(("dp", "tensor"), None),
            P(None, "tensor"),
            P("tensor", None, None),
            P("tensor", None),
            P(),
            P(),
            P(),
            P(),
            P(),
            P(None, "tensor"),
            P("tensor"),
            P("tensor", None),
            P(),
            P(),
        ),
        check_vma=False,
    )
```

```python
from functools import partial

import jax
import jax.numpy as jnp
from jax import lax
from jax.experimental import pallas as pl
from jax.experimental.pallas import tpu as pltpu
from jax.sharding import PartitionSpec as P

HEADS = 16
PREFIX_MOST = 512

epsilon = 1e-05
BF = jnp.bfloat16
F32 = jnp.float32
NT = (((1,), (1,)), ((), ()))
NN = (((1,), (0,)), ((), ()))
TN = (((0,), (0,)), ((), ()))


def dot(a, b, dims):
    return lax.dot_general(a, b, dims, preferred_element_type=F32)


def after(value, *others):
    return lax.optimization_barrier((value,) + others)[0]


def norm_parts(values):
    center = jnp.mean(values, axis=-1, keepdims=True)
    deviation = values - center
    variance = jnp.mean(deviation * deviation, axis=-1, keepdims=True)
    rstd = lax.rsqrt(variance + epsilon)
    return deviation * rstd, rstd


def norm_backward(values, gain, upstream):
    unit, rstd = norm_parts(values)
    scaled = upstream * gain
    grad = rstd * (
        scaled
        - jnp.mean(scaled, axis=-1, keepdims=True)
        - unit * jnp.mean(scaled * unit, axis=-1, keepdims=True)
    )
    return grad, jnp.sum(upstream * unit, axis=0), jnp.sum(upstream, axis=0)


def split3(value):
    high = value.astype(BF).astype(F32)
    rest = value - high
    mid = rest.astype(BF).astype(F32)
    return high, mid, rest - mid


def place(lane, base, items):
    out = jnp.zeros(lane.shape, F32)
    for i, item in enumerate(items):
        out = jnp.where(lane == base + i, item, out)
    return out


def causal_end(row_block, size, length):
    return min(max((row_block + 1) * size, min(PREFIX_MOST, length)), length)


def fill_masks(masks, prefix, size, blocks, transposed):
    shape = (size, size)
    for index, (row_block, col_block) in enumerate(blocks):
        rows = row_block * size + lax.broadcasted_iota(jnp.int32, shape, 1 if transposed else 0)
        cols = col_block * size + lax.broadcasted_iota(jnp.int32, shape, 0 if transposed else 1)
        allowed = (cols <= rows) | ((cols < prefix) & (rows < prefix))
        beyond = jnp.maximum(cols - rows, 0).astype(F32)
        masks[index] = jnp.where(allowed, -2.0 * beyond, -1e30)


def special_blocks(length, size):
    out = []
    for row_block in range(length // size):
        for col_block in range(causal_end(row_block, size, length) // size):
            if col_block >= row_block:
                out.append((row_block, col_block))
    return out


def load_order(me_ref, near_ref, far_ref, joined_ref):
    half = near_ref.shape[0]
    chip = me_ref[0] >> 1
    joined_ref[pl.ds(pl.multiple_of(chip * half, half), half), :] = near_ref[...]
    joined_ref[pl.ds(pl.multiple_of((1 - chip) * half, half), half), :] = far_ref[...]


def attend_forward_kernel(size, prefix_ref, slope_ref, me_ref, near_ref, far_ref, context_ref, total_ref, masks, joined_ref):
    length = joined_ref.shape[0]
    pair = pl.program_id(0)
    load_order(me_ref, near_ref, far_ref, joined_ref)
    blocks = special_blocks(length, size)

    @pl.when(pair == 0)
    def _():
        fill_masks(masks, prefix_ref[0], size, blocks, False)

    lane = lax.broadcasted_iota(jnp.int32, (length, 128), 1)
    low = lane < 64
    position = lax.broadcasted_iota(jnp.int32, (length, 1), 0).astype(F32)
    tiles = [joined_ref[:, i * 128 : (i + 1) * 128].astype(F32) for i in range(3)]
    rolled0 = pltpu.roll(tiles[0], 64, 1)
    rolled1 = pltpu.roll(tiles[1], 64, 1)
    sides = []
    for head in range(2):
        slope = slope_ref[pair * 2 + head]
        own = jnp.logical_not(low) if head == 0 else low
        base = 0 if head == 0 else 64
        query = jnp.where(own, (rolled0 if head == 0 else rolled1) * 0.125, place(lane, base, (1.0, 1.0, 1.0)))
        keys = jnp.where(own, tiles[0] if head == 0 else tiles[2], place(lane, base, split3(slope * position)))
        value = jnp.where(low, tiles[1], 1.0) if head == 0 else jnp.where(low, 1.0, tiles[2])
        sides.append((slope, query.astype(BF), keys.astype(BF), value.astype(BF)))
    low_block = low[:size]
    lane_block = lane[:size]
    for row_block in range(length // size):
        end = causal_end(row_block, size, length)
        rows = slice(row_block * size, (row_block + 1) * size)
        results = []
        for head in range(2):
            slope, query, keys, value = sides[head]
            scores = dot(query[rows], keys[:end], NT)
            columns = []
            for col_block in range(end // size):
                piece = scores[:, col_block * size : (col_block + 1) * size]
                if col_block >= row_block:
                    piece = piece + slope * masks[blocks.index((row_block, col_block))]
                columns.append(piece)
            highest = columns[0]
            for piece in columns[1:]:
                highest = jnp.maximum(highest, piece)
            highest = jnp.max(highest, axis=-1, keepdims=True)
            powered = jnp.concatenate([jnp.exp(piece - highest).astype(BF) for piece in columns], axis=1)
            gathered = dot(powered, value[:end], NN)
            total = gathered[:, 64:65] if head == 0 else gathered[:, 0:1]
            results.append((gathered / total, highest + jnp.log(total)))
        context_ref[rows, :] = jnp.where(low_block, results[0][0], results[1][0]).astype(BF)
        total_ref[rows, :] = jnp.where(lane_block == 0, results[0][1], results[1][1])


def attend_forward(near, far, prefix, slopes, me, size=256):
    length, columns = 2 * near.shape[0], near.shape[1]
    pairs = columns // 384
    count = len(special_blocks(length, size))
    tile = pl.BlockSpec((length, 128), lambda p, *_: (0, p))
    return pl.pallas_call(
        partial(attend_forward_kernel, size),
        grid_spec=pltpu.PrefetchScalarGridSpec(
            num_scalar_prefetch=3,
            grid=(pairs,),
            in_specs=[pl.BlockSpec((length // 2, 384), lambda p, *_: (0, p))] * 2,
            out_specs=[tile, tile],
            scratch_shapes=[pltpu.VMEM((count, size, size), F32), pltpu.VMEM((length, 384), BF)],
        ),
        out_shape=[
            jax.ShapeDtypeStruct((length, pairs * 128), BF),
            jax.ShapeDtypeStruct((length, pairs * 128), F32),
        ],
        compiler_params=pltpu.CompilerParams(vmem_limit_bytes=40 * 1024 * 1024),
        cost_estimate=pl.CostEstimate(flops=4 * 2 * 2 * length * length * 128, bytes_accessed=4 * 1024 * 1024, transcendentals=0),
        name="attend_forward",
    )(prefix, slopes, me, near, far)


def attend_backward_kernel(
    size, prefix_ref, slope_ref, me_ref, near_ref, far_ref, total_ref, context_ref, g0, g1, g2, g3,
    final_ref, masks, query_sum, grad_ref, joined_ref, out_ref,
):
    length = joined_ref.shape[0]
    pair = pl.program_id(0)
    load_order(me_ref, near_ref, far_ref, joined_ref)
    rows = g0.shape[0]
    for flip, ref in enumerate((g0, g1, g2, g3)):
        grad_ref[pl.ds(pl.multiple_of((me_ref[0] ^ flip) * rows, rows), rows), :] = ref[...]
    totals = total_ref[...]
    blocks = special_blocks(length, size)

    @pl.when(pair == 0)
    def _():
        fill_masks(masks, prefix_ref[0], size, blocks, True)

    lane = lax.broadcasted_iota(jnp.int32, (length, 128), 1)
    low = lane < 64
    position = lax.broadcasted_iota(jnp.int32, (length, 1), 0).astype(F32)
    tiles = [joined_ref[:, i * 128 : (i + 1) * 128].astype(F32) for i in range(3)]
    rolled = [pltpu.roll(tile, 64, 1) for tile in tiles]
    grad = grad_ref[...].astype(F32)
    product = grad * context_ref[...].astype(F32)
    grad_low = grad.astype(BF)
    rolled_low = [tile.astype(BF) for tile in rolled]
    sides = []
    for head in range(2):
        slope = slope_ref[pair * 2 + head]
        own = jnp.logical_not(low) if head == 0 else low
        base = 0 if head == 0 else 64
        log_total = totals[:, head : head + 1]
        query = jnp.where(
            own, rolled[head] * 0.125, place(lane, base, (1.0, 1.0, 1.0) + split3(log_total))
        )
        keys = jnp.where(
            own, tiles[0] if head == 0 else tiles[2], place(lane, base, split3(slope * position) + (-1.0, -1.0, -1.0))
        )
        head_lanes = low if head == 0 else jnp.logical_not(low)
        inner = jnp.sum(jnp.where(head_lanes, product, 0.0), axis=1, keepdims=True)
        base = 64 - base
        value = jnp.where(head_lanes, tiles[1] if head == 0 else tiles[2], place(lane, 64 if head == 0 else 0, (-1.0, -1.0, -1.0)))
        upstream = jnp.where(head_lanes, grad, place(lane, 64 if head == 0 else 0, split3(inner)))
        sides.append((slope, query.astype(BF), keys.astype(BF), value.astype(BF), upstream.astype(BF)))
    low_block = low[:size]
    for col_block in range(length // size):
        first = col_block if col_block * size >= PREFIX_MOST else 0
        cols = slice(col_block * size, (col_block + 1) * size)
        start = first * size
        results = []
        for head in range(2):
            slope, query, keys, value, upstream = sides[head]
            scores = dot(keys[cols], query[start:], NT)
            prob_grad = dot(value[cols], upstream[start:], NT)
            weights, score_grads = [], []
            for row_block in range(first, length // size):
                at = slice((row_block - first) * size, (row_block - first + 1) * size)
                piece = scores[:, at]
                if col_block >= row_block:
                    piece = piece + slope * masks[blocks.index((row_block, col_block))]
                powered = jnp.exp(piece)
                weights.append(powered.astype(BF))
                score_grads.append((powered * prob_grad[:, at]).astype(BF))
            weights = jnp.concatenate(weights, axis=1)
            score_grads = jnp.concatenate(score_grads, axis=1)
            value_grad = dot(weights, grad_low[start:], NN)
            key_grad = dot(score_grads, rolled_low[head][start:], NN) * 0.125
            query_grad = dot(score_grads, rolled_low[0 if head == 0 else 2][cols], TN)
            if col_block == 0:
                query_sum[head] = query_grad
            else:
                query_sum[head, start:] = query_sum[head, start:] + query_grad
            results.append((key_grad, value_grad))
        (key0, value0), (key1, value1) = results
        out_ref[cols, 0:128] = key0.astype(BF)
        out_ref[cols, 128:256] = value0.astype(BF)
        out_ref[cols, 256:384] = jnp.where(low_block, key1, value1).astype(BF)
    out_ref[:, 0:128] = jnp.where(low, query_sum[0] * 0.125, out_ref[:, 0:128].astype(F32)).astype(BF)
    out_ref[:, 128:256] = jnp.where(low, out_ref[:, 128:256].astype(F32), query_sum[1] * 0.125).astype(BF)
    half = length // 2
    chip = me_ref[0] >> 1
    final_ref[0:half, :] = out_ref[pl.ds(pl.multiple_of(chip * half, half), half), :]
    final_ref[half:, :] = out_ref[pl.ds(pl.multiple_of((1 - chip) * half, half), half), :]


def attend_backward(near, far, totals, context, grads, prefix, slopes, me, pair, size=256):
    length = 2 * near.shape[0]
    count = len(special_blocks(length, size))
    rows = grads[0].shape[0]
    return pl.pallas_call(
        partial(attend_backward_kernel, size),
        grid_spec=pltpu.PrefetchScalarGridSpec(
            num_scalar_prefetch=3,
            grid=(1,),
            in_specs=[pl.BlockSpec((length // 2, 384), lambda p, *_: (0, pair))] * 2
            + [pl.BlockSpec((length, 128), lambda p, *_: (0, pair))] * 2
            + [pl.BlockSpec((rows, 128), lambda p, *_: (0, pair))] * 4,
            out_specs=pl.BlockSpec((length, 384), lambda p, *_: (0, 0)),
            scratch_shapes=[
                pltpu.VMEM((count, size, size), F32),
                pltpu.VMEM((2, length, 128), F32),
                pltpu.VMEM((length, 128), BF),
                pltpu.VMEM((length, 384), BF),
                pltpu.VMEM((length, 384), BF),
            ],
        ),
        out_shape=jax.ShapeDtypeStruct((length, 384), BF),
        compiler_params=pltpu.CompilerParams(vmem_limit_bytes=48 * 1024 * 1024),
        cost_estimate=pl.CostEstimate(flops=2 * 5 * 2 * length * length * 256, bytes_accessed=3 * 1024 * 1024, transcendentals=0),
        name="attend_backward",
    )(prefix, slopes[2 * pair : 2 * pair + 2], me, near, far, totals, context, *grads)


MIB = 1024 * 1024


def whole(shape):
    return pl.BlockSpec(shape, lambda *_: (0,) * len(shape))


def once(shape):
    return pl.BlockSpec(shape, lambda *_: (0,) * len(shape), pipeline_mode=pl.Buffered(1))


def project_kernel(me_ref, own_ref, near_ref, weight_ref, bias_ref, gain_ref, shift_ref, normed_ref, joined_ref):
    block = jnp.where(pl.program_id(0) == 0, own_ref[...].astype(F32), near_ref[...].astype(F32))
    normed = (norm_parts(block)[0] * gain_ref[...] + shift_ref[...]).astype(BF)
    normed_ref[...] = normed
    joined_ref[...] = (dot(normed, weight_ref[...], NN) + bias_ref[...]).astype(BF)


def project(me, blocks, weight, bias, gain, shift):
    rows, features = blocks[0].shape
    columns = weight.shape[1]
    return pl.pallas_call(
        project_kernel,
        grid_spec=pltpu.PrefetchScalarGridSpec(
            num_scalar_prefetch=1,
            grid=(2,),
            in_specs=[once((rows, features))] * 2
            + [once((features, columns)), once((1, columns)), once((1, features)), once((1, features))],
            out_specs=[
                pl.BlockSpec((rows, features), lambda g, me: ((me[0] & 1) ^ g, 0)),
                pl.BlockSpec((rows, columns), lambda g, me: ((me[0] & 1) ^ g, 0)),
            ],
        ),
        out_shape=[
            jax.ShapeDtypeStruct((2 * rows, features), BF),
            jax.ShapeDtypeStruct((2 * rows, columns), BF),
        ],
        compiler_params=pltpu.CompilerParams(vmem_limit_bytes=32 * 1024 * 1024),
        cost_estimate=pl.CostEstimate(flops=2 * 2 * rows * features * columns, bytes_accessed=6 * MIB, transcendentals=0),
        name="project",
    )(me, *blocks, weight, bias, gain, shift)


def middle_kernel(me_ref, *refs):
    (c0, c1, c2, c3, w0, w1, w2, w3, hidden_ref, grad_ref, fc1_ref, fc2_ref, fc1_bias_ref,
     dense_bias_ref, gain_ref, shift_ref) = refs[:16]
    (normed_ref, act_ref, pre_ref, middle_ref, bias_sum_ref, squares_ref,
     part3_ref, part2_ref, part1_ref, part0_ref) = refs[16:]
    step = pl.program_id(0)
    grad = grad_ref[...]
    attn = dense_bias_ref[...]
    for context_ref, weight in ((c0, w0), (c1, w1), (c2, w2), (c3, w3)):
        attn = attn + dot(context_ref[...], weight[...], NN)
    middle = hidden_ref[...].astype(F32) + attn
    normed = (norm_parts(middle)[0] * gain_ref[...] + shift_ref[...]).astype(BF)
    normed_ref[...] = normed
    middle_ref[...] = middle
    squares_ref[...] = jnp.sum(attn * attn, axis=0, keepdims=True)
    pre = dot(normed, fc1_ref[...], NN) + fc1_bias_ref[...]
    act_grad = dot(grad, fc2_ref[...], NT)
    cubic = 0.7978845608028654
    square = pre * pre
    inner = jnp.tanh(pre * (cubic + cubic * 0.044715 * square))
    half = 0.5 + 0.5 * inner
    act = pre * half
    act_ref[...] = act.astype(BF)
    slope = half + act * (1.0 - inner) * (cubic + cubic * 3 * 0.044715 * square)
    pre_grad = (act_grad * slope).astype(BF)
    pre_ref[...] = pre_grad
    sums = jnp.sum(pre_grad.astype(F32), axis=0, keepdims=True)
    part = dot(pre_grad, fc1_ref[...], NT)

    @pl.when(step == 0)
    def _():
        bias_sum_ref[...] = sums

    @pl.when(step != 0)
    def _():
        bias_sum_ref[...] += sums

    for at, ref in enumerate((part3_ref, part2_ref, part1_ref, part0_ref)):
        @pl.when(step == at)
        def _():
            ref[...] = part.astype(ref.dtype)


def middle_part(me, contexts, weights, hidden, grad, fc1, fc2, fc1_bias, dense_bias, gain, shift):
    rows = hidden.shape[0] // 4
    features, hidden_units = fc1.shape
    flip = lambda g, me: (3 - g, 0)
    placed = lambda g, me: (me[0] ^ (3 - g), 0)
    columns = contexts[0].shape[1]
    return pl.pallas_call(
        middle_kernel,
        grid_spec=pltpu.PrefetchScalarGridSpec(
            num_scalar_prefetch=1,
            grid=(4,),
            in_specs=[pl.BlockSpec((rows, columns), placed)] * 4
            + [once(w.shape) for w in weights]
            + [pl.BlockSpec((rows, features), flip)] * 2
            + [once(fc1.shape), once(fc2.shape), once((1, hidden_units))] + [once((1, features))] * 3,
            out_specs=[
                pl.BlockSpec((rows, features), flip),
                pl.BlockSpec((rows, hidden_units), flip),
                pl.BlockSpec((rows, hidden_units), flip),
                whole((rows, features)),
                whole((1, hidden_units)),
                whole((1, features)),
            ]
            + [whole((rows, features))] * 4,
        ),
        out_shape=[
            jax.ShapeDtypeStruct((4 * rows, features), BF),
            jax.ShapeDtypeStruct((4 * rows, hidden_units), BF),
            jax.ShapeDtypeStruct((4 * rows, hidden_units), BF),
            jax.ShapeDtypeStruct((rows, features), F32),
            jax.ShapeDtypeStruct((1, hidden_units), F32),
            jax.ShapeDtypeStruct((1, features), F32),
        ]
        + [jax.ShapeDtypeStruct((rows, features), kind) for kind in (BF, F32, BF, F32)],
        compiler_params=pltpu.CompilerParams(vmem_limit_bytes=48 * 1024 * 1024),
        cost_estimate=pl.CostEstimate(flops=2 * 4 * rows * features * (features + 3 * hidden_units), bytes_accessed=14 * MIB, transcendentals=0),
        name="middle_part",
    )(me, *contexts, *weights, hidden, grad, fc1, fc2, fc1_bias, dense_bias, gain, shift)


def turn_kernel(part_ref, near_ref, far_ref, middle_ref, out_grad_ref, gain_ref, w0, w1, w2, w3,
                grad_ref, low_ref, g0, g1, g2, g3, sums_ref):
    upstream = part_ref[...] + near_ref[...].astype(F32) + far_ref[...].astype(F32)
    unit, rstd = norm_parts(middle_ref[...])
    scaled = upstream * gain_ref[...]
    grad = rstd * (
        scaled
        - jnp.mean(scaled, axis=-1, keepdims=True)
        - unit * jnp.mean(scaled * unit, axis=-1, keepdims=True)
    )
    out_grad = out_grad_ref[...].astype(F32)
    grad = grad + out_grad
    low = grad.astype(BF)
    grad_ref[...] = grad
    low_ref[...] = low
    for weight, ref in ((w0, g0), (w1, g1), (w2, g2), (w3, g3)):
        ref[...] = dot(low, weight[...], NT).astype(BF)
    sums_ref[0:1, :] = jnp.sum(grad, axis=0, keepdims=True)
    sums_ref[1:2, :] = jnp.sum(upstream * unit, axis=0, keepdims=True)
    sums_ref[2:3, :] = jnp.sum(upstream, axis=0, keepdims=True)
    sums_ref[3:4, :] = jnp.sum(out_grad, axis=0, keepdims=True)
    sums_ref[4:8, :] = jnp.zeros((4, grad.shape[1]), F32)


def turn(part, near, far, middle, out_grad, gain, weights):
    rows, features = middle.shape
    heads = weights[0].shape[0]
    return pl.pallas_call(
        turn_kernel,
        out_shape=[
            jax.ShapeDtypeStruct((rows, features), F32),
            jax.ShapeDtypeStruct((rows, features), BF),
        ]
        + [jax.ShapeDtypeStruct((rows, heads), BF)] * 4
        + [jax.ShapeDtypeStruct((8, features), F32)],
        compiler_params=pltpu.CompilerParams(vmem_limit_bytes=32 * 1024 * 1024),
        cost_estimate=pl.CostEstimate(flops=2 * 4 * rows * features * heads, bytes_accessed=7 * MIB, transcendentals=0),
        name="turn",
    )(part, near, far, middle, out_grad, gain, *weights)


def rows_kernel(dims, me_ref, left_ref, weight_ref, part3_ref, part2_ref, part1_ref, part0_ref):
    step = pl.program_id(0)
    part = dot(left_ref[...], weight_ref[...], dims)
    for at, ref in enumerate((part3_ref, part2_ref, part1_ref, part0_ref)):
        @pl.when(step == at)
        def _():
            ref[...] = part.astype(ref.dtype)


def rows_product(me, left, weight, dims, order):
    rows = left.shape[0] // 4
    features = weight.shape[1] if dims is NN else weight.shape[0]
    return pl.pallas_call(
        partial(rows_kernel, dims),
        grid_spec=pltpu.PrefetchScalarGridSpec(
            num_scalar_prefetch=1,
            grid=(4,),
            in_specs=[pl.BlockSpec((rows, left.shape[1]), lambda g, me: (order(3 - g, me), 0)), once(weight.shape)],
            out_specs=[whole((rows, features))] * 4,
        ),
        out_shape=[jax.ShapeDtypeStruct((rows, features), kind) for kind in (BF, F32, BF, F32)],
        compiler_params=pltpu.CompilerParams(vmem_limit_bytes=32 * 1024 * 1024),
        cost_estimate=pl.CostEstimate(flops=2 * 4 * rows * features * left.shape[1], bytes_accessed=6 * MIB, transcendentals=0),
        name="rows_product",
    )(me, left, weight)


def last_kernel(part_ref, near_ref, far_ref, hidden_ref, middle_grad_ref, gain_ref, out_ref):
    upstream = part_ref[...] + near_ref[...].astype(F32) + far_ref[...].astype(F32)
    unit, rstd = norm_parts(hidden_ref[...].astype(F32))
    scaled = upstream * gain_ref[...]
    grad = rstd * (
        scaled
        - jnp.mean(scaled, axis=-1, keepdims=True)
        - unit * jnp.mean(scaled * unit, axis=-1, keepdims=True)
    )
    out_ref[...] = (grad + middle_grad_ref[...]).astype(BF)


def last_norm(part, near, far, hidden, middle_grad, gain):
    rows, features = hidden.shape
    return pl.pallas_call(
        last_kernel,
        out_shape=jax.ShapeDtypeStruct((rows, features), BF),
        compiler_params=pltpu.CompilerParams(vmem_limit_bytes=32 * 1024 * 1024),
        cost_estimate=pl.CostEstimate(flops=2 * rows * features * 16, bytes_accessed=5 * MIB, transcendentals=0),
        name="last_norm",
    )(part, near, far, hidden, middle_grad, gain)


def last_product_kernel(me_ref, left_ref, hidden_ref, weight_ref, part3_ref, part2_ref, part1_ref, part0_ref, sums_ref, bias_ref):
    step = pl.program_id(0)
    left = left_ref[...]
    part = dot(left, weight_ref[...], NT)
    for at, ref in enumerate((part3_ref, part2_ref, part1_ref, part0_ref)):
        @pl.when(step == at)
        def _():
            ref[...] = part.astype(ref.dtype)
    unit, _ = norm_parts(hidden_ref[...].astype(F32))
    gain_sum = jnp.sum(part * unit, axis=0, keepdims=True)
    shift_sum = jnp.sum(part, axis=0, keepdims=True)
    bias_sum = jnp.sum(left.astype(F32), axis=0, keepdims=True)

    @pl.when(step == 0)
    def _():
        sums_ref[0:1, :] = gain_sum
        sums_ref[1:2, :] = shift_sum
        bias_ref[...] = bias_sum

    @pl.when(step != 0)
    def _():
        sums_ref[0:1, :] += gain_sum
        sums_ref[1:2, :] += shift_sum
        bias_ref[...] += bias_sum


def last_product(me, left, hidden, weight):
    rows, features, columns = left.shape[0] // 4, weight.shape[0], left.shape[1]
    return pl.pallas_call(
        last_product_kernel,
        grid_spec=pltpu.PrefetchScalarGridSpec(
            num_scalar_prefetch=1,
            grid=(4,),
            in_specs=[
                pl.BlockSpec((rows, columns), lambda g, me: ((me[0] & 1) ^ (3 - g), 0)),
                pl.BlockSpec((rows, features), lambda g, me: (3 - g, 0)),
                once(weight.shape),
            ],
            out_specs=[whole((rows, features))] * 4 + [whole((2, features)), whole((1, columns))],
        ),
        out_shape=[jax.ShapeDtypeStruct((rows, features), kind) for kind in (BF, F32, BF, F32)]
        + [jax.ShapeDtypeStruct((2, features), F32), jax.ShapeDtypeStruct((1, columns), F32)],
        compiler_params=pltpu.CompilerParams(vmem_limit_bytes=32 * 1024 * 1024),
        cost_estimate=pl.CostEstimate(flops=2 * 4 * rows * features * columns, bytes_accessed=6 * MIB, transcendentals=0),
        name="last_product",
    )(me, left, hidden, weight)


def finish_kernel(rows, width, parity_ref, c1_value, c1_came, c2_value, c2_came, qkv_ref, dense_ref, small_ref):
    first = pl.program_id(0) == parity_ref[0]

    def put(one, two):
        extra = one.shape[1] - width
        qkv_ref[:, 0:width] = one[:, 0:width].astype(F32)
        qkv_ref[:, width : 2 * width] = two[0:rows, 0:width].astype(F32)
        dense_ref[0:extra, :] = one[:, width:].astype(F32).T
        dense_ref[extra : 2 * extra, :] = two[0:rows, width:].astype(F32).T
        small_ref[...] = two[rows:, :].astype(F32)

    @pl.when(first)
    def _():
        put(c1_value, c2_value)

    @pl.when(jnp.logical_not(first))
    def _():
        put(c1_came, c2_came)


def finish(parity, width, c1, c2):
    half, both = c1.value.shape
    full = c2.value.shape[0]
    extra, more = both - width, full - half
    return pl.pallas_call(
        partial(finish_kernel, half, width),
        grid_spec=pltpu.PrefetchScalarGridSpec(
            num_scalar_prefetch=1,
            grid=(2,),
            in_specs=[once((half, both))] * 2 + [once((full, both))] * 2,
            out_specs=[
                pl.BlockSpec((half, 2 * width), lambda g, *_: (g, 0)),
                pl.BlockSpec((2 * extra, half), lambda g, *_: (0, g)),
                pl.BlockSpec((more, both), lambda g, *_: (g, 0)),
            ],
        ),
        out_shape=[
            jax.ShapeDtypeStruct((2 * half, 2 * width), F32),
            jax.ShapeDtypeStruct((2 * extra, 2 * half), F32),
            jax.ShapeDtypeStruct((2 * more, both), F32),
        ],
        compiler_params=pltpu.CompilerParams(vmem_limit_bytes=32 * 1024 * 1024),
        cost_estimate=pl.CostEstimate(flops=1024, bytes_accessed=6 * MIB, transcendentals=0),
        name="finish",
    )(parity, c1.value, c1.came, c2.value, c2.came)


def tensor_send(value, flip):
    return lax.ppermute(value, "tensor", [(i, i ^ flip) for i in range(4)])


def add_low(a, b):
    return (a.astype(F32) + b.astype(F32)).astype(BF)


class Ladder:
    def __init__(self, dp, array):
        self.inner, self.outer = 2, dp // 2
        index = lax.axis_index("dp")
        self.mine, self.place_of = index % 2, index // 2
        self.pairs = [(i, i ^ 1) for i in range(dp)]
        self.array, self.half = array, array.shape[0] // 2
        half = self.outer // 2
        count = self.outer
        self.steps = [("in", s) for s in range(half - 1)] + ([("mid", 0)] if count > 1 else [])
        self.steps += [("out", s) for s in reversed(range(half - 1))]
        self.stages = len(self.steps) + 2
        self.stage = 0
        self.came = self.value = None
        self.open = False

    def along(self, pairs):
        return [(a * self.inner + i, b * self.inner + i) for a, b in pairs for i in range(self.inner)]

    def part(self, which):
        return lax.dynamic_slice_in_dim(self.array, which * self.half, self.half, 0)

    def send(self, *gate):
        count, half = self.outer, self.outer // 2
        if self.stage == 0:
            self.sent, pairs = self.part(1 - self.mine), self.pairs
        elif self.stage == self.stages - 1:
            self.sent, pairs = self.value, self.pairs
        else:
            kind, step = self.steps[self.stage - 1]
            self.sent = self.value
            if kind == "in":
                pairs = [(step, step + 1), (count - 1 - step, count - 2 - step)]
            elif kind == "mid":
                pairs = [(half - 1, half), (half, half - 1)]
            else:
                pairs = [(step + 1, step), (count - 2 - step, count - 1 - step)]
            pairs = self.along(pairs)
        if gate:
            self.sent = after(self.sent, *gate)
        self.came = lax.ppermute(self.sent, "dp", pairs)
        self.open = True
        return self

    def take(self, *gate):
        count = self.outer
        if gate and self.value is not None:
            self.value = after(self.value, *gate)
        if self.stage == 0:
            own = self.part(self.mine)
            if gate:
                own = after(own, *gate)
            self.value = add_low(own, self.came)
        elif self.stage < self.stages - 1:
            kind, step = self.steps[self.stage - 1]
            if kind == "out":
                outside = (self.place_of <= step) | (self.place_of >= count - 1 - step)
                self.value = jnp.where(outside, self.came, self.value)
            else:
                self.value = add_low(self.value, self.came)
        self.stage += 1
        self.open = False
        return self

    def finish(self):
        if self.came is not None and self.open:
            self.take()
        while self.stage < self.stages:
            self.send().take()
        return self

    def rows(self):
        lower = self.mine == 0
        return [jnp.where(lower, self.value, self.came), jnp.where(lower, self.came, self.value)]


class Spread:
    def __init__(self, dp, array):
        self.lines = [[a * 2 + i for a in range(dp // 2)] for i in range(2)]
        self.pairs = [(i, i ^ 1) for i in range(dp)]
        self.mine = lax.axis_index("dp") % 2
        self.array = array
        self.blocks = array.reshape(dp // 2, 2, array.shape[0] // dp, array.shape[1])

    def send(self):
        self.came = lax.ppermute(lax.dynamic_index_in_dim(self.blocks, 1 - self.mine, 1, False), "dp", self.pairs)

    def take(self, *gate):
        self.value = add_low(after(lax.dynamic_index_in_dim(self.blocks, self.mine, 1, False), *gate), self.came)
        return self

    def trade(self):
        self.terms = lax.all_to_all(self.value, "dp", 0, 0, axis_index_groups=self.lines, tiled=True)

    def add(self, *gate):
        self.value = jnp.sum(after(self.terms, *gate).astype(F32), axis=0).astype(BF)
        return self

    def gather(self):
        self.all = lax.all_gather(self.value, "dp", axis=0, tiled=True)


def joined_rows(ladders):
    return jnp.concatenate([piece for ladder in ladders for piece in ladder.rows()], axis=0).astype(F32)


def local(
    dp,
    hidden_in,
    out_grad,
    prefix_len,
    qkv_weight,
    qv_bias,
    dense_weight,
    dense_bias,
    norm1_gain,
    norm1_shift,
    norm2_gain,
    norm2_shift,
    fc1_weight,
    fc1_bias,
    fc2_weight,
    fc2_bias,
):
    rows_here, features = hidden_in.shape
    heads_here, _, head_size = qv_bias.shape
    tensor_index = lax.axis_index("tensor")
    me = tensor_index.reshape(1)
    slopes = 2.0 ** (-8.0 * (tensor_index * heads_here + 1 + lax.iota(jnp.int32, heads_here)).astype(F32) / HEADS)
    bias_full = jnp.stack(
        [qv_bias[:, 0], jnp.zeros_like(qv_bias[:, 0]), qv_bias[:, 1]], axis=1
    ).reshape(1, -1)
    row = lambda v: v.reshape(1, -1)

    norm1 = (qkv_weight, bias_full, row(norm1_gain), row(norm1_shift))
    hidden_x = tensor_send(hidden_in, 2)
    hidden_c = tensor_send(hidden_in, 1)
    dense_c = tensor_send(dense_weight, 1)
    normed_near, joined_near = project(me, (hidden_in, hidden_c), *norm1)
    share = dense_weight.shape[0] // 2
    parity = lax.axis_index("dp") % 2
    dense_share = lax.dynamic_slice_in_dim(dense_weight, parity * share, share, 0)
    hidden_xc = tensor_send(after(hidden_x, joined_near), 1)
    dense_half = tensor_send(after(dense_share, hidden_x, joined_near), 2)
    grad_x = tensor_send(after(out_grad, hidden_x, joined_near), 2)
    normed_far, joined_far = project(me, (hidden_x, hidden_xc), *norm1)
    grad_c = tensor_send(after(out_grad, hidden_c), 1)
    context, totals = attend_forward(joined_near, joined_far, prefix_len, slopes, me)
    context_x = tensor_send(context, 2)
    context_c = tensor_send(context, 1)
    dense_other = lax.ppermute(after(dense_half, context), "dp", [(i, i ^ 1) for i in range(dp)])
    dense_x = jnp.where(
        parity == 0,
        jnp.concatenate([dense_half, dense_other], axis=0),
        jnp.concatenate([dense_other, dense_half], axis=0),
    )
    dense_xc = tensor_send(dense_x, 1)
    dense_blocks = [dense_weight, dense_c, dense_x, dense_xc]
    grad_xc = tensor_send(after(grad_x, context), 1)
    grad_all = jnp.concatenate([out_grad, grad_c, grad_x, grad_xc], axis=0)
    hidden_all = jnp.concatenate([hidden_in, hidden_c, hidden_x, after(hidden_xc, context)], axis=0)
    context_xc = tensor_send(after(context_x, grad_all, hidden_all), 1)

    (normed2_all, activated, pre_grad, middle, fc1_bias_sum, attn_squares, part3, part2, part1, part0) = middle_part(
        me, (context, context_c, context_x, context_xc), dense_blocks, hidden_all, grad_all,
        fc1_weight, fc2_weight, row(fc1_bias), row(dense_bias), row(norm2_gain), row(norm2_shift),
    )

    over = tensor_send(part3, 1)
    near = tensor_send(part1, 1)
    half = features // 2
    fc1_term = dot(normed2_all, pre_grad, TN).astype(BF)
    b1, b2 = Ladder(dp, fc1_term[:half]), Ladder(dp, fc1_term[half:])
    b1.send()
    chip = (after(part2, b1.sent) + over.astype(F32)).astype(BF)
    far = tensor_send(chip, 2)
    fc2_term = dot(after(activated, chip), grad_all, TN).astype(BF)
    a1, a2 = Ladder(dp, fc2_term[:half]), Ladder(dp, fc2_term[half:])
    b2.send(fc2_term)
    mlp3, mlp2, mlp1, mlp0 = rows_product(me, after(activated, b2.sent), fc2_weight, NN, lambda g, me: g)
    b1.take(mlp0).send()
    middle_grad, middle_low, *context_grads, turn_sums = turn(
        after(part0, b1.value), near, far, middle, out_grad, row(norm2_gain), dense_blocks
    )
    arrived = [context_grads[0]] + [tensor_send(context_grads[flip], flip) for flip in (2, 3, 1)]
    arrived = [arrived[0], arrived[3], arrived[1], arrived[2]]
    mlp_over = tensor_send(after(mlp3, arrived[1]), 1)
    mlp_near = tensor_send(after(mlp1, arrived[1]), 1)
    b1.take(arrived[1]).send()
    b2.take(b1.value).send()
    middle_x = tensor_send(after(middle_low, arrived[2]), 2)
    a1.send(b2.value)
    mlp_chip = (after(mlp2, a1.sent) + mlp_over.astype(F32)).astype(BF)
    joined_grad0 = attend_backward(
        after(joined_near, a1.sent, mlp_chip), joined_far, totals, context, arrived, prefix_len, slopes, me, 0
    )
    b1.take(joined_grad0).send()
    b2.take(b1.value).send()
    a1.take(b2.value).send()
    middle_c = tensor_send(after(middle_low, a1.value), 1)
    middle_xc = tensor_send(after(middle_x, a1.value), 1)
    a2.send(middle_xc)
    mlp_far = tensor_send(after(mlp_chip, middle_xc), 2)
    normed1_all = jnp.concatenate([after(normed_near, a2.sent), normed_far], axis=0)
    joined_grad1 = attend_backward(
        after(joined_near, a2.sent), joined_far, totals, context, arrived, prefix_len, slopes, me, 1
    )
    width, extra = joined_grad1.shape[1], context.shape[1] // 2
    wide = width + extra
    qkv_term = dot(normed1_all, joined_grad1, TN).astype(BF)
    middle_all = jnp.concatenate([after(middle_low, qkv_term), middle_c, middle_x, middle_xc], axis=0)
    context_flip = jnp.concatenate(
        [
            lax.dynamic_slice_in_dim(after(context, qkv_term), (tensor_index ^ flip) * rows_here, rows_here, 0)
            for flip in range(4)
        ],
        axis=0,
    )
    dense_term = dot(middle_all, context_flip, TN).astype(BF)
    joined_grad = jnp.concatenate([joined_grad0, after(joined_grad1, dense_term)], axis=1)
    last3, last2, last1, last0, last_sums, joined_sums = last_product(me, joined_grad, hidden_all, qkv_weight)
    b1.take(last0).send()
    b2.take(b1.value).send()
    a1.take(b2.value).send()
    qkv_first = dot(after(normed1_all, dense_term), joined_grad0, TN).astype(BF)
    c1 = Ladder(dp, jnp.concatenate([qkv_first, after(dense_term, a1.value)[:, :extra]], axis=1))
    c1.send()
    a2.take(c1.sent).send()
    mlp_out = after(mlp0, a2.value) + mlp_near.astype(F32) + mlp_far.astype(F32) + fc2_bias
    final = middle + mlp_out
    residual = hidden_in.astype(F32)
    column_squares = lambda v: jnp.sum(v * v, axis=0, keepdims=True)
    joined_sums = joined_sums.reshape(heads_here, 3, head_size)
    qv_sums = jnp.stack([joined_sums[:, 0], joined_sums[:, 2]], axis=1).reshape(1, -1)
    small = jnp.concatenate(
        [column_squares(residual), attn_squares, column_squares(mlp_out), column_squares(final), turn_sums[:4], last_sums],
        axis=0,
    )
    small = small + tensor_send(small, 1)
    small = small + tensor_send(small, 2)
    small = jnp.concatenate(
        [fc1_bias_sum, jnp.pad(qv_sums, ((0, 0), (0, features - qv_sums.shape[1]))), small], axis=0
    )
    small = jnp.pad(small, ((0, 16 - small.shape[0]), (0, 2 * wide - features))).astype(BF)
    c2_term = jnp.concatenate([qkv_term, dense_term[:, extra:]], axis=1)
    b1.take(small)
    c2 = Ladder(dp, jnp.concatenate([c2_term[:half], small[:, :wide], c2_term[half:], small[:, wide:]], axis=0))
    c2.send(b1.came)
    b2.take(c2.sent).send()
    a1.take(b2.value).send()
    c1.take(a1.value).send()
    a2.take(c1.value).send()
    b2.take(a2.value)
    last_over = tensor_send(after(last3, b2.came), 1)
    last_near = tensor_send(after(last1, b2.came), 1)
    a1.take(b2.came).send()
    c1.take(a1.value).send()
    a2.take(c1.value).send()
    c2.take(a2.value).send()
    last_chip = (after(last2, c2.value) + last_over.astype(F32)).astype(BF)
    last_far = tensor_send(last_chip, 2)
    fc1_sum = after(joined_rows([b1, b2]), last_chip)
    a1.take(fc1_sum)
    c1.take(a1.came).send()
    a2.take(c1.value).send()
    c2.take(a2.value).send()
    hidden_grad = last_norm(after(last0, c2.value), last_near, last_far, hidden_in, middle_grad, row(norm1_gain))
    a2.take(hidden_grad)
    c1.take(a2.came).send()
    c2.take(c1.value).send()
    fc2_sum = after(joined_rows([a1, a2]), c2.value)
    c1.take(fc2_sum)
    c2.take(c1.came).send()
    c2.finish()
    qkv_sum, dense_sum, small_sum = finish(parity.reshape(1), width, c1, c2)
    by_dp = jnp.concatenate([small_sum[:16], small_sum[16:]], axis=1)[:, :features]
    by_all = by_dp[5:]
    qv_bias_grad = by_dp[1, : qv_sums.shape[1]].reshape(heads_here, 2, head_size)
    entry_count = rows_here * features * dp * 4
    sublayer_rms = jnp.sqrt(jnp.sum(by_dp[2:6], axis=1) / float(entry_count))
    return (
        final.astype(BF),
        hidden_grad,
        qkv_sum,
        qv_bias_grad,
        dense_sum,
        by_all[1],
        by_all[5],
        by_all[6],
        by_all[2],
        by_all[3],
        fc1_sum.astype(F32),
        by_dp[0],
        fc2_sum.astype(F32),
        by_all[4],
        sublayer_rms,
    )


def solution(mesh):
    return jax.shard_map(
        partial(local, mesh.shape["dp"]),
        mesh=mesh,
        in_specs=(
            P(("dp", "tensor"), None),
            P(("dp", "tensor"), None),
            P("dp"),
            P(None, "tensor"),
            P("tensor", None, None),
            P("tensor", None),
            P(),
            P(),
            P(),
            P(),
            P(),
            P(None, "tensor"),
            P("tensor"),
            P("tensor", None),
            P(),
        ),
        out_specs=(
            P(("dp", "tensor"), None),
            P(("dp", "tensor"), None),
            P(None, "tensor"),
            P("tensor", None, None),
            P("tensor", None),
            P(),
            P(),
            P(),
            P(),
            P(),
            P(None, "tensor"),
            P("tensor"),
            P("tensor", None),
            P(),
            P(),
        ),
        check_vma=False,
    )
```
